32 devices in a mesh: ctx: 4 (over y, core), fsdp: 8 (over z, x).
Axes of the slice: x: 2, y: 2, z: 4, core: 2. Of those that a mesh axis runs over, the one named last changes fastest.
Arguments:
- tokens: bfloat16 [1024, 6144], P(('ctx', 'fsdp')), may hold values from -6 to 6
- qkv_weight: bfloat16 [3, 6144, 4096], P(None, None, 'fsdp'), may hold values from -0.078125 to 0.078125
- out_weight: bfloat16 [4096, 6144], P('fsdp'), may hold values from -0.09375 to 0.09375
- norm_gain: float32 [4096], P('fsdp'), may hold values from 0.1 to 1.9
- initial_state: float32 [32, 128, 128], P('fsdp'), may hold values from -2400 to 2400
Outputs:
- mixed: bfloat16 [1024, 6144], P(('ctx', 'fsdp'))
The draws below stay inside these ranges and needn't reach their ends.
All inputs are finite; a program needn't handle non-finite values.
Results may differ from the reference program's by a relative error of at most 0.013.
Values may be sent and summed in bfloat16 or wider, within the bound.
No kernel may reach another device: no remote copies, remote signals or barrier semaphores. Data moves between devices by JAX's collectives and lax.ppermute only.
A program may use at most 128 MiB of HBM per device.

```python
import jax
import jax.numpy as jnp
from jax import lax

D = 6144
HEADS = 32
HEAD_DIM = 128
BLOCK = 256
TOKENS = 1024
N_CTX = 4
N_FSDP = 8


def block_scale(key, dims, shards, least, high):
    def one(dim, blocks):
        draws = jax.random.uniform(jax.random.fold_in(jax.random.fold_in(key, 6), dim), (blocks,), jnp.float32, least / len(shards), high / len(shards))
        return jnp.repeat(jnp.exp(draws), dims[dim] // blocks).reshape((-1,) + (1,) * (len(dims) - dim - 1))

    loudness = one(*shards[0])
    for cut in shards[1:]:
        loudness = loudness * one(*cut)
    return loudness


def normal_values(own_key, dims, deviation, reach, cuts=(), dtype=jnp.bfloat16):
    result = jax.random.normal(own_key, dims, jnp.float32) * deviation
    if len(cuts) > 0:
        result = block_scale(own_key, dims, cuts, -0.22, 0.18) * result
    return jnp.clip(result, min=-reach, max=reach).astype(dtype)


def setup_inputs(seed: int = 0) -> dict:
    keys = jax.random.split(jax.random.key(seed), 6)
    return {
        "tokens": normal_values(keys[0], (TOKENS, D), 1.0, 6.0, ((0, 32),)),
        "qkv_weight": normal_values(keys[1], (3, D, HEADS * HEAD_DIM), D ** -0.5, 0.078125, ((2, 8),)),
        "out_weight": normal_values(keys[2], (HEADS * HEAD_DIM, D), (HEADS * HEAD_DIM) ** -0.5, 0.09375, ((0, 8),)),
        "norm_gain": jnp.clip(1.0 + 0.18 * jax.random.normal(keys[3], (HEADS * HEAD_DIM,), jnp.float32), 0.1, 1.9),
        "initial_state": normal_values(keys[4], (HEADS, HEAD_DIM, HEAD_DIM), 400.0, 2400.0, ((0, 8),), jnp.float32),
    }


def feature_map(projected):
    return jax.nn.elu(projected) + 1.0

def reference(tokens, qkv_weight, out_weight, norm_gain, initial_state):
    inner_width = HEADS * HEAD_DIM
    group_width = inner_width // N_FSDP
    feat_q = feature_map(jnp.dot(tokens, qkv_weight[0], preferred_element_type=jnp.float32)).astype(jnp.bfloat16)
    feat_k = feature_map(jnp.dot(tokens, qkv_weight[1], preferred_element_type=jnp.float32)).astype(jnp.bfloat16)
    values = jnp.dot(tokens, qkv_weight[2], preferred_element_type=jnp.float32).astype(jnp.bfloat16)
    shaped = (N_CTX, BLOCK, HEADS, HEAD_DIM)
    feat_q = feat_q.reshape(shaped)
    feat_k = feat_k.reshape(shaped)
    values = values.reshape(shaped)
    block_state = jnp.einsum('cthd,cthe->chde', feat_k.astype(jnp.float32), values.astype(jnp.float32), precision=lax.Precision.HIGHEST)
    running = jnp.cumsum(block_state, axis=0)
    earlier = jnp.concatenate([jnp.zeros_like(block_state[:1]), running[:-1]], axis=0)
    prefix = initial_state[None] + earlier
    causal = jnp.arange(BLOCK)[:, None] >= jnp.arange(BLOCK)[None, :]
    gain_heads = norm_gain.reshape(HEADS, HEAD_DIM)
    weight_groups = out_weight.reshape(N_FSDP, group_width, D)

    def one_block(packed):
        block_q, block_k, block_v, block_prefix = packed
        scores = jnp.einsum('ihd,jhd->hij', block_q.astype(jnp.float32), block_k.astype(jnp.float32), precision=lax.Precision.HIGHEST)
        scores = jnp.where(causal[None], scores, 0.0).astype(jnp.bfloat16)
        within = jnp.einsum('hij,jhd->ihd', scores.astype(jnp.float32), block_v.astype(jnp.float32), precision=lax.Precision.HIGHEST)
        carried = jnp.einsum('ihd,hde->ihe', block_q.astype(jnp.float32), block_prefix, precision=lax.Precision.HIGHEST)
        attended = within + carried
        scale = lax.rsqrt(lax.optimization_barrier(jnp.mean(attended * attended, axis=-1, keepdims=True)) + 1e-06)
        normalized = (attended * scale * gain_heads[None]).astype(jnp.bfloat16)
        normal_groups = jnp.transpose(normalized.reshape(BLOCK, N_FSDP, group_width), (1, 0, 2))

        def add_group(total, pair):
            group_rows, group_weight = pair
            partial_sum = jnp.dot(group_rows, group_weight, preferred_element_type=jnp.float32).astype(jnp.bfloat16)
            partial_sum = lax.optimization_barrier(partial_sum)
            return (total + partial_sum.astype(jnp.float32), None)
        total, unused = lax.scan(add_group, jnp.zeros((BLOCK, D), jnp.float32), (normal_groups, weight_groups))
        return total.astype(jnp.bfloat16)
    mixed = lax.map(one_block, (feat_q, feat_k, values, prefix))
    return mixed.reshape(TOKENS, D)
```

```python
import jax
import jax.numpy as jnp
from jax import lax
from jax.sharding import PartitionSpec as P


def ring_order(size):
    if size % 2:
        return list(range(size))
    return list(range(0, size, 2)) + list(range(size - 1, 0, -2))


def neighbours(size):
    ring = ring_order(size)
    right = [(ring[i], ring[(i + 1) % size]) for i in range(size)]
    left = [(b, a) for a, b in right]
    return right, left


def slots(size):
    far = size // 2
    order = [0]
    for step in range(1, far):
        order += [-step, step]
    return order + [far]


def ring_gather(block, size, right, left):
    half = block.shape[1] // 2
    own = [block[:, :half], block[:, half:]]
    going_right, going_left = list(own), list(own)
    held = [own]
    for _ in range(size // 2 - 1):
        for part in range(2):
            going_right[part] = lax.ppermute(going_right[part], "fsdp", right)
            going_left[part] = lax.ppermute(going_left[part], "fsdp", left)
        held.append(list(going_right))
        held.append(list(going_left))
    held.append([lax.ppermute(going_right[0], "fsdp", right), lax.ppermute(going_left[1], "fsdp", left)])
    return held


def add(a, b):
    return (a.astype(jnp.float32) + b.astype(jnp.float32)).astype(jnp.bfloat16)


def ring_scatter(part_of, size, right, left):
    far = size // 2
    to_right = [lax.ppermute(part_of(far, 0), "fsdp", right), None]
    to_left = [None, lax.ppermute(part_of(far, 1), "fsdp", left)]
    for step in range(far - 1, 0, -1):
        for half in range(2):
            mine = part_of(step, half)
            got = to_right[half]
            to_right[half] = lax.ppermute(mine if got is None else add(mine, got), "fsdp", right)
            mine = part_of(-step, half)
            got = to_left[half]
            to_left[half] = lax.ppermute(mine if got is None else add(mine, got), "fsdp", left)
    done = []
    for half in range(2):
        total = part_of(0, half).astype(jnp.float32)
        for got in (to_right[half], to_left[half]):
            if got is not None:
                total = total + got.astype(jnp.float32)
        done.append(total.astype(jnp.bfloat16))
    return jnp.concatenate(done, axis=1)


def earlier_states(state, size):
    place = lax.axis_index("ctx")
    before = jnp.zeros_like(state)
    total = state
    reach = 1
    while reach < size:
        pairs = [(i, i ^ reach) for i in range(size)]
        other = lax.ppermute(total.astype(jnp.bfloat16), "ctx", pairs).astype(jnp.float32)
        before = before + jnp.where((place & reach) != 0, other, 0.0)
        total = total + other
        reach *= 2
    return before


def feature_map(projected):
    return jax.nn.elu(projected) + 1.0


def per_device(n_ctx, n_fsdp, tokens, qkv_weight, out_weight, norm_gain, initial_state):
    rows = tokens.shape[0]
    heads_here, head_dim = initial_state.shape[:2]
    right, left = neighbours(n_fsdp)
    order = slots(n_fsdp)
    ring = jnp.asarray(ring_order(n_fsdp), jnp.int32)
    spot = jnp.argmax(ring == lax.axis_index("fsdp"))
    held_by = ring[(spot + jnp.asarray(order, jnp.int32)) % n_fsdp]
    position = (held_by[:, None] * rows + jnp.arange(rows)[None, :]).reshape(-1)

    held = ring_gather(tokens, n_fsdp, right, left)
    gathered = jnp.concatenate([jnp.concatenate(pair, axis=1) for pair in held], axis=0)
    projected = jnp.einsum("td,sdc->stc", gathered, qkv_weight, preferred_element_type=jnp.float32)
    block_len = gathered.shape[0]
    shaped = (block_len, heads_here, head_dim)
    feat_q = feature_map(projected[0]).astype(jnp.bfloat16).reshape(shaped)
    feat_k = feature_map(projected[1]).astype(jnp.bfloat16).reshape(shaped)
    values = projected[2].astype(jnp.bfloat16).reshape(shaped)
    block_state = jnp.einsum("thd,the->hde", feat_k, values, preferred_element_type=jnp.float32)
    prefix = initial_state + earlier_states(block_state, n_ctx)
    causal = position[:, None] >= position[None, :]
    scores = jnp.einsum("ihd,jhd->hij", feat_q, feat_k, preferred_element_type=jnp.float32)
    scores = jnp.where(causal[None], scores, 0.0).astype(jnp.bfloat16)
    within = jnp.einsum("hij,jhd->ihd", scores, values, preferred_element_type=jnp.float32)
    carried = jnp.einsum(
        "ihd,hde->ihe", feat_q.astype(jnp.float32), prefix, precision=lax.Precision.HIGHEST
    )
    attended = within + carried
    scale = lax.rsqrt(jnp.mean(attended * attended, axis=-1, keepdims=True) + 1e-06)
    gain_heads = norm_gain.reshape(heads_here, head_dim)
    normalized = (attended * scale * gain_heads[None]).astype(jnp.bfloat16)
    normalized = normalized.reshape(block_len, heads_here * head_dim)
    partial = jnp.dot(normalized, out_weight, preferred_element_type=jnp.float32).astype(jnp.bfloat16)
    half = partial.shape[1] // 2

    def part_of(distance, which):
        place = order.index(distance)
        return partial[place * rows : (place + 1) * rows, which * half : (which + 1) * half]

    return ring_scatter(part_of, n_fsdp, right, left)


def solution(mesh):
    n_ctx, n_fsdp = mesh.shape["ctx"], mesh.shape["fsdp"]

    def body(*args):
        return per_device(n_ctx, n_fsdp, *args)

    placed = (
        P(("ctx", "fsdp"), None),
        P(None, None, "fsdp"),
        P("fsdp", None),
        P("fsdp"),
        P("fsdp", None, None),
    )
    return jax.shard_map(
        body, mesh=mesh, in_specs=placed, out_specs=P(("ctx", "fsdp"), None), check_vma=False
    )
```

```python
import functools

import jax
import jax.numpy as jnp
from jax import lax
from jax.experimental import pallas as pl
from jax.experimental.pallas import tpu as pltpu
from jax.sharding import PartitionSpec as P

VMEM = pl.BlockSpec(memory_space=pltpu.VMEM)
ANY = pl.BlockSpec(memory_space=pl.ANY)
F32, BF16 = jnp.float32, jnp.bfloat16


def ring_order(size):
    return list(range(0, size, 2)) + list(range(size - 1, 0, -2))


def neighbours(size):
    ring = ring_order(size)
    right = [(ring[i], ring[(i + 1) % size]) for i in range(size)]
    left = [(b, a) for a, b in right]
    return right, left


def slots(size):
    order = [0]
    for step in range(1, size // 2):
        order += [-step, step]
    return order + [size // 2]


def call(body, out_shape, in_specs, out_specs, flops=0, nbytes=0, limit=16 << 20, **more):
    return pl.pallas_call(
        body,
        out_shape=out_shape,
        in_specs=in_specs,
        out_specs=out_specs,
        cost_estimate=pl.CostEstimate(flops=flops, bytes_accessed=nbytes, transcendentals=0),
        compiler_params=pltpu.CompilerParams(vmem_limit_bytes=limit),
        **more,
    )


def fetch(source, index, shape, after):
    def body(source_ref, after_ref, out_ref, sem):
        copy = pltpu.make_async_copy(source_ref.at[index], out_ref, sem)
        copy.start()
        copy.wait()

    return call(
        body,
        jax.ShapeDtypeStruct(shape, source.dtype),
        [ANY, ANY],
        VMEM,
        nbytes=2 * 2 * shape[0] * shape[1],
        scratch_shapes=[pltpu.SemaphoreType.DMA],
        name="fetch",
    )(source, after)


def ring_gather(block, size, right, left):
    half = block.shape[1] // 2
    quarter = half // 2
    going_right = [block[:, :half], block[:, half:]]
    going_left = list(going_right)
    held = [[going_right[0]], [going_right[1]]]
    for _ in range(size // 2 - 1):
        for part in range(2):
            going_right[part] = lax.ppermute(going_right[part], "fsdp", right)
            going_left[part] = lax.ppermute(going_left[part], "fsdp", left)
            held[part] += [going_right[part], going_left[part]]
    for part in range(2):
        held[part].append(lax.ppermute(going_right[part][:, :quarter], "fsdp", right))
        held[part].append(lax.ppermute(going_left[part][:, quarter:], "fsdp", left))
    return held


def assemble(pieces, into):
    rows = pieces[0].shape[0]
    for place, piece in enumerate(pieces[:-2]):
        into[place * rows : (place + 1) * rows, :] = piece[...]
    quarter = pieces[-1].shape[1]
    start = (len(pieces) - 2) * rows
    into[start : start + rows, :quarter] = pieces[-2][...]
    into[start : start + rows, quarter:] = pieces[-1][...]


def first_pass(pieces, weight, n_rows):
    n_out, width, columns = weight.shape
    half = width // 2
    tile = min(columns, 256)
    tiles = columns // tile

    def body(*refs):
        rows = refs[: len(pieces)]
        weight_ref, out_ref, whole = refs[len(pieces) :]
        step = pl.program_id(0)

        @pl.when(step == 0)
        def _():
            assemble(rows, whole)

        start = pl.multiple_of((step % tiles) * tile, tile)
        out_ref[step // tiles, :, pl.ds(start, tile)] = jnp.dot(
            whole[...], weight_ref[...], preferred_element_type=F32
        )

    return call(
        body,
        jax.ShapeDtypeStruct((n_out, n_rows, columns), F32),
        [VMEM] * len(pieces)
        + [pl.BlockSpec((None, half, tile), lambda i: (i // tiles, 0, i % tiles))],
        VMEM,
        flops=2 * n_out * n_rows * half * columns,
        nbytes=2 * n_out * half * columns,
        limit=24 << 20,
        grid=(n_out * tiles,),
        scratch_shapes=[pltpu.VMEM((n_rows, half), BF16)],
        name="first_pass",
    )(*pieces, weight)


def feature_map(projected):
    return jnp.where(projected > 0.0, projected + 1.0, jnp.exp(jnp.minimum(projected, 0.0)))


def keys_and_values(pieces, key_weight, value_weight, first, head_dim):
    _, n_rows, columns = first.shape
    half = key_weight.shape[0]

    def body(*refs):
        rows = refs[: len(pieces)]
        key_ref, value_ref, first_ref, feat_ref, values_ref, state_ref, whole = refs[len(pieces) :]
        assemble(rows, whole)
        tile = min(columns, 256)
        for start in range(0, columns, tile):
            span = slice(start, start + tile)
            projected = first_ref[1, :, span] + jnp.dot(whole[...], key_ref[:, span], preferred_element_type=F32)
            feat = feature_map(projected).astype(BF16)
            feat_ref[:, span] = feat
            projected = first_ref[2, :, span] + jnp.dot(whole[...], value_ref[:, span], preferred_element_type=F32)
            values = projected.astype(BF16)
            values_ref[:, span] = values
            for head in range(start, start + tile, head_dim):
                at = slice(head - start, head - start + head_dim)
                state_ref[head // head_dim] = lax.dot_general(
                    feat[:, at], values[:, at], (((0,), (0,)), ((), ())), preferred_element_type=F32
                ).astype(BF16)

    return call(
        body,
        (
            jax.ShapeDtypeStruct((n_rows, columns), BF16),
            jax.ShapeDtypeStruct((n_rows, columns), BF16),
            jax.ShapeDtypeStruct((columns // head_dim, head_dim, head_dim), BF16),
            jax.ShapeDtypeStruct((n_rows, half), BF16),
        ),
        [VMEM] * (len(pieces) + 3),
        (VMEM,) * 4,
        flops=2 * 2 * n_rows * half * columns,
        nbytes=2 * 2 * half * columns,
        name="keys_and_values",
    )(*pieces, key_weight, value_weight, first)


def queries_within(whole, query_weight, first, feat_k, values, head_dim, size, rows):
    n_rows, columns = feat_k.shape
    order = slots(size)

    def place(shape, axis):
        spot = lax.axis_index("fsdp")
        spot = jnp.where(spot % 2 == 0, spot // 2, size - (spot + 1) // 2)
        row = lax.broadcasted_iota(jnp.int32, shape, axis)
        slot = row // rows
        start = jnp.zeros(shape, jnp.int32)
        for at, distance in enumerate(order):
            there = (spot + distance + size) % size
            holder = jnp.where(there < size // 2, 2 * there, 2 * (size - there) - 1)
            start = jnp.where(slot == at, holder * rows, start)
        return start + row - slot * rows

    def body(whole_ref, weight_ref, first_ref, k_ref, v_ref, feat_ref, within_ref):
        causal = place((n_rows, 1), 0) >= place((1, n_rows), 1)
        tile = min(columns, 256)
        for start in range(0, columns, tile):
            span = slice(start, start + tile)
            projected = first_ref[0, :, span] + jnp.dot(whole_ref[...], weight_ref[:, span], preferred_element_type=F32)
            feat = feature_map(projected).astype(BF16)
            feat_ref[:, span] = feat
            for head in range(start, start + tile, head_dim):
                at = slice(head, head + head_dim)
                scores = lax.dot_general(
                    feat[:, head - start : head - start + head_dim],
                    k_ref[:, at],
                    (((1,), (1,)), ((), ())),
                    preferred_element_type=F32,
                )
                scores = jnp.where(causal, scores, 0.0).astype(BF16)
                within_ref[:, at] = jnp.dot(scores, v_ref[:, at], preferred_element_type=F32)

    half = whole.shape[1]
    return call(
        body,
        (jax.ShapeDtypeStruct((n_rows, columns), BF16), jax.ShapeDtypeStruct((n_rows, columns), F32)),
        [VMEM] * 5,
        (VMEM,) * 2,
        flops=2 * n_rows * half * columns + 4 * n_rows * n_rows * columns,
        nbytes=2 * half * columns,
        limit=24 << 20,
        name="queries_within",
    )(whole, query_weight, first, feat_k, values)


def part_shapes(count, rows, half):
    return [jax.ShapeDtypeStruct((rows, half), BF16)] * (count - 1) + [
        jax.ShapeDtypeStruct((rows, half // 2), BF16)
    ] * 2


def spread(product, start, parts, rows, width):
    for place, part in enumerate(parts[:-2]):
        part[:, start : start + width] = product[place * rows : (place + 1) * rows, :]
    last = product[(len(parts) - 2) * rows :, :]
    quarter = parts[-1].shape[1]
    target = parts[-2] if start < quarter else parts[-1]
    start = start % quarter
    target[:, start : start + width] = last


def project_out(normalized, weight_ref, first_column, parts, rows):
    half = parts[0].shape[1]
    tile = 512 if (half // 2) % 512 == 0 else 128
    for start in range(0, half, tile):
        columns = slice(first_column + start, first_column + start + tile)
        product = jnp.dot(normalized, weight_ref[:, columns], preferred_element_type=F32).astype(BF16)
        spread(product, start, parts, rows, tile)


def attend_and_project(feat_q, within, initial, earlier, gain, out_weight, size, head_dim):
    n_rows, columns = feat_q.shape
    rows = n_rows // size
    half = out_weight.shape[1] // 2
    shapes = part_shapes(size, rows, half)

    def body(q_ref, within_ref, initial_ref, earlier_ref, gain_ref, weight_ref, *refs):
        normalized_ref, parts = refs[0], refs[1:]
        for head in range(columns // head_dim):
            at = slice(head * head_dim, (head + 1) * head_dim)
            prefix = initial_ref[head] + earlier_ref[head]
            high = prefix.astype(BF16)
            low = (prefix - high.astype(F32)).astype(BF16)
            q = q_ref[:, at]
            attended = within_ref[:, at] + jnp.dot(q, high, preferred_element_type=F32)
            attended = attended + jnp.dot(q, low, preferred_element_type=F32)
            scale = lax.rsqrt(jnp.mean(attended * attended, axis=-1, keepdims=True) + 1e-06)
            normalized_ref[:, at] = (attended * scale * gain_ref[:, at]).astype(BF16)
        project_out(normalized_ref[...], weight_ref, 0, parts, rows)

    out = call(
        body,
        [jax.ShapeDtypeStruct((n_rows, columns), BF16)] + shapes,
        [VMEM] * 6,
        [VMEM] * (1 + len(shapes)),
        flops=2 * n_rows * half * columns,
        nbytes=2 * half * columns,
        name="attend_and_project",
    )(feat_q, within, initial, earlier, gain.reshape(1, columns), out_weight)
    return out[0], out[1:]


def project_rest(normalized, out_weight, size):
    n_rows, columns = normalized.shape
    rows = n_rows // size
    half = out_weight.shape[1] // 2
    shapes = part_shapes(size, rows, half)

    def body(normalized_ref, weight_ref, *parts):
        project_out(normalized_ref[...], weight_ref, half, parts, rows)

    return call(
        body,
        shapes,
        [VMEM] * 2,
        [VMEM] * len(shapes),
        flops=2 * n_rows * half * columns,
        nbytes=2 * half * columns,
        name="project_rest",
    )(normalized, out_weight)


def add_step(mine_right, got_right, mine_left, got_left):
    rows, half = mine_right.shape
    partial = got_right.shape[1]

    def body(mr, gr, ml, gl, to_right, to_left):
        if partial < half:
            to_right[:, partial:] = mr[:, partial:]
            to_left[:, : half - partial] = ml[:, : half - partial]
        to_right[:, :partial] = (mr[:, :partial].astype(F32) + gr[...].astype(F32)).astype(BF16)
        to_left[:, half - partial :] = (ml[:, half - partial :].astype(F32) + gl[...].astype(F32)).astype(BF16)

    return call(
        body,
        [jax.ShapeDtypeStruct((rows, half), BF16)] * 2,
        [VMEM] * 4,
        [VMEM] * 2,
        nbytes=12 * rows * half,
        name="add_step",
    )(mine_right, got_right, mine_left, got_left)


def finish(groups):
    rows, half = groups[0][0].shape

    def body(*refs):
        out = refs[-1]
        for part in range(len(groups)):
            mine, got_right, got_left = refs[3 * part : 3 * part + 3]
            total = mine[...].astype(F32) + got_right[...].astype(F32) + got_left[...].astype(F32)
            out[:, part * half : (part + 1) * half] = total.astype(BF16)

    flat = [value for group in groups for value in group]
    return call(
        body,
        jax.ShapeDtypeStruct((rows, half * len(groups)), BF16),
        [VMEM] * len(flat),
        VMEM,
        nbytes=4 * rows * half,
        name="finish",
    )(*flat)


def earlier_states(state, size):
    place = lax.axis_index("ctx")
    before = None
    total = state
    reach = 1
    while reach < size:
        pairs = [(i, i ^ reach) for i in range(size)]
        other = lax.ppermute(total, "ctx", pairs)
        mine = jnp.where((place & reach) != 0, other.astype(F32), 0.0)
        before = mine if before is None else before + mine
        total = (total.astype(F32) + other.astype(F32)).astype(BF16)
        reach *= 2
    return before


def per_device(n_ctx, n_fsdp, tokens, qkv_weight, out_weight, norm_gain, initial_state):
    rows, width = tokens.shape
    heads_here, head_dim = initial_state.shape[:2]
    columns = heads_here * head_dim
    n_rows = rows * n_fsdp
    far = n_fsdp // 2
    right, left = neighbours(n_fsdp)
    order = slots(n_fsdp)

    held = ring_gather(tokens, n_fsdp, right, left)
    half = width // 2
    second = [
        fetch(qkv_weight, (s, pl.ds(half, half)), (half, columns), held[0][1 + at])
        for at, s in enumerate(range(3))
    ]
    fetched_out = fetch(out_weight, (pl.ds(0, columns),), out_weight.shape, held[1][2])

    first = first_pass(held[0], qkv_weight, n_rows)
    feat_k, values, state, whole = keys_and_values(held[1], second[1], second[2], first, head_dim)
    feat_q, within = queries_within(whole, second[0], first, feat_k, values, head_dim, n_fsdp, rows)
    earlier = earlier_states(state, n_ctx)
    normalized, parts_a = attend_and_project(
        feat_q, within, initial_state, earlier, norm_gain, fetched_out, n_fsdp, head_dim
    )
    parts_b = project_rest(normalized, fetched_out, n_fsdp)

    groups = []
    for parts in (parts_a, parts_b):
        got_right = lax.ppermute(parts[-2], "fsdp", right)
        got_left = lax.ppermute(parts[-1], "fsdp", left)
        for step in range(far - 1, 0, -1):
            to_right, to_left = add_step(
                parts[order.index(step)], got_right, parts[order.index(-step)], got_left
            )
            got_right = lax.ppermute(to_right, "fsdp", right)
            got_left = lax.ppermute(to_left, "fsdp", left)
        groups.append((parts[0], got_right, got_left))
    return finish(groups)


def solution(mesh):
    body = functools.partial(per_device, mesh.shape["ctx"], mesh.shape["fsdp"])
    placed = (
        P(("ctx", "fsdp"), None),
        P(None, None, "fsdp"),
        P("fsdp", None),
        P("fsdp"),
        P("fsdp", None, None),
    )
    return jax.shard_map(
        body, mesh=mesh, in_specs=placed, out_specs=P(("ctx", "fsdp"), None), check_vma=False
    )
```

```python
import functools

import jax
import jax.numpy as jnp
from jax import lax
from jax.experimental import pallas as pl
from jax.experimental.pallas import tpu as pltpu
from jax.sharding import PartitionSpec as P

VMEM = pl.BlockSpec(memory_space=pltpu.VMEM)
ANY = pl.BlockSpec(memory_space=pl.ANY)
HBM = pl.BlockSpec(memory_space=pltpu.HBM)
F32, BF16 = jnp.float32, jnp.bfloat16


def ring_order(size):
    return list(range(0, size, 2)) + list(range(size - 1, 0, -2))


def neighbours(size):
    ring = ring_order(size)
    right = [(ring[i], ring[(i + 1) % size]) for i in range(size)]
    left = [(b, a) for a, b in right]
    return right, left


def slots(size):
    order = [0]
    for step in range(1, size // 2):
        order += [-step, step]
    return order + [size // 2]


def in_hbm(array):
    return pltpu.with_memory_space_constraint(array, pltpu.HBM)


def call(body, out_shape, in_specs, out_specs, flops=0, nbytes=0, limit=12 << 20, **more):
    return pl.pallas_call(
        body,
        out_shape=out_shape,
        in_specs=in_specs,
        out_specs=out_specs,
        cost_estimate=pl.CostEstimate(flops=flops, bytes_accessed=nbytes, transcendentals=0),
        compiler_params=pltpu.CompilerParams(vmem_limit_bytes=limit),
        **more,
    )


def fetch(source, index, shape, through):
    def body(source_ref, through_ref, out_ref, passed_ref, sem):
        copy = pltpu.make_async_copy(source_ref.at[index], out_ref, sem)
        copy.start()
        copy.wait()

    return call(
        body,
        (jax.ShapeDtypeStruct(shape, source.dtype), jax.ShapeDtypeStruct(through.shape, through.dtype)),
        [HBM, ANY],
        (VMEM, ANY),
        nbytes=2 * 2 * shape[0] * shape[1],
        scratch_shapes=[pltpu.SemaphoreType.DMA],
        input_output_aliases={1: 1},
        name="fetch",
    )(in_hbm(source), through)


def ring_gather(block, size, right, left, fetches):
    fetches = list(fetches)
    brought = []
    half = block.shape[1] // 2
    quarter = half // 2
    going_right = [block[:, :half], block[:, half:]]
    going_left = list(going_right)
    held = [[going_right[0]], [going_right[1]]]
    for _ in range(size // 2 - 1):
        for part in range(2):
            going_right[part] = lax.ppermute(going_right[part], "fsdp", right)
            going_left[part] = lax.ppermute(going_left[part], "fsdp", left)
            if fetches:
                source, index, shape = fetches.pop(0)
                got, going_right[part] = fetch(source, index, shape, going_right[part])
                brought.append(got)
            held[part] += [going_right[part], going_left[part]]
    for part in range(2):
        held[part].append(lax.ppermute(going_right[part][:, :quarter], "fsdp", right))
        held[part].append(lax.ppermute(going_left[part][:, quarter:], "fsdp", left))
    return held, brought


def assemble(pieces, into):
    rows = pieces[0].shape[0]
    for place, piece in enumerate(pieces[:-2]):
        into[place * rows : (place + 1) * rows, :] = piece[...]
    quarter = pieces[-1].shape[1]
    start = (len(pieces) - 2) * rows
    into[start : start + rows, :quarter] = pieces[-2][...]
    into[start : start + rows, quarter:] = pieces[-1][...]


def first_pass(pieces, weight, n_rows):
    n_out, width, columns = weight.shape
    half = width // 2
    tile = min(columns, 256)
    tiles = columns // tile

    def body(*refs):
        rows = refs[: len(pieces)]
        weight_ref, out_ref, whole, local, sems = refs[len(pieces) :]
        copies = [
            pltpu.make_async_copy(
                weight_ref.at[step // tiles, pl.ds(0, half), pl.ds((step % tiles) * tile, tile)],
                local.at[step],
                sems.at[step],
            )
            for step in range(n_out * tiles)
        ]
        for copy in copies:
            copy.start()
        assemble(rows, whole)
        for step, copy in enumerate(copies):
            copy.wait()
            start = (step % tiles) * tile
            out_ref[step // tiles, :, start : start + tile] = jnp.dot(
                whole[...], local[step], preferred_element_type=F32
            )

    return call(
        body,
        jax.ShapeDtypeStruct((n_out, n_rows, columns), F32),
        [VMEM] * len(pieces) + [HBM],
        VMEM,
        flops=2 * n_out * n_rows * half * columns,
        nbytes=2 * n_out * half * columns,
        limit=14 << 20,
        scratch_shapes=[
            pltpu.VMEM((n_rows, half), BF16),
            pltpu.VMEM((n_out * tiles, half, tile), BF16),
            pltpu.SemaphoreType.DMA((n_out * tiles,)),
        ],
        name="first_pass",
    )(*pieces, in_hbm(weight))


def feature_map(projected):
    return jnp.where(projected > 0.0, projected + 1.0, jnp.exp(jnp.minimum(projected, 0.0)))


def keys_and_values(pieces, key_weight, value_weight, first, head_dim):
    _, n_rows, columns = first.shape
    half = key_weight.shape[0]

    def body(*refs):
        rows = refs[: len(pieces)]
        key_ref, value_ref, first_ref, feat_ref, values_ref, state_ref, whole = refs[len(pieces) :]
        assemble(rows, whole)
        tile = min(columns, 256)
        for start in range(0, columns, tile):
            span = slice(start, start + tile)
            projected = first_ref[1, :, span] + jnp.dot(whole[...], key_ref[:, span], preferred_element_type=F32)
            feat = feature_map(projected).astype(BF16)
            feat_ref[:, span] = feat
            projected = first_ref[2, :, span] + jnp.dot(whole[...], value_ref[:, span], preferred_element_type=F32)
            values = projected.astype(BF16)
            values_ref[:, span] = values
            for head in range(start, start + tile, head_dim):
                at = slice(head - start, head - start + head_dim)
                state_ref[head // head_dim] = lax.dot_general(
                    feat[:, at], values[:, at], (((0,), (0,)), ((), ())), preferred_element_type=F32
                ).astype(BF16)

    return call(
        body,
        (
            jax.ShapeDtypeStruct((n_rows, columns), BF16),
            jax.ShapeDtypeStruct((n_rows, columns), BF16),
            jax.ShapeDtypeStruct((columns // head_dim, head_dim, head_dim), BF16),
            jax.ShapeDtypeStruct((n_rows, half), BF16),
        ),
        [VMEM] * (len(pieces) + 3),
        (VMEM,) * 4,
        flops=2 * 2 * n_rows * half * columns,
        nbytes=2 * 2 * half * columns,
        name="keys_and_values",
    )(*pieces, key_weight, value_weight, first)


def queries_within(whole, query_weight, first, feat_k, values, head_dim, size, rows):
    n_rows, columns = feat_k.shape
    order = slots(size)

    def place(shape, axis):
        spot = lax.axis_index("fsdp")
        spot = jnp.where(spot % 2 == 0, spot // 2, size - (spot + 1) // 2)
        row = lax.broadcasted_iota(jnp.int32, shape, axis)
        slot = row // rows
        start = jnp.zeros(shape, jnp.int32)
        for at, distance in enumerate(order):
            there = (spot + distance + size) % size
            holder = jnp.where(there < size // 2, 2 * there, 2 * (size - there) - 1)
            start = jnp.where(slot == at, holder * rows, start)
        return start + row - slot * rows

    def body(whole_ref, weight_ref, first_ref, k_ref, v_ref, feat_ref, within_ref):
        causal = place((n_rows, 1), 0) >= place((1, n_rows), 1)
        tile = min(columns, 256)
        for start in range(0, columns, tile):
            span = slice(start, start + tile)
            projected = first_ref[0, :, span] + jnp.dot(whole_ref[...], weight_ref[:, span], preferred_element_type=F32)
            feat = feature_map(projected).astype(BF16)
            feat_ref[:, span] = feat
            for head in range(start, start + tile, head_dim):
                at = slice(head, head + head_dim)
                scores = lax.dot_general(
                    feat[:, head - start : head - start + head_dim],
                    k_ref[:, at],
                    (((1,), (1,)), ((), ())),
                    preferred_element_type=F32,
                )
                scores = jnp.where(causal, scores, 0.0).astype(BF16)
                within_ref[:, at] = jnp.dot(scores, v_ref[:, at], preferred_element_type=F32)

    half = whole.shape[1]
    return call(
        body,
        (jax.ShapeDtypeStruct((n_rows, columns), BF16), jax.ShapeDtypeStruct((n_rows, columns), F32)),
        [VMEM] * 5,
        (VMEM,) * 2,
        flops=2 * n_rows * half * columns + 4 * n_rows * n_rows * columns,
        nbytes=2 * half * columns,
        limit=14 << 20,
        name="queries_within",
    )(whole, query_weight, first, feat_k, values)


def part_shapes(count, rows, half):
    return [jax.ShapeDtypeStruct((rows, half), BF16)] * (count - 1) + [
        jax.ShapeDtypeStruct((rows, half // 2), BF16)
    ] * 2


def spread(product, start, parts, rows, width):
    for place, part in enumerate(parts[:-2]):
        part[:, start : start + width] = product[place * rows : (place + 1) * rows, :]
    last = product[(len(parts) - 2) * rows :, :]
    quarter = parts[-1].shape[1]
    target = parts[-2] if start < quarter else parts[-1]
    start = start % quarter
    target[:, start : start + width] = last


def project_out(normalized, weight_ref, parts, rows):
    half = parts[0].shape[1]
    tile = 512 if (half // 2) % 512 == 0 else 128
    for start in range(0, half, tile):
        product = jnp.dot(normalized, weight_ref[:, start : start + tile], preferred_element_type=F32).astype(BF16)
        spread(product, start, parts, rows, tile)


def attend_and_project(feat_q, within, initial, others, gain, out_weight, size, head_dim):
    n_rows, columns = feat_q.shape
    rows = n_rows // size
    half = out_weight.shape[1]
    shapes = part_shapes(size, rows, half)

    def body(q_ref, within_ref, initial_ref, gain_ref, weight_ref, *refs):
        other_refs, normalized_ref, parts = refs[: len(others)], refs[len(others)], refs[len(others) + 1 :]
        place = lax.axis_index("ctx")
        for head in range(columns // head_dim):
            at = slice(head * head_dim, (head + 1) * head_dim)
            prefix = initial_ref[head]
            for bit, other_ref in enumerate(other_refs):
                later = (place // 2**bit) % 2 == 1
                prefix = prefix + jnp.where(later, other_ref[head].astype(F32), 0.0)
            high = prefix.astype(BF16)
            low = (prefix - high.astype(F32)).astype(BF16)
            q = q_ref[:, at]
            attended = within_ref[:, at] + jnp.dot(q, high, preferred_element_type=F32)
            attended = attended + jnp.dot(q, low, preferred_element_type=F32)
            scale = lax.rsqrt(jnp.mean(attended * attended, axis=-1, keepdims=True) + 1e-06)
            normalized_ref[:, at] = (attended * scale * gain_ref[:, at]).astype(BF16)
        project_out(normalized_ref[...], weight_ref, parts, rows)

    out = call(
        body,
        [jax.ShapeDtypeStruct((n_rows, columns), BF16)] + shapes,
        [VMEM] * (5 + len(others)),
        [VMEM] * (1 + len(shapes)),
        flops=2 * n_rows * half * columns,
        nbytes=2 * half * columns,
        name="attend_and_project",
    )(feat_q, within, initial, gain.reshape(1, columns), out_weight, *others)
    return out[0], out[1:]


def project_rest(normalized, out_weight, size):
    n_rows, columns = normalized.shape
    rows = n_rows // size
    half = out_weight.shape[1]
    shapes = part_shapes(size, rows, half)

    def body(normalized_ref, weight_ref, *parts):
        project_out(normalized_ref[...], weight_ref, parts, rows)

    return call(
        body,
        shapes,
        [VMEM] * 2,
        [VMEM] * len(shapes),
        flops=2 * n_rows * half * columns,
        nbytes=2 * half * columns,
        name="project_rest",
    )(normalized, out_weight)


def add_step(mine_right, got_right, mine_left, got_left):
    rows, half = mine_right.shape
    partial = got_right.shape[1]

    def body(mr, gr, ml, gl, to_right, to_left):
        if partial < half:
            to_right[:, partial:] = mr[:, partial:]
            to_left[:, : half - partial] = ml[:, : half - partial]
        to_right[:, :partial] = (mr[:, :partial].astype(F32) + gr[...].astype(F32)).astype(BF16)
        to_left[:, half - partial :] = (ml[:, half - partial :].astype(F32) + gl[...].astype(F32)).astype(BF16)

    return call(
        body,
        [jax.ShapeDtypeStruct((rows, half), BF16)] * 2,
        [VMEM] * 4,
        [VMEM] * 2,
        nbytes=12 * rows * half,
        name="add_step",
    )(mine_right, got_right, mine_left, got_left)


def finish(groups):
    rows, half = groups[0][0].shape

    def body(*refs):
        out = refs[-1]
        for part in range(len(groups)):
            mine, got_right, got_left = refs[3 * part : 3 * part + 3]
            total = mine[...].astype(F32) + got_right[...].astype(F32) + got_left[...].astype(F32)
            out[:, part * half : (part + 1) * half] = total.astype(BF16)

    flat = [value for group in groups for value in group]
    return call(
        body,
        jax.ShapeDtypeStruct((rows, half * len(groups)), BF16),
        [VMEM] * len(flat),
        VMEM,
        nbytes=4 * rows * half,
        name="finish",
    )(*flat)


def add_states(one, two):
    def body(one_ref, two_ref, out_ref):
        out_ref[...] = (one_ref[...].astype(F32) + two_ref[...].astype(F32)).astype(BF16)

    return call(
        body, jax.ShapeDtypeStruct(one.shape, BF16), [VMEM] * 2, VMEM, nbytes=6 * one.size, limit=4 << 20, name="add_states"
    )(one, two)


def exchange_states(state, size):
    others = []
    total = state
    reach = 1
    while reach < size:
        pairs = [(i, i ^ reach) for i in range(size)]
        others.append(lax.ppermute(total, "ctx", pairs))
        reach *= 2
        if reach < size:
            total = add_states(total, others[-1])
    return others


def per_device(n_ctx, n_fsdp, tokens, qkv_weight, out_weight, norm_gain, initial_state):
    rows, width = tokens.shape
    heads_here, head_dim = initial_state.shape[:2]
    columns = heads_here * head_dim
    n_rows = rows * n_fsdp
    far = n_fsdp // 2
    right, left = neighbours(n_fsdp)
    order = slots(n_fsdp)

    half = width // 2
    fetches = [(qkv_weight, (s, pl.ds(half, half)), (half, columns)) for s in (1, 2, 0)]
    fetches += [(out_weight, (slice(None), pl.ds(h * half, half)), (columns, half)) for h in range(2)]
    held, brought = ring_gather(tokens, n_fsdp, right, left, fetches)
    key_weight, value_weight, query_weight, out_first, out_second = brought

    first = first_pass(held[0], qkv_weight, n_rows)
    feat_k, values, state, whole = keys_and_values(held[1], key_weight, value_weight, first, head_dim)
    feat_q, within = queries_within(whole, query_weight, first, feat_k, values, head_dim, n_fsdp, rows)
    others = exchange_states(state, n_ctx)
    normalized, parts_a = attend_and_project(
        feat_q, within, initial_state, others, norm_gain, out_first, n_fsdp, head_dim
    )
    parts_b = project_rest(normalized, out_second, n_fsdp)

    groups = []
    for parts in (parts_a, parts_b):
        got_right = lax.ppermute(parts[-2], "fsdp", right)
        got_left = lax.ppermute(parts[-1], "fsdp", left)
        for step in range(far - 1, 0, -1):
            to_right, to_left = add_step(
                parts[order.index(step)], got_right, parts[order.index(-step)], got_left
            )
            got_right = lax.ppermute(to_right, "fsdp", right)
            got_left = lax.ppermute(to_left, "fsdp", left)
        groups.append((parts[0], got_right, got_left))
    return finish(groups)


def solution(mesh):
    body = functools.partial(per_device, mesh.shape["ctx"], mesh.shape["fsdp"])
    placed = (
        P(("ctx", "fsdp"), None),
        P(None, None, "fsdp"),
        P("fsdp", None),
        P("fsdp"),
        P("fsdp", None, None),
    )
    return jax.shard_map(
        body, mesh=mesh, in_specs=placed, out_specs=P(("ctx", "fsdp"), None), check_vma=False
    )
```

```python
import functools

import jax
import jax.numpy as jnp
from jax import lax
from jax.experimental import pallas as pl
from jax.experimental.pallas import tpu as pltpu
from jax.sharding import PartitionSpec as P

VMEM = pl.BlockSpec(memory_space=pltpu.VMEM)
ANY = pl.BlockSpec(memory_space=pl.ANY)
HBM = pl.BlockSpec(memory_space=pltpu.HBM)
F32, BF16 = jnp.float32, jnp.bfloat16
HOP_FLOPS = 5 * 10**9


def ring_order(size):
    return list(range(0, size, 2)) + list(range(size - 1, 0, -2))


def neighbours(size):
    ring = ring_order(size)
    right = [(ring[i], ring[(i + 1) % size]) for i in range(size)]
    left = [(b, a) for a, b in right]
    return right, left


def slots(size):
    order = [0]
    for step in range(1, size // 2):
        order += [-step, step]
    return order + [size // 2]


def in_hbm(array):
    return pltpu.with_memory_space_constraint(array, pltpu.HBM)


def call(body, out_shape, in_specs, out_specs, flops=0, nbytes=0, limit=12 << 20, **more):
    return pl.pallas_call(
        body,
        out_shape=out_shape,
        in_specs=in_specs,
        out_specs=out_specs,
        cost_estimate=pl.CostEstimate(flops=flops, bytes_accessed=nbytes, transcendentals=0),
        compiler_params=pltpu.CompilerParams(vmem_limit_bytes=limit),
        **more,
    )


def fetch(source, index, shape, through):
    def body(source_ref, through_ref, out_ref, passed_ref, sem):
        copy = pltpu.make_async_copy(source_ref.at[index], out_ref, sem)
        copy.start()
        copy.wait()

    return call(
        body,
        (jax.ShapeDtypeStruct(shape, source.dtype), jax.ShapeDtypeStruct(through.shape, through.dtype)),
        [HBM, ANY],
        (VMEM, ANY),
        nbytes=2 * 2 * shape[0] * shape[1],
        scratch_shapes=[pltpu.SemaphoreType.DMA],
        input_output_aliases={1: 1},
        name="fetch",
    )(in_hbm(source), through)


def ring_gather(block, size, right, left, fetches):
    fetches = list(fetches)
    brought = []
    half = block.shape[1] // 2
    quarter = half // 2
    going_right = [block[:, :half], block[:, half:]]
    source, index, shape = fetches.pop(0)
    got, going_right[1] = fetch(source, index, shape, going_right[1])
    brought.append(got)
    going_left = list(going_right)
    held = [[going_right[0]], [going_right[1]]]
    for _ in range(size // 2 - 1):
        for part in range(2):
            going_right[part] = lax.ppermute(going_right[part], "fsdp", right)
            going_left[part] = lax.ppermute(going_left[part], "fsdp", left)
            if fetches:
                source, index, shape = fetches.pop(0)
                got, going_right[part] = fetch(source, index, shape, going_right[part])
                brought.append(got)
            held[part] += [going_right[part], going_left[part]]
    for part in range(2):
        held[part].append(lax.ppermute(going_right[part][:, :quarter], "fsdp", right))
        held[part].append(lax.ppermute(going_left[part][:, quarter:], "fsdp", left))
    return held, brought


def assemble(pieces, into):
    rows = pieces[0].shape[0]
    for place, piece in enumerate(pieces[:-2]):
        into[place * rows : (place + 1) * rows, :] = piece[...]
    quarter = pieces[-1].shape[1]
    start = (len(pieces) - 2) * rows
    into[start : start + rows, :quarter] = pieces[-2][...]
    into[start : start + rows, quarter:] = pieces[-1][...]


def first_pass(pieces, weights, n_rows):
    half, columns = weights[0].shape

    def body(*refs):
        rows = refs[: len(pieces)]
        weight_refs = refs[len(pieces) : len(pieces) + len(weights)]
        out_ref, whole = refs[len(pieces) + len(weights) :]
        assemble(rows, whole)
        for place, weight_ref in enumerate(weight_refs):
            out_ref[place] = jnp.dot(whole[...], weight_ref[...], preferred_element_type=F32)

    return call(
        body,
        (
            jax.ShapeDtypeStruct((len(weights), n_rows, columns), F32),
            jax.ShapeDtypeStruct((n_rows, half), BF16),
        ),
        [VMEM] * (len(pieces) + len(weights)),
        (VMEM, VMEM),
        flops=2 * len(weights) * n_rows * half * columns,
        nbytes=2 * len(weights) * half * columns,
        name="first_pass",
    )(*pieces, *weights)


def feature_map(projected):
    return jnp.where(projected > 0.0, projected + 1.0, jnp.exp(jnp.minimum(projected, 0.0)))


def keys_and_values(pieces, key_weight, value_weight, first, head_dim):
    _, n_rows, columns = first.shape
    half = key_weight.shape[0]

    def body(*refs):
        rows = refs[: len(pieces)]
        key_ref, value_ref, first_ref, feat_ref, values_ref, state_ref, whole = refs[len(pieces) :]
        assemble(rows, whole)
        tile = min(columns, 256)
        for start in range(0, columns, tile):
            span = slice(start, start + tile)
            projected = first_ref[0, :, span] + jnp.dot(whole[...], key_ref[:, span], preferred_element_type=F32)
            feat = feature_map(projected).astype(BF16)
            feat_ref[:, span] = feat
            projected = first_ref[1, :, span] + jnp.dot(whole[...], value_ref[:, span], preferred_element_type=F32)
            values = projected.astype(BF16)
            values_ref[:, span] = values
            for head in range(start, start + tile, head_dim):
                at = slice(head - start, head - start + head_dim)
                state_ref[head // head_dim] = lax.dot_general(
                    feat[:, at], values[:, at], (((0,), (0,)), ((), ())), preferred_element_type=F32
                ).astype(BF16)

    return call(
        body,
        (
            jax.ShapeDtypeStruct((n_rows, columns), BF16),
            jax.ShapeDtypeStruct((n_rows, columns), BF16),
            jax.ShapeDtypeStruct((columns // head_dim, head_dim, head_dim), BF16),
            jax.ShapeDtypeStruct((n_rows, half), BF16),
        ),
        [VMEM] * (len(pieces) + 3),
        (VMEM,) * 4,
        flops=2 * 2 * n_rows * half * columns,
        nbytes=2 * 2 * half * columns,
        name="keys_and_values",
    )(*pieces, key_weight, value_weight, first)


def queries_within(halves, qkv_weight, feat_k, values, head_dim, size, rows):
    n_rows, columns = feat_k.shape
    half = halves[0].shape[1]
    order = slots(size)
    pieces = 3
    chunk = half // pieces

    def place(shape, axis):
        spot = lax.axis_index("fsdp")
        spot = jnp.where(spot % 2 == 0, spot // 2, size - (spot + 1) // 2)
        row = lax.broadcasted_iota(jnp.int32, shape, axis)
        slot = row // rows
        start = jnp.zeros(shape, jnp.int32)
        for at, distance in enumerate(order):
            there = (spot + distance + size) % size
            holder = jnp.where(there < size // 2, 2 * there, 2 * (size - there) - 1)
            start = jnp.where(slot == at, holder * rows, start)
        return start + row - slot * rows

    def body(first_ref, second_ref, weight_ref, k_ref, v_ref, feat_ref, within_ref, local, sems):
        copies = [
            pltpu.make_async_copy(
                weight_ref.at[0, pl.ds(at * chunk, chunk)], local.at[pl.ds(at * chunk, chunk)], sems.at[at]
            )
            for at in range(2 * pieces)
        ]
        for copy in copies:
            copy.start()
        causal = place((n_rows, 1), 0) >= place((1, n_rows), 1)
        projected = None
        for at, copy in enumerate(copies):
            rows_ref = (first_ref, second_ref)[at // pieces]
            start = (at % pieces) * chunk
            copy.wait()
            product = jnp.dot(
                rows_ref[:, start : start + chunk],
                local[at * chunk : (at + 1) * chunk, :],
                preferred_element_type=F32,
            )
            projected = product if projected is None else projected + product
        feat_ref[...] = feature_map(projected).astype(BF16)
        for head in range(0, columns, head_dim):
            span = slice(head, head + head_dim)
            scores = lax.dot_general(
                feat_ref[:, span], k_ref[:, span], (((1,), (1,)), ((), ())), preferred_element_type=F32
            )
            scores = jnp.where(causal, scores, 0.0).astype(BF16)
            within_ref[:, span] = jnp.dot(scores, v_ref[:, span], preferred_element_type=F32)

    return call(
        body,
        (jax.ShapeDtypeStruct((n_rows, columns), BF16), jax.ShapeDtypeStruct((n_rows, columns), F32)),
        [VMEM, VMEM, HBM, VMEM, VMEM],
        (VMEM,) * 2,
        flops=4 * n_rows * half * columns + 4 * n_rows * n_rows * columns,
        nbytes=4 * half * columns,
        limit=16 << 20,
        scratch_shapes=[
            pltpu.VMEM((2 * half, columns), BF16),
            pltpu.SemaphoreType.DMA((2 * pieces,)),
        ],
        name="queries_within",
    )(*halves, in_hbm(qkv_weight), feat_k, values)


def project_out(normalized, weight_refs, parts, rows):
    for which, weight_ref in enumerate(weight_refs):
        half = weight_ref.shape[1]
        tile = 512 if half % 512 == 0 else 128
        for start in range(0, half, tile):
            span = slice(start, start + tile)
            product = jnp.dot(normalized, weight_ref[:, span], preferred_element_type=F32).astype(BF16)
            for block in range(len(parts) // 2):
                parts[2 * block + which][:, span] = product[block * rows : (block + 1) * rows, :]


def attend_and_project(feat_q, within, initial, others, gain, out_weights, blocks, rows, head_dim):
    n_rows, columns = feat_q.shape
    half = out_weights[0].shape[1]

    def body(q_ref, within_ref, initial_ref, gain_ref, first_ref, second_ref, *refs):
        other_refs, normalized_ref, parts = refs[: len(others)], refs[len(others)], refs[len(others) + 1 :]
        place = lax.axis_index("ctx")
        for head in range(columns // head_dim):
            at = slice(head * head_dim, (head + 1) * head_dim)
            prefix = initial_ref[head]
            for bit, other_ref in enumerate(other_refs):
                later = (place // 2**bit) % 2 == 1
                prefix = prefix + jnp.where(later, other_ref[head].astype(F32), 0.0)
            high = prefix.astype(BF16)
            low = (prefix - high.astype(F32)).astype(BF16)
            q = q_ref[:, at]
            attended = within_ref[:, at] + jnp.dot(q, high, preferred_element_type=F32)
            attended = attended + jnp.dot(q, low, preferred_element_type=F32)
            scale = lax.rsqrt(jnp.mean(attended * attended, axis=-1, keepdims=True) + 1e-06)
            normalized_ref[:, at] = (attended * scale * gain_ref[:, at]).astype(BF16)
        project_out(normalized_ref[n_rows - blocks * rows :, :], (first_ref, second_ref), parts, rows)

    out = call(
        body,
        [jax.ShapeDtypeStruct((n_rows, columns), BF16)] + [jax.ShapeDtypeStruct((rows, half), BF16)] * (2 * blocks),
        [VMEM] * (6 + len(others)),
        [VMEM] * (1 + 2 * blocks),
        flops=4 * n_rows * half * columns,
        nbytes=4 * half * columns,
        name="attend_and_project",
    )(feat_q, within, initial, gain.reshape(1, columns), *out_weights, *others)
    return out[0], [out[1 + 2 * block : 3 + 2 * block] for block in range(blocks)]


def project_rest(normalized, out_weights, blocks, rows):
    columns = normalized.shape[1]
    half = out_weights[0].shape[1]

    def body(normalized_ref, first_ref, second_ref, *parts):
        project_out(normalized_ref[: blocks * rows, :], (first_ref, second_ref), parts, rows)

    out = call(
        body,
        [jax.ShapeDtypeStruct((rows, half), BF16)] * (2 * blocks),
        [VMEM] * 3,
        [VMEM] * (2 * blocks),
        flops=HOP_FLOPS,
        nbytes=4 * half * columns,
        name="project_rest",
    )(normalized, *out_weights)
    return [out[2 * block : 2 * block + 2] for block in range(blocks)]


def add_step(mine_right, got_right, mine_left, got_left):
    def body(mr, gr, ml, gl, to_right, to_left):
        to_right[...] = (mr[...].astype(F32) + gr[...].astype(F32)).astype(BF16)
        to_left[...] = (ml[...].astype(F32) + gl[...].astype(F32)).astype(BF16)

    return call(
        body,
        [jax.ShapeDtypeStruct(mine_right.shape, BF16)] * 2,
        [VMEM] * 4,
        [VMEM] * 2,
        nbytes=12 * mine_right.size,
        limit=4 << 20,
        name="add_step",
    )(mine_right, got_right, mine_left, got_left)


def add_own(own, trailing):
    def body(first, second, got_first, got_second, out):
        out[0] = first[...].astype(F32) + got_first[...].astype(F32)
        out[1] = second[...].astype(F32) + got_second[...].astype(F32)

    return call(
        body,
        jax.ShapeDtypeStruct((2,) + own[0].shape, F32),
        [VMEM] * 4,
        VMEM,
        flops=HOP_FLOPS,
        nbytes=16 * own[0].size,
        limit=4 << 20,
        name="add_own",
    )(*own, *trailing)


def finish(gathered, leading):
    rows, half = leading[0].shape

    def body(gathered_ref, first, second, out):
        out[:, :half] = (gathered_ref[0] + first[...].astype(F32)).astype(BF16)
        out[:, half:] = (gathered_ref[1] + second[...].astype(F32)).astype(BF16)

    return call(
        body,
        jax.ShapeDtypeStruct((rows, 2 * half), BF16),
        [VMEM] * 3,
        VMEM,
        nbytes=4 * rows * half,
        limit=4 << 20,
        name="finish",
    )(gathered, *leading)


def ring_scatter(parts, order, right, left):
    far = max(order)

    def part(distance, half):
        return parts[order.index(distance)][half]

    def hop(to_right, to_left):
        return lax.ppermute(to_right, "fsdp", right), lax.ppermute(to_left, "fsdp", left)

    leading = hop(part(far, 0), part(far, 1))
    trailing = hop(part(far - 1, 1), part(1 - far, 0))
    for step in range(far - 1, 0, -1):
        leading = hop(*add_step(part(step, 0), leading[0], part(-step, 1), leading[1]))
        if step > 1:
            trailing = hop(*add_step(part(step - 1, 1), trailing[0], part(1 - step, 0), trailing[1]))
    gathered = add_own(parts[0], (trailing[1], trailing[0]))
    return finish(gathered, leading)


def add_states(one, two):
    def body(one_ref, two_ref, out_ref):
        out_ref[...] = (one_ref[...].astype(F32) + two_ref[...].astype(F32)).astype(BF16)

    return call(
        body, jax.ShapeDtypeStruct(one.shape, BF16), [VMEM] * 2, VMEM, nbytes=6 * one.size, limit=4 << 20, name="add_states"
    )(one, two)


def exchange_states(state, size):
    others = []
    total = state
    reach = 1
    while reach < size:
        pairs = [(i, i ^ reach) for i in range(size)]
        others.append(lax.ppermute(total, "ctx", pairs))
        reach *= 2
        if reach < size:
            total = add_states(total, others[-1])
    return others


def per_device(n_ctx, n_fsdp, tokens, qkv_weight, out_weight, norm_gain, initial_state):
    rows, width = tokens.shape
    heads_here, head_dim = initial_state.shape[:2]
    columns = heads_here * head_dim
    n_rows = rows * n_fsdp
    right, left = neighbours(n_fsdp)
    order = slots(n_fsdp)

    half = width // 2
    fetches = [(qkv_weight, (s, pl.ds(part * half, half)), (half, columns)) for part in range(2) for s in (1, 2)]
    fetches += [(out_weight, (slice(None), pl.ds(part * half, half)), (columns, half)) for part in range(2)]
    held, brought = ring_gather(tokens, n_fsdp, right, left, fetches)

    first, first_rows = first_pass(held[0], brought[:2], n_rows)
    feat_k, values, state, second_rows = keys_and_values(held[1], brought[2], brought[3], first, head_dim)
    feat_q, within = queries_within((first_rows, second_rows), qkv_weight, feat_k, values, head_dim, n_fsdp, rows)
    others = exchange_states(state, n_ctx)
    soon = 1
    normalized, parts = attend_and_project(
        feat_q, within, initial_state, others, norm_gain, brought[4:], soon, rows, head_dim
    )
    parts = project_rest(normalized, brought[4:], n_fsdp - soon, rows) + parts
    return ring_scatter(parts, order, right, left)


def solution(mesh):
    body = functools.partial(per_device, mesh.shape["ctx"], mesh.shape["fsdp"])
    placed = (
        P(("ctx", "fsdp"), None),
        P(None, None, "fsdp"),
        P("fsdp", None),
        P("fsdp"),
        P("fsdp", None, None),
    )
    return jax.shard_map(
        body, mesh=mesh, in_specs=placed, out_specs=P(("ctx", "fsdp"), None), check_vma=False
    )
```

```python
import functools

import jax
import jax.numpy as jnp
from jax import lax
from jax.experimental import pallas as pl
from jax.experimental.pallas import tpu as pltpu
from jax.sharding import PartitionSpec as P

VMEM = pl.BlockSpec(memory_space=pltpu.VMEM)
ANY = pl.BlockSpec(memory_space=pl.ANY)
HBM = pl.BlockSpec(memory_space=pltpu.HBM)
F32, BF16 = jnp.float32, jnp.bfloat16
HOP_FLOPS = 5 * 10**9


def ring_order(size):
    return list(range(0, size, 2)) + list(range(size - 1, 0, -2))


def neighbours(size):
    ring = ring_order(size)
    right = [(ring[i], ring[(i + 1) % size]) for i in range(size)]
    left = [(b, a) for a, b in right]
    return right, left


def slots(size):
    order = [0]
    for step in range(1, size // 2):
        order += [-step, step]
    return order + [size // 2]


def in_hbm(array):
    return pltpu.with_memory_space_constraint(array, pltpu.HBM)


def call(body, out_shape, in_specs, out_specs, flops=0, nbytes=0, limit=12 << 20, **more):
    return pl.pallas_call(
        body,
        out_shape=out_shape,
        in_specs=in_specs,
        out_specs=out_specs,
        cost_estimate=pl.CostEstimate(flops=flops, bytes_accessed=nbytes, transcendentals=0),
        compiler_params=pltpu.CompilerParams(vmem_limit_bytes=limit),
        **more,
    )


def touch(first, second):
    def body(first_ref, second_ref, first_out, second_out):
        pass

    return call(
        body,
        [jax.ShapeDtypeStruct(first.shape, first.dtype)] * 2,
        [ANY] * 2,
        [ANY] * 2,
        flops=HOP_FLOPS,
        input_output_aliases={0: 0, 1: 1},
        limit=1 << 20,
        name="touch",
    )(first, second)


def ring_gather(block, size, right, left):
    half = block.shape[1] // 2
    quarter = half // 2
    going_right = [block[:, :half], block[:, half:]]
    going_left = list(going_right)
    held = [[going_right[0]], [going_right[1]]]
    for hop in range(1, size // 2):
        for part in range(2):
            going_right[part] = lax.ppermute(going_right[part], "fsdp", right)
            going_left[part] = lax.ppermute(going_left[part], "fsdp", left)
            if hop > 1:
                going_right[part], going_left[part] = touch(going_right[part], going_left[part])
            held[part] += [going_right[part], going_left[part]]
    for part in range(2):
        held[part].append(lax.ppermute(going_right[part][:, :quarter], "fsdp", right))
        held[part].append(lax.ppermute(going_left[part][:, quarter:], "fsdp", left))
    return held


def assemble(pieces, into):
    rows = pieces[0].shape[0]
    for place, piece in enumerate(pieces[:-2]):
        into[place * rows : (place + 1) * rows, :] = piece[...]
    quarter = pieces[-1].shape[1]
    start = (len(pieces) - 2) * rows
    into[start : start + rows, :quarter] = pieces[-2][...]
    into[start : start + rows, quarter:] = pieces[-1][...]


def first_pass(pieces, weight, n_rows):
    half, columns = weight.shape[1] // 2, weight.shape[2]

    def body(*refs):
        rows = refs[: len(pieces)]
        weight_ref, out_ref, whole = refs[len(pieces) :]
        assemble(rows, whole)
        for place in range(2):
            out_ref[place] = jnp.dot(whole[...], weight_ref[1 + place, :half, :], preferred_element_type=F32)

    return call(
        body,
        (
            jax.ShapeDtypeStruct((2, n_rows, columns), F32),
            jax.ShapeDtypeStruct((n_rows, half), BF16),
        ),
        [VMEM] * (len(pieces) + 1),
        (VMEM, VMEM),
        flops=4 * n_rows * half * columns,
        nbytes=4 * half * columns,
        name="first_pass",
    )(*pieces, weight)


def feature_map(projected):
    return jnp.where(projected > 0.0, projected + 1.0, jnp.exp(jnp.minimum(projected, 0.0)))


def keys_and_values(pieces, weight, first, head_dim):
    _, n_rows, columns = first.shape
    half = weight.shape[1] // 2

    def body(*refs):
        rows = refs[: len(pieces)]
        weight_ref, first_ref, feat_ref, values_ref, state_ref, whole = refs[len(pieces) :]
        assemble(rows, whole)
        tile = min(columns, 256)
        for start in range(0, columns, tile):
            span = slice(start, start + tile)
            projected = first_ref[0, :, span] + jnp.dot(whole[...], weight_ref[1, half:, span], preferred_element_type=F32)
            feat = feature_map(projected).astype(BF16)
            feat_ref[:, span] = feat
            projected = first_ref[1, :, span] + jnp.dot(whole[...], weight_ref[2, half:, span], preferred_element_type=F32)
            values = projected.astype(BF16)
            values_ref[:, span] = values
            for head in range(start, start + tile, head_dim):
                at = slice(head - start, head - start + head_dim)
                state_ref[head // head_dim] = lax.dot_general(
                    feat[:, at], values[:, at], (((0,), (0,)), ((), ())), preferred_element_type=F32
                ).astype(BF16)

    return call(
        body,
        (
            jax.ShapeDtypeStruct((n_rows, columns), BF16),
            jax.ShapeDtypeStruct((n_rows, columns), BF16),
            jax.ShapeDtypeStruct((columns // head_dim, head_dim, head_dim), BF16),
            jax.ShapeDtypeStruct((n_rows, half), BF16),
        ),
        [VMEM] * (len(pieces) + 2),
        (VMEM,) * 4,
        flops=2 * 2 * n_rows * half * columns,
        nbytes=2 * 2 * half * columns,
        name="keys_and_values",
    )(*pieces, weight, first)


def queries_within(halves, qkv_weight, feat_k, values, head_dim, size, rows):
    n_rows, columns = feat_k.shape
    half = halves[0].shape[1]
    order = slots(size)

    def place(shape, axis):
        spot = lax.axis_index("fsdp")
        spot = jnp.where(spot % 2 == 0, spot // 2, size - (spot + 1) // 2)
        row = lax.broadcasted_iota(jnp.int32, shape, axis)
        slot = row // rows
        start = jnp.zeros(shape, jnp.int32)
        for at, distance in enumerate(order):
            there = (spot + distance + size) % size
            holder = jnp.where(there < size // 2, 2 * there, 2 * (size - there) - 1)
            start = jnp.where(slot == at, holder * rows, start)
        return start + row - slot * rows

    def body(first_ref, second_ref, weight_ref, k_ref, v_ref, feat_ref, within_ref):
        causal = place((n_rows, 1), 0) >= place((1, n_rows), 1)
        projected = jnp.dot(first_ref[...], weight_ref[0, :half, :], preferred_element_type=F32)
        projected += jnp.dot(second_ref[...], weight_ref[0, half:, :], preferred_element_type=F32)
        feat_ref[...] = feature_map(projected).astype(BF16)
        for head in range(0, columns, head_dim):
            span = slice(head, head + head_dim)
            scores = lax.dot_general(
                feat_ref[:, span], k_ref[:, span], (((1,), (1,)), ((), ())), preferred_element_type=F32
            )
            scores = jnp.where(causal, scores, 0.0).astype(BF16)
            within_ref[:, span] = jnp.dot(scores, v_ref[:, span], preferred_element_type=F32)

    return call(
        body,
        (jax.ShapeDtypeStruct((n_rows, columns), BF16), jax.ShapeDtypeStruct((n_rows, columns), F32)),
        [VMEM] * 5,
        (VMEM,) * 2,
        flops=4 * n_rows * half * columns + 4 * n_rows * n_rows * columns,
        nbytes=4 * half * columns,
        name="queries_within",
    )(*halves, qkv_weight, feat_k, values)


def project_out(normalized, weight_ref, parts, rows):
    half = weight_ref.shape[1] // 2
    for which in range(2):
        tile = 512 if half % 512 == 0 else 128
        for start in range(0, half, tile):
            span = slice(start, start + tile)
            product = jnp.dot(normalized, weight_ref[:, which * half + start : which * half + start + tile], preferred_element_type=F32).astype(BF16)
            for block in range(len(parts) // 2):
                parts[2 * block + which][:, span] = product[block * rows : (block + 1) * rows, :]


def attend_and_project(feat_q, within, initial, others, gain, out_weight, blocks, rows, head_dim):
    n_rows, columns = feat_q.shape
    half = out_weight.shape[1] // 2

    def body(q_ref, within_ref, initial_ref, gain_ref, weight_ref, *refs):
        other_refs, normalized_ref, parts = refs[: len(others)], refs[len(others)], refs[len(others) + 1 :]
        place = lax.axis_index("ctx")
        for head in range(columns // head_dim):
            at = slice(head * head_dim, (head + 1) * head_dim)
            prefix = initial_ref[head]
            for bit, other_ref in enumerate(other_refs):
                later = (place // 2**bit) % 2 == 1
                prefix = prefix + jnp.where(later, other_ref[head].astype(F32), 0.0)
            high = prefix.astype(BF16)
            low = (prefix - high.astype(F32)).astype(BF16)
            q = q_ref[:, at]
            attended = within_ref[:, at] + jnp.dot(q, high, preferred_element_type=F32)
            attended = attended + jnp.dot(q, low, preferred_element_type=F32)
            scale = lax.rsqrt(jnp.mean(attended * attended, axis=-1, keepdims=True) + 1e-06)
            normalized_ref[:, at] = (attended * scale * gain_ref[:, at]).astype(BF16)
        project_out(normalized_ref[n_rows - blocks * rows :, :], weight_ref, parts, rows)

    out = call(
        body,
        [jax.ShapeDtypeStruct((n_rows, columns), BF16)] + [jax.ShapeDtypeStruct((rows, half), BF16)] * (2 * blocks),
        [VMEM] * (5 + len(others)),
        [VMEM] * (1 + 2 * blocks),
        flops=4 * n_rows * half * columns,
        nbytes=4 * half * columns,
        name="attend_and_project",
    )(feat_q, within, initial, gain.reshape(1, columns), out_weight, *others)
    return out[0], [out[1 + 2 * block : 3 + 2 * block] for block in range(blocks)]


def project_rest(normalized, out_weight, blocks, rows):
    columns = normalized.shape[1]
    half = out_weight.shape[1] // 2

    def body(normalized_ref, weight_ref, *parts):
        project_out(normalized_ref[: blocks * rows, :], weight_ref, parts, rows)

    out = call(
        body,
        [jax.ShapeDtypeStruct((rows, half), BF16)] * (2 * blocks),
        [VMEM] * 2,
        [VMEM] * (2 * blocks),
        flops=HOP_FLOPS,
        nbytes=4 * half * columns,
        name="project_rest",
    )(normalized, out_weight)
    return [out[2 * block : 2 * block + 2] for block in range(blocks)]


def add_step(mine_right, got_right, mine_left, got_left):
    def body(mr, gr, ml, gl, to_right, to_left):
        to_right[...] = (mr[...].astype(F32) + gr[...].astype(F32)).astype(BF16)
        to_left[...] = (ml[...].astype(F32) + gl[...].astype(F32)).astype(BF16)

    return call(
        body,
        [jax.ShapeDtypeStruct(mine_right.shape, BF16)] * 2,
        [VMEM] * 4,
        [VMEM] * 2,
        nbytes=12 * mine_right.size,
        limit=4 << 20,
        name="add_step",
    )(mine_right, got_right, mine_left, got_left)


def add_own(own, trailing):
    def body(first, second, got_first, got_second, out):
        out[0] = first[...].astype(F32) + got_first[...].astype(F32)
        out[1] = second[...].astype(F32) + got_second[...].astype(F32)

    return call(
        body,
        jax.ShapeDtypeStruct((2,) + own[0].shape, F32),
        [VMEM] * 4,
        VMEM,
        flops=HOP_FLOPS,
        nbytes=16 * own[0].size,
        limit=4 << 20,
        name="add_own",
    )(*own, *trailing)


def finish(gathered, leading):
    rows, half = leading[0].shape

    def body(gathered_ref, first, second, out):
        out[:, :half] = (gathered_ref[0] + first[...].astype(F32)).astype(BF16)
        out[:, half:] = (gathered_ref[1] + second[...].astype(F32)).astype(BF16)

    return call(
        body,
        jax.ShapeDtypeStruct((rows, 2 * half), BF16),
        [VMEM] * 3,
        VMEM,
        nbytes=4 * rows * half,
        limit=4 << 20,
        name="finish",
    )(gathered, *leading)


def ring_scatter(parts, order, right, left):
    far = max(order)

    def part(distance, half):
        return parts[order.index(distance)][half]

    def hop(to_right, to_left):
        return lax.ppermute(to_right, "fsdp", right), lax.ppermute(to_left, "fsdp", left)

    leading = hop(part(far, 0), part(far, 1))
    trailing = hop(part(far - 1, 1), part(1 - far, 0))
    for step in range(far - 1, 0, -1):
        leading = hop(*add_step(part(step, 0), leading[0], part(-step, 1), leading[1]))
        if step > 1:
            trailing = hop(*add_step(part(step - 1, 1), trailing[0], part(1 - step, 0), trailing[1]))
    gathered = add_own(parts[0], (trailing[1], trailing[0]))
    return finish(gathered, leading)


def add_states(one, two):
    def body(one_ref, two_ref, out_ref):
        out_ref[...] = (one_ref[...].astype(F32) + two_ref[...].astype(F32)).astype(BF16)

    return call(
        body, jax.ShapeDtypeStruct(one.shape, BF16), [VMEM] * 2, VMEM, nbytes=6 * one.size, limit=4 << 20, name="add_states"
    )(one, two)


def exchange_states(state, size):
    others = []
    total = state
    reach = 1
    while reach < size:
        pairs = [(i, i ^ reach) for i in range(size)]
        others.append(lax.ppermute(total, "ctx", pairs))
        reach *= 2
        if reach < size:
            total = add_states(total, others[-1])
    return others


def per_device(n_ctx, n_fsdp, tokens, qkv_weight, out_weight, norm_gain, initial_state):
    rows, width = tokens.shape
    heads_here, head_dim = initial_state.shape[:2]
    columns = heads_here * head_dim
    n_rows = rows * n_fsdp
    right, left = neighbours(n_fsdp)
    order = slots(n_fsdp)

    half = width // 2
    held = ring_gather(tokens, n_fsdp, right, left)

    first, first_rows = first_pass(held[0], qkv_weight, n_rows)
    feat_k, values, state, second_rows = keys_and_values(held[1], qkv_weight, first, head_dim)
    feat_q, within = queries_within((first_rows, second_rows), qkv_weight, feat_k, values, head_dim, n_fsdp, rows)
    others = exchange_states(state, n_ctx)
    soon = 1
    normalized, parts = attend_and_project(
        feat_q, within, initial_state, others, norm_gain, out_weight, soon, rows, head_dim
    )
    parts = project_rest(normalized, out_weight, n_fsdp - soon, rows) + parts
    return ring_scatter(parts, order, right, left)


def solution(mesh):
    body = functools.partial(per_device, mesh.shape["ctx"], mesh.shape["fsdp"])
    placed = (
        P(("ctx", "fsdp"), None),
        P(None, None, "fsdp"),
        P("fsdp", None),
        P("fsdp"),
        P("fsdp", None, None),
    )
    return jax.shard_map(
        body, mesh=mesh, in_specs=placed, out_specs=P(("ctx", "fsdp"), None), check_vma=False
    )
```

```python
import functools

import jax
import jax.numpy as jnp
from jax import lax
from jax.experimental import pallas as pl
from jax.experimental.pallas import tpu as pltpu
from jax.sharding import PartitionSpec as P

VMEM = pl.BlockSpec(memory_space=pltpu.VMEM)
ANY = pl.BlockSpec(memory_space=pl.ANY)
HBM = pl.BlockSpec(memory_space=pltpu.HBM)
F32, BF16 = jnp.float32, jnp.bfloat16
HOP_FLOPS = 5 * 10**9


def ring_order(size):
    return list(range(0, size, 2)) + list(range(size - 1, 0, -2))


def neighbours(size):
    ring = ring_order(size)
    right = [(ring[i], ring[(i + 1) % size]) for i in range(size)]
    left = [(b, a) for a, b in right]
    return right, left


def slots(size):
    order = [0]
    for step in range(1, size // 2):
        order += [-step, step]
    return order + [size // 2]


def in_hbm(array):
    return pltpu.with_memory_space_constraint(array, pltpu.HBM)


def call(body, out_shape, in_specs, out_specs, flops=0, nbytes=0, limit=12 << 20, **more):
    return pl.pallas_call(
        body,
        out_shape=out_shape,
        in_specs=in_specs,
        out_specs=out_specs,
        cost_estimate=pl.CostEstimate(flops=flops, bytes_accessed=nbytes, transcendentals=0),
        compiler_params=pltpu.CompilerParams(vmem_limit_bytes=limit),
        **more,
    )


def mark(arrived):
    def body(arrived_ref, out_ref):
        out_ref[...] = jnp.zeros_like(out_ref)

    return call(
        body,
        jax.ShapeDtypeStruct((8, 128), F32),
        [ANY],
        VMEM,
        flops=HOP_FLOPS,
        limit=1 << 20,
        name="mark",
    )(arrived)


def ring_gather(block, size, right, left):
    half = block.shape[1] // 2
    quarter = half // 2
    going_right = [block[:, :half], block[:, half:]]
    going_left = list(going_right)
    held = [[going_right[0]], [going_right[1]]]
    for hop in range(1, size // 2):
        for part in range(2):
            going_right[part] = lax.ppermute(going_right[part], "fsdp", right)
            going_left[part] = lax.ppermute(going_left[part], "fsdp", left)
            held[part] += [going_right[part], going_left[part]]
    for part in range(2):
        held[part].append(lax.ppermute(going_right[part][:, :quarter], "fsdp", right))
        held[part].append(lax.ppermute(going_left[part][:, quarter:], "fsdp", left))
    return held


def assemble(pieces, into):
    rows = pieces[0].shape[0]
    for place, piece in enumerate(pieces[:-2]):
        into[place * rows : (place + 1) * rows, :] = piece[...]
    quarter = pieces[-1].shape[1]
    start = (len(pieces) - 2) * rows
    into[start : start + rows, :quarter] = pieces[-2][...]
    into[start : start + rows, quarter:] = pieces[-1][...]


def first_pass(pieces, weight, n_rows, marks):
    half, columns = weight.shape[1] // 2, weight.shape[2]

    def body(*refs):
        rows = refs[: len(pieces)]
        weight_ref, out_ref, whole = refs[len(pieces)], *refs[-2:]
        assemble(rows, whole)
        for place in range(2):
            out_ref[place] = jnp.dot(whole[...], weight_ref[1 + place, :half, :], preferred_element_type=F32)

    return call(
        body,
        (
            jax.ShapeDtypeStruct((2, n_rows, columns), F32),
            jax.ShapeDtypeStruct((n_rows, half), BF16),
        ),
        [VMEM] * (len(pieces) + 1) + [ANY] * len(marks),
        (VMEM, VMEM),
        flops=4 * n_rows * half * columns,
        nbytes=4 * half * columns,
        name="first_pass",
    )(*pieces, weight, *marks)


def feature_map(projected):
    return jnp.where(projected > 0.0, projected + 1.0, jnp.exp(jnp.minimum(projected, 0.0)))


def keys_and_values(rows_or_pieces, weight, first, start, count, head_dim):
    _, n_rows, _ = first.shape
    half = weight.shape[1] // 2
    columns = count * head_dim
    whole = not isinstance(rows_or_pieces, list)
    operands = [rows_or_pieces] if whole else rows_or_pieces

    def body(*refs):
        rows = refs[: len(operands)]
        weight_ref, first_ref, feat_ref, values_ref, state_ref = refs[len(operands) : len(operands) + 5]
        if not whole:
            assemble(rows, refs[-1])
        rows_ref = rows[0] if whole else refs[-1]
        span = slice(start * head_dim, start * head_dim + columns)
        projected = first_ref[0, :, span] + jnp.dot(
            rows_ref[...], weight_ref[1, half:, span], preferred_element_type=F32
        )
        feat_ref[...] = feature_map(projected).astype(BF16)
        projected = first_ref[1, :, span] + jnp.dot(
            rows_ref[...], weight_ref[2, half:, span], preferred_element_type=F32
        )
        values_ref[...] = projected.astype(BF16)
        for head in range(count):
            at = slice(head * head_dim, (head + 1) * head_dim)
            state_ref[head] = lax.dot_general(
                feat_ref[:, at], values_ref[:, at], (((0,), (0,)), ((), ())), preferred_element_type=F32
            ).astype(BF16)

    outs = [
        jax.ShapeDtypeStruct((n_rows, columns), BF16),
        jax.ShapeDtypeStruct((n_rows, columns), BF16),
        jax.ShapeDtypeStruct((count, head_dim, head_dim), BF16),
    ]
    if not whole:
        outs.append(jax.ShapeDtypeStruct((n_rows, half), BF16))
    out = call(
        body,
        outs,
        [VMEM] * (len(operands) + 2),
        [VMEM] * len(outs),
        flops=HOP_FLOPS if whole else 4 * n_rows * half * columns,
        nbytes=4 * half * columns,
        name="keys_and_values",
    )(*operands, weight, first)
    return out if whole else (out[:3], out[3])


def queries_within(halves, qkv_weight, groups, head_dim, size, rows):
    n_rows, half = halves[0].shape
    columns = qkv_weight.shape[2]
    per_group = columns // len(groups)
    order = slots(size)

    def place(shape, axis):
        spot = lax.axis_index("fsdp")
        spot = jnp.where(spot % 2 == 0, spot // 2, size - (spot + 1) // 2)
        row = lax.broadcasted_iota(jnp.int32, shape, axis)
        slot = row // rows
        start = jnp.zeros(shape, jnp.int32)
        for at, distance in enumerate(order):
            there = (spot + distance + size) % size
            holder = jnp.where(there < size // 2, 2 * there, 2 * (size - there) - 1)
            start = jnp.where(slot == at, holder * rows, start)
        return start + row - slot * rows

    def body(first_ref, second_ref, weight_ref, *refs):
        group_refs, (feat_ref, within_ref) = refs[:-2], refs[-2:]
        causal = place((n_rows, 1), 0) >= place((1, n_rows), 1)
        projected = jnp.dot(first_ref[...], weight_ref[0, :half, :], preferred_element_type=F32)
        projected += jnp.dot(second_ref[...], weight_ref[0, half:, :], preferred_element_type=F32)
        feat_ref[...] = feature_map(projected).astype(BF16)
        for head in range(0, columns, head_dim):
            span = slice(head, head + head_dim)
            k_ref, v_ref = group_refs[2 * (head // per_group) : 2 * (head // per_group) + 2]
            at = slice(head % per_group, head % per_group + head_dim)
            scores = lax.dot_general(
                feat_ref[:, span], k_ref[:, at], (((1,), (1,)), ((), ())), preferred_element_type=F32
            )
            scores = jnp.where(causal, scores, 0.0).astype(BF16)
            within_ref[:, span] = jnp.dot(scores, v_ref[:, at], preferred_element_type=F32)

    return call(
        body,
        (jax.ShapeDtypeStruct((n_rows, columns), BF16), jax.ShapeDtypeStruct((n_rows, columns), F32)),
        [VMEM] * (3 + 2 * len(groups)),
        (VMEM,) * 2,
        flops=4 * n_rows * half * columns + 4 * n_rows * n_rows * columns,
        nbytes=4 * half * columns,
        name="queries_within",
    )(*halves, qkv_weight, *[array for group in groups for array in group[:2]])


def project_out(normalized, weight_ref, parts, rows):
    half = weight_ref.shape[1] // 2
    for which in range(2):
        tile = 512 if half % 512 == 0 else 128
        for start in range(0, half, tile):
            span = slice(start, start + tile)
            product = jnp.dot(normalized, weight_ref[:, which * half + start : which * half + start + tile], preferred_element_type=F32).astype(BF16)
            for block in range(len(parts) // 2):
                parts[2 * block + which][:, span] = product[block * rows : (block + 1) * rows, :]


def attend_and_project(feat_q, within, initial, exchanged, gain, out_weight, blocks, rows, head_dim):
    per_group = initial.shape[0] // len(exchanged)
    steps = len(exchanged[0])
    others = [other for group in exchanged for other in group]
    n_rows, columns = feat_q.shape
    half = out_weight.shape[1] // 2

    def body(q_ref, within_ref, initial_ref, gain_ref, weight_ref, *refs):
        other_refs, normalized_ref, parts = refs[: len(others)], refs[len(others)], refs[len(others) + 1 :]
        place = lax.axis_index("ctx")
        for head in range(columns // head_dim):
            at = slice(head * head_dim, (head + 1) * head_dim)
            prefix = initial_ref[head]
            group, within_group = divmod(head, per_group)
            for bit, other_ref in enumerate(other_refs[group * steps : (group + 1) * steps]):
                later = (place // 2**bit) % 2 == 1
                prefix = prefix + jnp.where(later, other_ref[within_group].astype(F32), 0.0)
            high = prefix.astype(BF16)
            low = (prefix - high.astype(F32)).astype(BF16)
            q = q_ref[:, at]
            attended = within_ref[:, at] + jnp.dot(q, high, preferred_element_type=F32)
            attended = attended + jnp.dot(q, low, preferred_element_type=F32)
            scale = lax.rsqrt(jnp.mean(attended * attended, axis=-1, keepdims=True) + 1e-06)
            normalized_ref[:, at] = (attended * scale * gain_ref[:, at]).astype(BF16)
        project_out(normalized_ref[n_rows - blocks * rows :, :], weight_ref, parts, rows)

    out = call(
        body,
        [jax.ShapeDtypeStruct((n_rows, columns), BF16)] + [jax.ShapeDtypeStruct((rows, half), BF16)] * (2 * blocks),
        [VMEM] * (5 + len(others)),
        [VMEM] * (1 + 2 * blocks),
        flops=4 * n_rows * half * columns,
        nbytes=4 * half * columns,
        name="attend_and_project",
    )(feat_q, within, initial, gain.reshape(1, columns), out_weight, *others)
    return out[0], [out[1 + 2 * block : 3 + 2 * block] for block in range(blocks)]


def project_rest(normalized, out_weight, blocks, rows):
    columns = normalized.shape[1]
    half = out_weight.shape[1] // 2

    def body(normalized_ref, weight_ref, *parts):
        project_out(normalized_ref[: blocks * rows, :], weight_ref, parts, rows)

    out = call(
        body,
        [jax.ShapeDtypeStruct((rows, half), BF16)] * (2 * blocks),
        [VMEM] * 2,
        [VMEM] * (2 * blocks),
        flops=HOP_FLOPS,
        nbytes=4 * half * columns,
        name="project_rest",
    )(normalized, out_weight)
    return [out[2 * block : 2 * block + 2] for block in range(blocks)]


def add_step(mine_right, got_right, mine_left, got_left):
    def body(mr, gr, ml, gl, to_right, to_left):
        to_right[...] = (mr[...].astype(F32) + gr[...].astype(F32)).astype(BF16)
        to_left[...] = (ml[...].astype(F32) + gl[...].astype(F32)).astype(BF16)

    return call(
        body,
        [jax.ShapeDtypeStruct(mine_right.shape, BF16)] * 2,
        [VMEM] * 4,
        [VMEM] * 2,
        nbytes=12 * mine_right.size,
        limit=4 << 20,
        name="add_step",
    )(mine_right, got_right, mine_left, got_left)


def add_own(own, trailing):
    def body(first, second, got_first, got_second, out):
        out[0] = first[...].astype(F32) + got_first[...].astype(F32)
        out[1] = second[...].astype(F32) + got_second[...].astype(F32)

    return call(
        body,
        jax.ShapeDtypeStruct((2,) + own[0].shape, F32),
        [VMEM] * 4,
        VMEM,
        flops=HOP_FLOPS,
        nbytes=16 * own[0].size,
        limit=4 << 20,
        name="add_own",
    )(*own, *trailing)


def finish(gathered, leading):
    rows, half = leading[0].shape

    def body(gathered_ref, first, second, out):
        out[:, :half] = (gathered_ref[0] + first[...].astype(F32)).astype(BF16)
        out[:, half:] = (gathered_ref[1] + second[...].astype(F32)).astype(BF16)

    return call(
        body,
        jax.ShapeDtypeStruct((rows, 2 * half), BF16),
        [VMEM] * 3,
        VMEM,
        nbytes=4 * rows * half,
        limit=4 << 20,
        name="finish",
    )(gathered, *leading)


def ring_scatter(parts, order, right, left):
    far = max(order)

    def part(distance, half):
        return parts[order.index(distance)][half]

    def hop(to_right, to_left):
        return lax.ppermute(to_right, "fsdp", right), lax.ppermute(to_left, "fsdp", left)

    leading = hop(part(far, 0), part(far, 1))
    trailing = hop(part(far - 1, 1), part(1 - far, 0))
    for step in range(far - 1, 0, -1):
        leading = hop(*add_step(part(step, 0), leading[0], part(-step, 1), leading[1]))
        if step > 1:
            trailing = hop(*add_step(part(step - 1, 1), trailing[0], part(1 - step, 0), trailing[1]))
    gathered = add_own(parts[0], (trailing[1], trailing[0]))
    return finish(gathered, leading)


def add_states(one, two, after):
    def body(one_ref, two_ref, *refs):
        refs[-1][...] = (one_ref[...].astype(F32) + two_ref[...].astype(F32)).astype(BF16)

    return call(
        body,
        jax.ShapeDtypeStruct(one.shape, BF16),
        [VMEM] * 2 + [ANY] * len(after),
        VMEM,
        nbytes=6 * one.size,
        limit=4 << 20,
        name="add_states",
    )(one, two, *after)


def exchange_states(states, size):
    received = [[] for _ in states]
    totals = list(states)
    reach = 1
    while reach < size:
        pairs = [(i, i ^ reach) for i in range(size)]
        for at, total in enumerate(totals):
            received[at].append(lax.ppermute(total, "ctx", pairs))
        reach *= 2
        if reach < size:
            after = []
            for at, total in enumerate(totals):
                totals[at] = add_states(total, received[at][-1], after)
                after = [totals[at]]
    return received


def per_device(n_ctx, n_fsdp, tokens, qkv_weight, out_weight, norm_gain, initial_state):
    rows, width = tokens.shape
    heads_here, head_dim = initial_state.shape[:2]
    columns = heads_here * head_dim
    n_rows = rows * n_fsdp
    right, left = neighbours(n_fsdp)
    order = slots(n_fsdp)

    half = width // 2
    held = ring_gather(tokens, n_fsdp, right, left)

    first, first_rows = first_pass(held[0], qkv_weight, n_rows, [mark(held[1][-6]), mark(held[1][-5])])
    count = heads_here // 2 if heads_here % 2 == 0 else heads_here
    group, second_rows = keys_and_values(held[1], qkv_weight, first, 0, count, head_dim)
    groups = [group]
    for start in range(count, heads_here, count):
        groups.append(keys_and_values(second_rows, qkv_weight, first, start, count, head_dim))
    feat_q, within = queries_within((first_rows, second_rows), qkv_weight, groups, head_dim, n_fsdp, rows)
    exchanged = exchange_states([group[2] for group in groups], n_ctx)
    soon = 1
    normalized, parts = attend_and_project(
        feat_q, within, initial_state, exchanged, norm_gain, out_weight, soon, rows, head_dim
    )
    parts = project_rest(normalized, out_weight, n_fsdp - soon, rows) + parts
    return ring_scatter(parts, order, right, left)


def solution(mesh):
    body = functools.partial(per_device, mesh.shape["ctx"], mesh.shape["fsdp"])
    placed = (
        P(("ctx", "fsdp"), None),
        P(None, None, "fsdp"),
        P("fsdp", None),
        P("fsdp"),
        P("fsdp", None, None),
    )
    return jax.shard_map(
        body, mesh=mesh, in_specs=placed, out_specs=P(("ctx", "fsdp"), None), check_vma=False
    )
```

```python
import functools

import jax
import jax.numpy as jnp
from jax import lax
from jax.experimental import pallas as pl
from jax.experimental.pallas import tpu as pltpu
from jax.sharding import PartitionSpec as P

VMEM = pl.BlockSpec(memory_space=pltpu.VMEM)
ANY = pl.BlockSpec(memory_space=pl.ANY)
HBM = pl.BlockSpec(memory_space=pltpu.HBM)
F32, BF16 = jnp.float32, jnp.bfloat16
HOP_FLOPS = 5 * 10**9


def ring_order(size):
    return list(range(0, size, 2)) + list(range(size - 1, 0, -2))


def neighbours(size):
    ring = ring_order(size)
    right = [(ring[i], ring[(i + 1) % size]) for i in range(size)]
    left = [(b, a) for a, b in right]
    return right, left


def slots(size):
    order = [0]
    for step in range(1, size // 2):
        order += [-step, step]
    return order + [size // 2]


def in_hbm(array):
    return pltpu.with_memory_space_constraint(array, pltpu.HBM)


def call(body, out_shape, in_specs, out_specs, flops=0, nbytes=0, limit=12 << 20, **more):
    return pl.pallas_call(
        body,
        out_shape=out_shape,
        in_specs=in_specs,
        out_specs=out_specs,
        cost_estimate=pl.CostEstimate(flops=flops, bytes_accessed=nbytes, transcendentals=0),
        compiler_params=pltpu.CompilerParams(vmem_limit_bytes=limit),
        **more,
    )


def mark(arrived):
    def body(arrived_ref, out_ref):
        out_ref[...] = jnp.zeros_like(out_ref)

    return call(
        body,
        jax.ShapeDtypeStruct((8, 128), F32),
        [ANY],
        VMEM,
        flops=HOP_FLOPS,
        limit=1 << 20,
        name="mark",
    )(arrived)


def ring_gather(block, size, right, left):
    half = block.shape[1] // 2
    quarter = half // 2
    going_right = [block[:, :half], block[:, half:]]
    going_left = list(going_right)
    held = [[going_right[0]], [going_right[1]]]
    for hop in range(1, size // 2):
        for part in range(2):
            going_right[part] = lax.ppermute(going_right[part], "fsdp", right)
            going_left[part] = lax.ppermute(going_left[part], "fsdp", left)
            held[part] += [going_right[part], going_left[part]]
    for part in range(2):
        held[part].append(lax.ppermute(going_right[part][:, :quarter], "fsdp", right))
        held[part].append(lax.ppermute(going_left[part][:, quarter:], "fsdp", left))
    return held


def assemble(pieces, into):
    rows = pieces[0].shape[0]
    for place, piece in enumerate(pieces[:-2]):
        into[place * rows : (place + 1) * rows, :] = piece[...]
    quarter = pieces[-1].shape[1]
    start = (len(pieces) - 2) * rows
    into[start : start + rows, :quarter] = pieces[-2][...]
    into[start : start + rows, quarter:] = pieces[-1][...]


def first_pass(pieces, weight, n_rows, marks):
    half, columns = weight.shape[1] // 2, weight.shape[2]

    def body(*refs):
        rows = refs[: len(pieces)]
        weight_ref, out_ref, whole = refs[len(pieces)], *refs[-2:]
        assemble(rows, whole)
        for place in range(2):
            out_ref[place] = jnp.dot(whole[...], weight_ref[1 + place, :half, :], preferred_element_type=F32)

    return call(
        body,
        (
            jax.ShapeDtypeStruct((2, n_rows, columns), F32),
            jax.ShapeDtypeStruct((n_rows, half), BF16),
        ),
        [VMEM] * (len(pieces) + 1) + [ANY] * len(marks),
        (VMEM, VMEM),
        flops=4 * n_rows * half * columns,
        nbytes=4 * half * columns,
        name="first_pass",
    )(*pieces, weight, *marks)


def feature_map(projected):
    return jnp.where(projected > 0.0, projected + 1.0, jnp.exp(jnp.minimum(projected, 0.0)))


def keys_and_values(rows_or_pieces, weight, first, start, count, head_dim):
    _, n_rows, _ = first.shape
    half = weight.shape[1] // 2
    columns = count * head_dim
    whole = not isinstance(rows_or_pieces, list)
    operands = [rows_or_pieces] if whole else rows_or_pieces

    def body(*refs):
        rows = refs[: len(operands)]
        weight_ref, first_ref, feat_ref, values_ref, state_ref = refs[len(operands) : len(operands) + 5]
        if not whole:
            assemble(rows, refs[-1])
        rows_ref = rows[0] if whole else refs[-1]
        span = slice(start * head_dim, start * head_dim + columns)
        projected = first_ref[0, :, span] + jnp.dot(
            rows_ref[...], weight_ref[1, half:, span], preferred_element_type=F32
        )
        feat_ref[...] = feature_map(projected).astype(BF16)
        projected = first_ref[1, :, span] + jnp.dot(
            rows_ref[...], weight_ref[2, half:, span], preferred_element_type=F32
        )
        values_ref[...] = projected.astype(BF16)
        for head in range(count):
            at = slice(head * head_dim, (head + 1) * head_dim)
            state_ref[head] = lax.dot_general(
                feat_ref[:, at], values_ref[:, at], (((0,), (0,)), ((), ())), preferred_element_type=F32
            ).astype(BF16)

    outs = [
        jax.ShapeDtypeStruct((n_rows, columns), BF16),
        jax.ShapeDtypeStruct((n_rows, columns), BF16),
        jax.ShapeDtypeStruct((count, head_dim, head_dim), BF16),
    ]
    if not whole:
        outs.append(jax.ShapeDtypeStruct((n_rows, half), BF16))
    out = call(
        body,
        outs,
        [VMEM] * (len(operands) + 2),
        [VMEM] * len(outs),
        flops=HOP_FLOPS if whole else 4 * n_rows * half * columns,
        nbytes=4 * half * columns,
        name="keys_and_values",
    )(*operands, weight, first)
    return out if whole else (out[:3], out[3])


def queries_within(halves, qkv_weight, groups, head_dim, size, rows):
    n_rows, half = halves[0].shape
    columns = qkv_weight.shape[2]
    per_group = columns // len(groups)
    order = slots(size)

    def place(shape, axis):
        spot = lax.axis_index("fsdp")
        spot = jnp.where(spot % 2 == 0, spot // 2, size - (spot + 1) // 2)
        row = lax.broadcasted_iota(jnp.int32, shape, axis)
        slot = row // rows
        start = jnp.zeros(shape, jnp.int32)
        for at, distance in enumerate(order):
            there = (spot + distance + size) % size
            holder = jnp.where(there < size // 2, 2 * there, 2 * (size - there) - 1)
            start = jnp.where(slot == at, holder * rows, start)
        return start + row - slot * rows

    def body(first_ref, second_ref, weight_ref, *refs):
        group_refs, (feat_ref, within_ref) = refs[:-2], refs[-2:]
        causal = place((n_rows, 1), 0) >= place((1, n_rows), 1)
        projected = jnp.dot(first_ref[...], weight_ref[0, :half, :], preferred_element_type=F32)
        projected += jnp.dot(second_ref[...], weight_ref[0, half:, :], preferred_element_type=F32)
        feat_ref[...] = feature_map(projected).astype(BF16)
        for head in range(0, columns, head_dim):
            span = slice(head, head + head_dim)
            k_ref, v_ref = group_refs[2 * (head // per_group) : 2 * (head // per_group) + 2]
            at = slice(head % per_group, head % per_group + head_dim)
            scores = lax.dot_general(
                feat_ref[:, span], k_ref[:, at], (((1,), (1,)), ((), ())), preferred_element_type=F32
            )
            scores = jnp.where(causal, scores, 0.0).astype(BF16)
            within_ref[:, span] = jnp.dot(scores, v_ref[:, at], preferred_element_type=F32)

    return call(
        body,
        (jax.ShapeDtypeStruct((n_rows, columns), BF16), jax.ShapeDtypeStruct((n_rows, columns), F32)),
        [VMEM] * (3 + 2 * len(groups)),
        (VMEM,) * 2,
        flops=4 * n_rows * half * columns + 4 * n_rows * n_rows * columns,
        nbytes=4 * half * columns,
        name="queries_within",
    )(*halves, qkv_weight, *[array for group in groups for array in group[:2]])


def project_out(normalized, weight_ref, parts, rows):
    half = weight_ref.shape[1] // 2
    for which in range(2):
        tile = 512 if half % 512 == 0 else 128
        for start in range(0, half, tile):
            span = slice(start, start + tile)
            product = jnp.dot(normalized, weight_ref[:, which * half + start : which * half + start + tile], preferred_element_type=F32).astype(BF16)
            for block in range(len(parts) // 2):
                parts[2 * block + which][:, span] = product[block * rows : (block + 1) * rows, :]


def attend_and_project(feat_q, within, initial, exchanged, gain, out_weight, blocks, rows, head_dim):
    per_group = initial.shape[0] // len(exchanged)
    steps = len(exchanged[0])
    others = [other for group in exchanged for other in group]
    n_rows, columns = feat_q.shape
    half = out_weight.shape[1] // 2

    def body(q_ref, within_ref, initial_ref, gain_ref, weight_ref, *refs):
        other_refs, normalized_ref, parts = refs[: len(others)], refs[len(others)], refs[len(others) + 1 :]
        place = lax.axis_index("ctx")
        for head in range(columns // head_dim):
            at = slice(head * head_dim, (head + 1) * head_dim)
            prefix = initial_ref[head]
            group, within_group = divmod(head, per_group)
            for bit, other_ref in enumerate(other_refs[group * steps : (group + 1) * steps]):
                later = (place // 2**bit) % 2 == 1
                prefix = prefix + jnp.where(later, other_ref[within_group].astype(F32), 0.0)
            high = prefix.astype(BF16)
            low = (prefix - high.astype(F32)).astype(BF16)
            q = q_ref[:, at]
            attended = within_ref[:, at] + jnp.dot(q, high, preferred_element_type=F32)
            attended = attended + jnp.dot(q, low, preferred_element_type=F32)
            scale = lax.rsqrt(jnp.mean(attended * attended, axis=-1, keepdims=True) + 1e-06)
            normalized_ref[:, at] = (attended * scale * gain_ref[:, at]).astype(BF16)
        project_out(normalized_ref[n_rows - blocks * rows :, :], weight_ref, parts, rows)

    out = call(
        body,
        [jax.ShapeDtypeStruct((n_rows, columns), BF16)] + [jax.ShapeDtypeStruct((rows, half), BF16)] * (2 * blocks),
        [VMEM] * (5 + len(others)),
        [VMEM] * (1 + 2 * blocks),
        flops=4 * n_rows * half * columns,
        nbytes=4 * half * columns,
        name="attend_and_project",
    )(feat_q, within, initial, gain.reshape(1, columns), out_weight, *others)
    return out[0], [out[1 + 2 * block : 3 + 2 * block] for block in range(blocks)]


def project_rest(normalized, out_weight, blocks, rows):
    columns = normalized.shape[1]
    half = out_weight.shape[1] // 2

    def body(normalized_ref, weight_ref, *parts):
        project_out(normalized_ref[: blocks * rows, :], weight_ref, parts, rows)

    out = call(
        body,
        [jax.ShapeDtypeStruct((rows, half), BF16)] * (2 * blocks),
        [VMEM] * 2,
        [VMEM] * (2 * blocks),
        flops=HOP_FLOPS,
        nbytes=4 * half * columns,
        name="project_rest",
    )(normalized, out_weight)
    return [out[2 * block : 2 * block + 2] for block in range(blocks)]


def add_step(mine, got):
    def body(mine_ref, got_ref, out_ref):
        out_ref[...] = (mine_ref[...].astype(F32) + got_ref[...].astype(F32)).astype(BF16)

    return call(
        body,
        jax.ShapeDtypeStruct(mine.shape, BF16),
        [VMEM] * 2,
        VMEM,
        nbytes=6 * mine.size,
        limit=4 << 20,
        name="add_step",
    )(mine, got)


def add_own(own, trailing):
    def body(first, second, got_first, got_second, out):
        out[0] = first[...].astype(F32) + got_first[...].astype(F32)
        out[1] = second[...].astype(F32) + got_second[...].astype(F32)

    return call(
        body,
        jax.ShapeDtypeStruct((2,) + own[0].shape, F32),
        [VMEM] * 4,
        VMEM,
        flops=HOP_FLOPS,
        nbytes=16 * own[0].size,
        limit=4 << 20,
        name="add_own",
    )(*own, *trailing)


def finish(gathered, leading):
    rows, half = leading[0].shape

    def body(gathered_ref, first, second, out):
        out[:, :half] = (gathered_ref[0] + first[...].astype(F32)).astype(BF16)
        out[:, half:] = (gathered_ref[1] + second[...].astype(F32)).astype(BF16)

    return call(
        body,
        jax.ShapeDtypeStruct((rows, 2 * half), BF16),
        [VMEM] * 3,
        VMEM,
        nbytes=4 * rows * half,
        limit=4 << 20,
        name="finish",
    )(gathered, *leading)


def ring_scatter(parts, order, right, left):
    far = max(order)

    def part(distance, half):
        return parts[order.index(distance)][half]

    def hop(to_right, to_left):
        return lax.ppermute(to_right, "fsdp", right), lax.ppermute(to_left, "fsdp", left)

    leading = hop(part(far, 0), part(far, 1))
    trailing = hop(part(far - 1, 1), part(1 - far, 0))
    for step in range(far - 1, 0, -1):
        leading = hop(add_step(part(step, 0), leading[0]), add_step(part(-step, 1), leading[1]))
        if step > 1:
            trailing = hop(
                add_step(part(step - 1, 1), trailing[0]), add_step(part(1 - step, 0), trailing[1])
            )
    gathered = add_own(parts[0], (trailing[1], trailing[0]))
    return finish(gathered, leading)


def add_states(one, two, after):
    def body(one_ref, two_ref, *refs):
        refs[-1][...] = (one_ref[...].astype(F32) + two_ref[...].astype(F32)).astype(BF16)

    return call(
        body,
        jax.ShapeDtypeStruct(one.shape, BF16),
        [VMEM] * 2 + [ANY] * len(after),
        VMEM,
        nbytes=6 * one.size,
        limit=4 << 20,
        name="add_states",
    )(one, two, *after)


def exchange_states(states, size):
    received = [[] for _ in states]
    totals = list(states)
    reach = 1
    while reach < size:
        pairs = [(i, i ^ reach) for i in range(size)]
        for at, total in enumerate(totals):
            received[at].append(lax.ppermute(total, "ctx", pairs))
        reach *= 2
        if reach < size:
            after = []
            for at, total in enumerate(totals):
                totals[at] = add_states(total, received[at][-1], after)
                after = [totals[at]]
    return received


def per_device(n_ctx, n_fsdp, tokens, qkv_weight, out_weight, norm_gain, initial_state):
    rows, width = tokens.shape
    heads_here, head_dim = initial_state.shape[:2]
    columns = heads_here * head_dim
    n_rows = rows * n_fsdp
    right, left = neighbours(n_fsdp)
    order = slots(n_fsdp)

    half = width // 2
    held = ring_gather(tokens, n_fsdp, right, left)

    first, first_rows = first_pass(held[0], qkv_weight, n_rows, [mark(held[1][-6]), mark(held[1][-5])])
    count = heads_here // 2 if heads_here % 2 == 0 else heads_here
    group, second_rows = keys_and_values(held[1], qkv_weight, first, 0, count, head_dim)
    groups = [group]
    for start in range(count, heads_here, count):
        groups.append(keys_and_values(second_rows, qkv_weight, first, start, count, head_dim))
    feat_q, within = queries_within((first_rows, second_rows), qkv_weight, groups, head_dim, n_fsdp, rows)
    exchanged = exchange_states([group[2] for group in groups], n_ctx)
    soon = 1
    normalized, parts = attend_and_project(
        feat_q, within, initial_state, exchanged, norm_gain, out_weight, soon, rows, head_dim
    )
    parts = project_rest(normalized, out_weight, n_fsdp - soon, rows) + parts
    return ring_scatter(parts, order, right, left)


def solution(mesh):
    body = functools.partial(per_device, mesh.shape["ctx"], mesh.shape["fsdp"])
    placed = (
        P(("ctx", "fsdp"), None),
        P(None, None, "fsdp"),
        P("fsdp", None),
        P("fsdp"),
        P("fsdp", None, None),
    )
    return jax.shard_map(
        body, mesh=mesh, in_specs=placed, out_specs=P(("ctx", "fsdp"), None), check_vma=False
    )
```

```python
import functools

import jax
import jax.numpy as jnp
from jax import lax
from jax.experimental import pallas as pl
from jax.experimental.pallas import tpu as pltpu
from jax.sharding import PartitionSpec as P

VMEM = pl.BlockSpec(memory_space=pltpu.VMEM)
ANY = pl.BlockSpec(memory_space=pl.ANY)
HBM = pl.BlockSpec(memory_space=pltpu.HBM)
F32, BF16 = jnp.float32, jnp.bfloat16
HOP_FLOPS = 5 * 10**9


def ring_order(size):
    return list(range(0, size, 2)) + list(range(size - 1, 0, -2))


def neighbours(size):
    ring = ring_order(size)
    right = [(ring[i], ring[(i + 1) % size]) for i in range(size)]
    left = [(b, a) for a, b in right]
    return right, left


def slots(size):
    order = [0]
    for step in range(1, size // 2):
        order += [-step, step]
    return order + [size // 2]


def in_hbm(array):
    return pltpu.with_memory_space_constraint(array, pltpu.HBM)


def call(body, out_shape, in_specs, out_specs, flops=0, nbytes=0, limit=12 << 20, **more):
    return pl.pallas_call(
        body,
        out_shape=out_shape,
        in_specs=in_specs,
        out_specs=out_specs,
        cost_estimate=pl.CostEstimate(flops=flops, bytes_accessed=nbytes, transcendentals=0),
        compiler_params=pltpu.CompilerParams(vmem_limit_bytes=limit),
        **more,
    )


def mark(arrived):
    def body(arrived_ref, out_ref):
        out_ref[...] = jnp.zeros_like(out_ref)

    return call(
        body,
        jax.ShapeDtypeStruct((8, 128), F32),
        [ANY],
        VMEM,
        flops=HOP_FLOPS,
        limit=1 << 20,
        name="mark",
    )(arrived)


def ring_gather(block, size, right, left):
    half = block.shape[1] // 2
    quarter = half // 2
    going_right = [block[:, :half], block[:, half:]]
    going_left = list(going_right)
    held = [[going_right[0]], [going_right[1]]]
    for hop in range(1, size // 2):
        for part in range(2):
            going_right[part] = lax.ppermute(going_right[part], "fsdp", right)
            going_left[part] = lax.ppermute(going_left[part], "fsdp", left)
            held[part] += [going_right[part], going_left[part]]
    for part in range(2):
        held[part].append(lax.ppermute(going_right[part][:, :quarter], "fsdp", right))
        held[part].append(lax.ppermute(going_left[part][:, quarter:], "fsdp", left))
    return held


def assemble(pieces, into, first_row):
    rows = pieces[0].shape[0]
    row = first_row
    column = 0
    for piece in pieces:
        width = piece.shape[1]
        into[row : row + rows, column : column + width] = piece[...]
        column = (column + width) % into.shape[1]
        if column == 0:
            row += rows


def feature_map(projected):
    return jnp.where(projected > 0.0, projected + 1.0, jnp.exp(jnp.minimum(projected, 0.0)))


def early_keys(first_pieces, second_pieces, weight, n_rows):
    _, width, columns = weight.shape
    half = width // 2
    count = len(first_pieces)
    early = count * first_pieces[0].shape[0]

    def body(*refs):
        weight_ref, feat_ref, first_ref, second_ref = refs[2 * count :]
        assemble(refs[:count], first_ref, 0)
        assemble(refs[count : 2 * count], second_ref, 0)
        projected = jnp.dot(first_ref[:early, :], weight_ref[1, :half, :], preferred_element_type=F32)
        projected += jnp.dot(second_ref[:early, :], weight_ref[1, half:, :], preferred_element_type=F32)
        feat_ref[:early, :] = feature_map(projected).astype(BF16)

    return call(
        body,
        [jax.ShapeDtypeStruct((n_rows, columns), BF16)] + [jax.ShapeDtypeStruct((n_rows, half), BF16)] * 2,
        [VMEM] * (2 * count + 1),
        [VMEM] * 3,
        flops=2 * early * width * columns,
        nbytes=2 * width * columns,
        name="early_keys",
    )(*first_pieces, *second_pieces, weight)


def early_values(first_rows, second_rows, weight, early):
    n_rows, half = first_rows.shape
    columns = weight.shape[2]

    def body(first_ref, second_ref, weight_ref, values_ref):
        projected = jnp.dot(first_ref[:early, :], weight_ref[2, :half, :], preferred_element_type=F32)
        projected += jnp.dot(second_ref[:early, :], weight_ref[2, half:, :], preferred_element_type=F32)
        values_ref[:early, :] = projected.astype(BF16)

    return call(
        body,
        jax.ShapeDtypeStruct((n_rows, columns), BF16),
        [VMEM] * 3,
        VMEM,
        flops=4 * early * half * columns,
        nbytes=4 * half * columns,
        name="early_values",
    )(first_rows, second_rows, weight)


def first_pass(pieces, first_rows, weight, early, after):
    n_rows, half = first_rows.shape
    columns = weight.shape[2]
    count = len(pieces)

    def body(*refs):
        weight_ref, (out_ref, whole) = refs[count + 1], refs[-2:]
        assemble(refs[:count], whole, early)
        for place in range(2):
            out_ref[place] = jnp.dot(whole[early:, :], weight_ref[1 + place, :half, :], preferred_element_type=F32)

    return call(
        body,
        (
            jax.ShapeDtypeStruct((2, n_rows - early, columns), F32),
            jax.ShapeDtypeStruct((n_rows, half), BF16),
        ),
        [VMEM] * (count + 2) + [ANY] * len(after),
        (VMEM, VMEM),
        flops=4 * (n_rows - early) * half * columns,
        nbytes=4 * half * columns,
        input_output_aliases={count: 1},
        name="first_pass",
    )(*pieces, first_rows, weight, *after)


def late_keys_and_values(pieces, second_rows, weight, first, feat_k, values, start, count, head_dim, early):
    n_rows, half = second_rows.shape
    columns = count * head_dim
    n_pieces = len(pieces)
    span = slice(start * head_dim, start * head_dim + columns)

    def body(*refs):
        weight_ref, first_ref = refs[n_pieces + 1 : n_pieces + 3]
        rows_ref, feat_ref, values_ref, state_ref = refs[-4:]
        if pieces:
            assemble(refs[:n_pieces], rows_ref, early)
        projected = first_ref[0, :, span] + jnp.dot(
            rows_ref[early:, :], weight_ref[1, half:, span], preferred_element_type=F32
        )
        feat_ref[early:, span] = feature_map(projected).astype(BF16)
        projected = first_ref[1, :, span] + jnp.dot(
            rows_ref[early:, :], weight_ref[2, half:, span], preferred_element_type=F32
        )
        values_ref[early:, span] = projected.astype(BF16)
        for head in range(count):
            at = slice((start + head) * head_dim, (start + head + 1) * head_dim)
            state_ref[head] = lax.dot_general(
                feat_ref[:, at], values_ref[:, at], (((0,), (0,)), ((), ())), preferred_element_type=F32
            ).astype(BF16)

    return call(
        body,
        [jax.ShapeDtypeStruct(array.shape, BF16) for array in (second_rows, feat_k, values)]
        + [jax.ShapeDtypeStruct((count, head_dim, head_dim), BF16)],
        [VMEM] * (n_pieces + 5),
        [VMEM] * 4,
        flops=4 * (n_rows - early) * half * columns if pieces else HOP_FLOPS,
        nbytes=4 * half * columns,
        input_output_aliases={n_pieces: 0, n_pieces + 3: 1, n_pieces + 4: 2},
        name="late_keys_and_values",
    )(*pieces, second_rows, weight, first, feat_k, values)


def queries_within(halves, qkv_weight, feat_k, values, head_dim, size, rows):
    n_rows, half = halves[0].shape
    columns = qkv_weight.shape[2]
    order = slots(size)

    def place(shape, axis):
        spot = lax.axis_index("fsdp")
        spot = jnp.where(spot % 2 == 0, spot // 2, size - (spot + 1) // 2)
        row = lax.broadcasted_iota(jnp.int32, shape, axis)
        slot = row // rows
        start = jnp.zeros(shape, jnp.int32)
        for at, distance in enumerate(order):
            there = (spot + distance + size) % size
            holder = jnp.where(there < size // 2, 2 * there, 2 * (size - there) - 1)
            start = jnp.where(slot == at, holder * rows, start)
        return start + row - slot * rows

    def body(first_ref, second_ref, weight_ref, k_ref, v_ref, feat_ref, within_ref):
        causal = place((n_rows, 1), 0) >= place((1, n_rows), 1)
        projected = jnp.dot(first_ref[...], weight_ref[0, :half, :], preferred_element_type=F32)
        projected += jnp.dot(second_ref[...], weight_ref[0, half:, :], preferred_element_type=F32)
        feat_ref[...] = feature_map(projected).astype(BF16)
        for head in range(0, columns, head_dim):
            span = slice(head, head + head_dim)
            scores = lax.dot_general(
                feat_ref[:, span], k_ref[:, span], (((1,), (1,)), ((), ())), preferred_element_type=F32
            )
            scores = jnp.where(causal, scores, 0.0).astype(BF16)
            within_ref[:, span] = jnp.dot(scores, v_ref[:, span], preferred_element_type=F32)

    return call(
        body,
        (jax.ShapeDtypeStruct((n_rows, columns), BF16), jax.ShapeDtypeStruct((n_rows, columns), F32)),
        [VMEM] * 5,
        (VMEM,) * 2,
        flops=4 * n_rows * half * columns + 4 * n_rows * n_rows * columns,
        nbytes=4 * half * columns,
        name="queries_within",
    )(*halves, qkv_weight, feat_k, values)


def project_out(normalized, weight_ref, parts, rows):
    half = weight_ref.shape[1] // 2
    for which in range(2):
        tile = 512 if half % 512 == 0 else 128
        for start in range(0, half, tile):
            span = slice(start, start + tile)
            product = jnp.dot(normalized, weight_ref[:, which * half + start : which * half + start + tile], preferred_element_type=F32).astype(BF16)
            for block in range(len(parts) // 2):
                parts[2 * block + which][:, span] = product[block * rows : (block + 1) * rows, :]


def attend_and_project(feat_q, within, initial, exchanged, gain, out_weight, blocks, rows, head_dim):
    per_group = initial.shape[0] // len(exchanged)
    steps = len(exchanged[0])
    others = [other for group in exchanged for other in group]
    n_rows, columns = feat_q.shape
    half = out_weight.shape[1] // 2

    def body(q_ref, within_ref, initial_ref, gain_ref, weight_ref, *refs):
        other_refs, normalized_ref, parts = refs[: len(others)], refs[len(others)], refs[len(others) + 1 :]
        place = lax.axis_index("ctx")
        for head in range(columns // head_dim):
            at = slice(head * head_dim, (head + 1) * head_dim)
            prefix = initial_ref[head]
            group, within_group = divmod(head, per_group)
            for bit, other_ref in enumerate(other_refs[group * steps : (group + 1) * steps]):
                later = (place // 2**bit) % 2 == 1
                prefix = prefix + jnp.where(later, other_ref[within_group].astype(F32), 0.0)
            high = prefix.astype(BF16)
            low = (prefix - high.astype(F32)).astype(BF16)
            q = q_ref[:, at]
            attended = within_ref[:, at] + jnp.dot(q, high, preferred_element_type=F32)
            attended = attended + jnp.dot(q, low, preferred_element_type=F32)
            scale = lax.rsqrt(jnp.mean(attended * attended, axis=-1, keepdims=True) + 1e-06)
            normalized_ref[:, at] = (attended * scale * gain_ref[:, at]).astype(BF16)
        project_out(normalized_ref[n_rows - blocks * rows :, :], weight_ref, parts, rows)

    out = call(
        body,
        [jax.ShapeDtypeStruct((n_rows, columns), BF16)] + [jax.ShapeDtypeStruct((rows, half), BF16)] * (2 * blocks),
        [VMEM] * (5 + len(others)),
        [VMEM] * (1 + 2 * blocks),
        flops=4 * n_rows * half * columns,
        nbytes=4 * half * columns,
        name="attend_and_project",
    )(feat_q, within, initial, gain.reshape(1, columns), out_weight, *others)
    return out[0], [out[1 + 2 * block : 3 + 2 * block] for block in range(blocks)]


def project_rest(normalized, out_weight, blocks, rows):
    columns = normalized.shape[1]
    half = out_weight.shape[1] // 2

    def body(normalized_ref, weight_ref, *parts):
        project_out(normalized_ref[: blocks * rows, :], weight_ref, parts, rows)

    out = call(
        body,
        [jax.ShapeDtypeStruct((rows, half), BF16)] * (2 * blocks),
        [VMEM] * 2,
        [VMEM] * (2 * blocks),
        flops=HOP_FLOPS,
        nbytes=4 * half * columns,
        name="project_rest",
    )(normalized, out_weight)
    return [out[2 * block : 2 * block + 2] for block in range(blocks)]


def add_step(mine, got):
    def body(mine_ref, got_ref, out_ref):
        out_ref[...] = (mine_ref[...].astype(F32) + got_ref[...].astype(F32)).astype(BF16)

    return call(
        body,
        jax.ShapeDtypeStruct(mine.shape, BF16),
        [VMEM] * 2,
        VMEM,
        nbytes=6 * mine.size,
        limit=4 << 20,
        name="add_step",
    )(mine, got)


def add_own(own, trailing):
    def body(first, second, got_first, got_second, out):
        out[0] = first[...].astype(F32) + got_first[...].astype(F32)
        out[1] = second[...].astype(F32) + got_second[...].astype(F32)

    return call(
        body,
        jax.ShapeDtypeStruct((2,) + own[0].shape, F32),
        [VMEM] * 4,
        VMEM,
        flops=HOP_FLOPS,
        nbytes=16 * own[0].size,
        limit=4 << 20,
        name="add_own",
    )(*own, *trailing)


def finish(gathered, leading):
    rows, half = leading[0].shape

    def body(gathered_ref, first, second, out):
        out[:, :half] = (gathered_ref[0] + first[...].astype(F32)).astype(BF16)
        out[:, half:] = (gathered_ref[1] + second[...].astype(F32)).astype(BF16)

    return call(
        body,
        jax.ShapeDtypeStruct((rows, 2 * half), BF16),
        [VMEM] * 3,
        VMEM,
        nbytes=4 * rows * half,
        limit=4 << 20,
        name="finish",
    )(gathered, *leading)


def ring_scatter(parts, order, right, left):
    far = max(order)

    def part(distance, half):
        return parts[order.index(distance)][half]

    def hop(to_right, to_left):
        return lax.ppermute(to_right, "fsdp", right), lax.ppermute(to_left, "fsdp", left)

    leading = hop(part(far, 0), part(far, 1))
    trailing = hop(part(far - 1, 1), part(1 - far, 0))
    for step in range(far - 1, 0, -1):
        leading = hop(add_step(part(step, 0), leading[0]), add_step(part(-step, 1), leading[1]))
        if step > 1:
            trailing = hop(
                add_step(part(step - 1, 1), trailing[0]), add_step(part(1 - step, 0), trailing[1])
            )
    gathered = add_own(parts[0], (trailing[1], trailing[0]))
    return finish(gathered, leading)


def add_states(one, two, after):
    def body(one_ref, two_ref, *refs):
        refs[-1][...] = (one_ref[...].astype(F32) + two_ref[...].astype(F32)).astype(BF16)

    return call(
        body,
        jax.ShapeDtypeStruct(one.shape, BF16),
        [VMEM] * 2 + [ANY] * len(after),
        VMEM,
        nbytes=6 * one.size,
        limit=4 << 20,
        name="add_states",
    )(one, two, *after)


def exchange_states(states, size):
    received = [[] for _ in states]
    totals = list(states)
    reach = 1
    while reach < size:
        pairs = [(i, i ^ reach) for i in range(size)]
        for at, total in enumerate(totals):
            received[at].append(lax.ppermute(total, "ctx", pairs))
        reach *= 2
        if reach < size:
            after = []
            for at, total in enumerate(totals):
                totals[at] = add_states(total, received[at][-1], after)
                after = [totals[at]]
    return received


def per_device(n_ctx, n_fsdp, tokens, qkv_weight, out_weight, norm_gain, initial_state):
    rows, width = tokens.shape
    heads_here, head_dim = initial_state.shape[:2]
    columns = heads_here * head_dim
    n_rows = rows * n_fsdp
    right, left = neighbours(n_fsdp)
    order = slots(n_fsdp)

    half = width // 2
    held = ring_gather(tokens, n_fsdp, right, left)

    blocks = n_fsdp - 3
    early = blocks * rows
    marks = [mark(held[1][1]), mark(held[1][2])]
    feat_k, first_rows, second_rows = early_keys(held[0][:blocks], held[1][:blocks], qkv_weight, n_rows)
    values = early_values(first_rows, second_rows, qkv_weight, early)
    first, first_rows = first_pass(held[0][blocks:], first_rows, qkv_weight, early, [values, feat_k] + marks)
    count = heads_here // 2 if heads_here % 2 == 0 else heads_here
    states = []
    for start in range(0, heads_here, count):
        pieces = held[1][blocks:] if start == 0 else []
        second_rows, feat_k, values, state = late_keys_and_values(
            pieces, second_rows, qkv_weight, first, feat_k, values, start, count, head_dim, early
        )
        states.append(state)
    feat_q, within = queries_within((first_rows, second_rows), qkv_weight, feat_k, values, head_dim, n_fsdp, rows)
    exchanged = exchange_states(states, n_ctx)
    soon = 1
    normalized, parts = attend_and_project(
        feat_q, within, initial_state, exchanged, norm_gain, out_weight, soon, rows, head_dim
    )
    parts = project_rest(normalized, out_weight, n_fsdp - soon, rows) + parts
    return ring_scatter(parts, order, right, left)


def solution(mesh):
    body = functools.partial(per_device, mesh.shape["ctx"], mesh.shape["fsdp"])
    placed = (
        P(("ctx", "fsdp"), None),
        P(None, None, "fsdp"),
        P("fsdp", None),
        P("fsdp"),
        P("fsdp", None, None),
    )
    return jax.shard_map(
        body, mesh=mesh, in_specs=placed, out_specs=P(("ctx", "fsdp"), None), check_vma=False
    )
```

```python
import functools

import jax
import jax.numpy as jnp
from jax import lax
from jax.experimental import pallas as pl
from jax.experimental.pallas import tpu as pltpu
from jax.sharding import PartitionSpec as P

VMEM = pl.BlockSpec(memory_space=pltpu.VMEM)
ANY = pl.BlockSpec(memory_space=pl.ANY)
HBM = pl.BlockSpec(memory_space=pltpu.HBM)
F32, BF16 = jnp.float32, jnp.bfloat16
HOP_FLOPS = 5 * 10**9


def ring_order(size):
    return list(range(0, size, 2)) + list(range(size - 1, 0, -2))


def neighbours(size):
    ring = ring_order(size)
    right = [(ring[i], ring[(i + 1) % size]) for i in range(size)]
    left = [(b, a) for a, b in right]
    return right, left


def slots(size):
    order = [0]
    for step in range(1, size // 2):
        order += [-step, step]
    return order + [size // 2]


def in_hbm(array):
    return pltpu.with_memory_space_constraint(array, pltpu.HBM)


def call(body, out_shape, in_specs, out_specs, flops=0, nbytes=0, limit=12 << 20, **more):
    return pl.pallas_call(
        body,
        out_shape=out_shape,
        in_specs=in_specs,
        out_specs=out_specs,
        cost_estimate=pl.CostEstimate(flops=flops, bytes_accessed=nbytes, transcendentals=0),
        compiler_params=pltpu.CompilerParams(vmem_limit_bytes=limit),
        **more,
    )


def mark(arrived):
    def body(arrived_ref, out_ref):
        out_ref[...] = jnp.zeros_like(out_ref)

    return call(
        body,
        jax.ShapeDtypeStruct((8, 128), F32),
        [ANY],
        VMEM,
        flops=HOP_FLOPS,
        limit=1 << 20,
        name="mark",
    )(arrived)


def ring_gather(block, size, right, left):
    half = block.shape[1] // 2
    quarter = half // 2
    going_right = [block[:, :half], block[:, half:]]
    going_left = list(going_right)
    held = [[going_right[0]], [going_right[1]]]
    for hop in range(1, size // 2):
        for part in range(2):
            going_right[part] = lax.ppermute(going_right[part], "fsdp", right)
            going_left[part] = lax.ppermute(going_left[part], "fsdp", left)
            held[part] += [going_right[part], going_left[part]]
    for part in range(2):
        held[part].append(lax.ppermute(going_right[part][:, :quarter], "fsdp", right))
        held[part].append(lax.ppermute(going_left[part][:, quarter:], "fsdp", left))
    return held


def assemble(pieces, into, first_row):
    rows = pieces[0].shape[0]
    row = first_row
    column = 0
    for piece in pieces:
        width = piece.shape[1]
        into[row : row + rows, column : column + width] = piece[...]
        column = (column + width) % into.shape[1]
        if column == 0:
            row += rows


def feature_map(projected):
    return jnp.where(projected > 0.0, projected + 1.0, jnp.exp(jnp.minimum(projected, 0.0)))


def early_keys(first_pieces, second_pieces, weight, n_rows):
    _, width, columns = weight.shape
    half = width // 2
    count = len(first_pieces)
    early = count * first_pieces[0].shape[0]

    def body(*refs):
        weight_ref, feat_ref, first_ref, second_ref = refs[2 * count :]
        assemble(refs[:count], first_ref, 0)
        assemble(refs[count : 2 * count], second_ref, 0)
        projected = jnp.dot(first_ref[:early, :], weight_ref[1, :half, :], preferred_element_type=F32)
        projected += jnp.dot(second_ref[:early, :], weight_ref[1, half:, :], preferred_element_type=F32)
        feat_ref[:early, :] = feature_map(projected).astype(BF16)

    return call(
        body,
        [jax.ShapeDtypeStruct((n_rows, columns), BF16)] + [jax.ShapeDtypeStruct((n_rows, half), BF16)] * 2,
        [VMEM] * (2 * count + 1),
        [VMEM] * 3,
        flops=2 * early * width * columns,
        nbytes=2 * width * columns,
        name="early_keys",
    )(*first_pieces, *second_pieces, weight)


def early_values(first_rows, second_rows, weight, early):
    n_rows, half = first_rows.shape
    columns = weight.shape[2]

    def body(first_ref, second_ref, weight_ref, values_ref):
        projected = jnp.dot(first_ref[:early, :], weight_ref[2, :half, :], preferred_element_type=F32)
        projected += jnp.dot(second_ref[:early, :], weight_ref[2, half:, :], preferred_element_type=F32)
        values_ref[:early, :] = projected.astype(BF16)

    return call(
        body,
        jax.ShapeDtypeStruct((n_rows, columns), BF16),
        [VMEM] * 3,
        VMEM,
        flops=4 * early * half * columns,
        nbytes=4 * half * columns,
        name="early_values",
    )(first_rows, second_rows, weight)


def first_pass(pieces, first_rows, weight, early, after):
    n_rows, half = first_rows.shape
    columns = weight.shape[2]
    count = len(pieces)

    def body(*refs):
        weight_ref, (out_ref, whole) = refs[count + 1], refs[-2:]
        assemble(refs[:count], whole, early)
        for place in range(2):
            out_ref[place] = jnp.dot(whole[early:, :], weight_ref[1 + place, :half, :], preferred_element_type=F32)

    return call(
        body,
        (
            jax.ShapeDtypeStruct((2, n_rows - early, columns), F32),
            jax.ShapeDtypeStruct((n_rows, half), BF16),
        ),
        [VMEM] * (count + 2) + [ANY] * len(after),
        (VMEM, VMEM),
        flops=4 * (n_rows - early) * half * columns,
        nbytes=4 * half * columns,
        input_output_aliases={count: 1},
        name="first_pass",
    )(*pieces, first_rows, weight, *after)


def late_keys_and_values(pieces, second_rows, weight, first, feat_k, values, start, count, head_dim, early):
    n_rows, half = second_rows.shape
    columns = count * head_dim
    n_pieces = len(pieces)
    span = slice(start * head_dim, start * head_dim + columns)

    def body(*refs):
        weight_ref, first_ref = refs[n_pieces + 1 : n_pieces + 3]
        rows_ref, feat_ref, values_ref, state_ref = refs[-4:]
        if pieces:
            assemble(refs[:n_pieces], rows_ref, early)
        projected = first_ref[0, :, span] + jnp.dot(
            rows_ref[early:, :], weight_ref[1, half:, span], preferred_element_type=F32
        )
        feat_ref[early:, span] = feature_map(projected).astype(BF16)
        projected = first_ref[1, :, span] + jnp.dot(
            rows_ref[early:, :], weight_ref[2, half:, span], preferred_element_type=F32
        )
        values_ref[early:, span] = projected.astype(BF16)
        for head in range(count):
            at = slice((start + head) * head_dim, (start + head + 1) * head_dim)
            state_ref[head] = lax.dot_general(
                feat_ref[:, at], values_ref[:, at], (((0,), (0,)), ((), ())), preferred_element_type=F32
            ).astype(BF16)

    return call(
        body,
        [jax.ShapeDtypeStruct(array.shape, BF16) for array in (second_rows, feat_k, values)]
        + [jax.ShapeDtypeStruct((count, head_dim, head_dim), BF16)],
        [VMEM] * (n_pieces + 5),
        [VMEM] * 4,
        flops=4 * (n_rows - early) * half * columns if pieces else HOP_FLOPS,
        nbytes=4 * half * columns,
        input_output_aliases={n_pieces: 0, n_pieces + 3: 1, n_pieces + 4: 2},
        name="late_keys_and_values",
    )(*pieces, second_rows, weight, first, feat_k, values)


def queries_within(halves, qkv_weight, feat_k, values, head_dim, size, rows):
    n_rows, half = halves[0].shape
    columns = qkv_weight.shape[2]
    order = slots(size)

    def place(shape, axis):
        spot = lax.axis_index("fsdp")
        spot = jnp.where(spot % 2 == 0, spot // 2, size - (spot + 1) // 2)
        row = lax.broadcasted_iota(jnp.int32, shape, axis)
        slot = row // rows
        start = jnp.zeros(shape, jnp.int32)
        for at, distance in enumerate(order):
            there = (spot + distance + size) % size
            holder = jnp.where(there < size // 2, 2 * there, 2 * (size - there) - 1)
            start = jnp.where(slot == at, holder * rows, start)
        return start + row - slot * rows

    def body(first_ref, second_ref, weight_ref, k_ref, v_ref, feat_ref, within_ref):
        causal = place((n_rows, 1), 0) >= place((1, n_rows), 1)
        projected = jnp.dot(first_ref[...], weight_ref[0, :half, :], preferred_element_type=F32)
        projected += jnp.dot(second_ref[...], weight_ref[0, half:, :], preferred_element_type=F32)
        feat_ref[...] = feature_map(projected).astype(BF16)
        for head in range(0, columns, head_dim):
            span = slice(head, head + head_dim)
            scores = lax.dot_general(
                feat_ref[:, span], k_ref[:, span], (((1,), (1,)), ((), ())), preferred_element_type=F32
            )
            scores = jnp.where(causal, scores, 0.0).astype(BF16)
            within_ref[:, span] = jnp.dot(scores, v_ref[:, span], preferred_element_type=F32)

    return call(
        body,
        (jax.ShapeDtypeStruct((n_rows, columns), BF16), jax.ShapeDtypeStruct((n_rows, columns), F32)),
        [VMEM] * 5,
        (VMEM,) * 2,
        flops=4 * n_rows * half * columns + 4 * n_rows * n_rows * columns,
        nbytes=4 * half * columns,
        name="queries_within",
    )(*halves, qkv_weight, feat_k, values)


def project_out(normalized, weight_ref, parts, rows):
    half = weight_ref.shape[1] // 2
    for which in range(2):
        tile = 512 if half % 512 == 0 else 128
        for start in range(0, half, tile):
            span = slice(start, start + tile)
            product = jnp.dot(normalized, weight_ref[:, which * half + start : which * half + start + tile], preferred_element_type=F32).astype(BF16)
            for block in range(len(parts) // 2):
                parts[2 * block + which][:, span] = product[block * rows : (block + 1) * rows, :]


def attend_and_project(feat_q, within, initial, exchanged, gain, out_weight, blocks, rows, head_dim):
    per_group = initial.shape[0] // len(exchanged)
    steps = len(exchanged[0])
    others = [other for group in exchanged for other in group]
    n_rows, columns = feat_q.shape
    half = out_weight.shape[1] // 2

    def body(q_ref, within_ref, initial_ref, gain_ref, weight_ref, *refs):
        other_refs, normalized_ref, parts = refs[: len(others)], refs[len(others)], refs[len(others) + 1 :]
        place = lax.axis_index("ctx")
        for head in range(columns // head_dim):
            at = slice(head * head_dim, (head + 1) * head_dim)
            prefix = initial_ref[head]
            group, within_group = divmod(head, per_group)
            for bit, other_ref in enumerate(other_refs[group * steps : (group + 1) * steps]):
                later = (place // 2**bit) % 2 == 1
                prefix = prefix + jnp.where(later, other_ref[within_group].astype(F32), 0.0)
            high = prefix.astype(BF16)
            low = (prefix - high.astype(F32)).astype(BF16)
            q = q_ref[:, at]
            attended = within_ref[:, at] + jnp.dot(q, high, preferred_element_type=F32)
            attended = attended + jnp.dot(q, low, preferred_element_type=F32)
            scale = lax.rsqrt(jnp.mean(attended * attended, axis=-1, keepdims=True) + 1e-06)
            normalized_ref[:, at] = (attended * scale * gain_ref[:, at]).astype(BF16)
        project_out(normalized_ref[n_rows - blocks * rows :, :], weight_ref, parts, rows)

    out = call(
        body,
        [jax.ShapeDtypeStruct((n_rows, columns), BF16)] + [jax.ShapeDtypeStruct((rows, half), BF16)] * (2 * blocks),
        [VMEM] * (5 + len(others)),
        [VMEM] * (1 + 2 * blocks),
        flops=4 * n_rows * half * columns,
        nbytes=4 * half * columns,
        name="attend_and_project",
    )(feat_q, within, initial, gain.reshape(1, columns), out_weight, *others)
    return out[0], [out[1 + 2 * block : 3 + 2 * block] for block in range(blocks)]


def project_rest(normalized, out_weight, blocks, rows):
    columns = normalized.shape[1]
    half = out_weight.shape[1] // 2

    def body(normalized_ref, weight_ref, *parts):
        project_out(normalized_ref[: blocks * rows, :], weight_ref, parts, rows)

    out = call(
        body,
        [jax.ShapeDtypeStruct((rows, half), BF16)] * (2 * blocks),
        [VMEM] * 2,
        [VMEM] * (2 * blocks),
        flops=HOP_FLOPS,
        nbytes=4 * half * columns,
        name="project_rest",
    )(normalized, out_weight)
    return [out[2 * block : 2 * block + 2] for block in range(blocks)]


def add_step(mine, got):
    def body(mine_ref, got_ref, out_ref):
        out_ref[...] = (mine_ref[...].astype(F32) + got_ref[...].astype(F32)).astype(BF16)

    return call(
        body,
        jax.ShapeDtypeStruct(mine.shape, BF16),
        [VMEM] * 2,
        VMEM,
        nbytes=6 * mine.size,
        limit=4 << 20,
        name="add_step",
    )(mine, got)


def add_own(own, trailing):
    def body(first, second, got_first, got_second, out):
        out[0] = first[...].astype(F32) + got_first[...].astype(F32)
        out[1] = second[...].astype(F32) + got_second[...].astype(F32)

    return call(
        body,
        jax.ShapeDtypeStruct((2,) + own[0].shape, F32),
        [VMEM] * 4,
        VMEM,
        flops=HOP_FLOPS,
        nbytes=16 * own[0].size,
        limit=4 << 20,
        name="add_own",
    )(*own, *trailing)


def finish(gathered, leading):
    rows, half = leading[0].shape

    def body(gathered_ref, first, second, out):
        out[:, :half] = (gathered_ref[0] + first[...].astype(F32)).astype(BF16)
        out[:, half:] = (gathered_ref[1] + second[...].astype(F32)).astype(BF16)

    return call(
        body,
        jax.ShapeDtypeStruct((rows, 2 * half), BF16),
        [VMEM] * 3,
        VMEM,
        nbytes=4 * rows * half,
        limit=4 << 20,
        name="finish",
    )(gathered, *leading)


def ring_scatter(parts, order, right, left):
    far = max(order)

    def part(distance, half):
        return parts[order.index(distance)][half]

    def hop(to_right, to_left):
        return lax.ppermute(to_right, "fsdp", right), lax.ppermute(to_left, "fsdp", left)

    leading = hop(part(far, 0), part(far, 1))
    trailing = hop(part(far - 1, 1), part(1 - far, 0))
    for step in range(far - 1, 0, -1):
        leading = hop(add_step(part(step, 0), leading[0]), add_step(part(-step, 1), leading[1]))
        if step > 1:
            trailing = hop(
                add_step(part(step - 1, 1), trailing[0]), add_step(part(1 - step, 0), trailing[1])
            )
    gathered = add_own(parts[0], (trailing[1], trailing[0]))
    return finish(gathered, leading)


def add_states(one, two, after):
    def body(one_ref, two_ref, *refs):
        refs[-1][...] = (one_ref[...].astype(F32) + two_ref[...].astype(F32)).astype(BF16)

    return call(
        body,
        jax.ShapeDtypeStruct(one.shape, BF16),
        [VMEM] * 2 + [ANY] * len(after),
        VMEM,
        nbytes=6 * one.size,
        limit=4 << 20,
        name="add_states",
    )(one, two, *after)


def exchange_states(states, size):
    received = [[] for _ in states]
    totals = list(states)
    reach = 1
    while reach < size:
        pairs = [(i, i ^ reach) for i in range(size)]
        for at, total in enumerate(totals):
            received[at].append(lax.ppermute(total, "ctx", pairs))
        reach *= 2
        if reach < size:
            after = []
            for at, total in enumerate(totals):
                totals[at] = add_states(total, received[at][-1], after)
                after = [totals[at]]
    return received


def per_device(n_ctx, n_fsdp, tokens, qkv_weight, out_weight, norm_gain, initial_state):
    rows, width = tokens.shape
    heads_here, head_dim = initial_state.shape[:2]
    columns = heads_here * head_dim
    n_rows = rows * n_fsdp
    right, left = neighbours(n_fsdp)
    order = slots(n_fsdp)

    half = width // 2
    held = ring_gather(tokens, n_fsdp, right, left)

    blocks = n_fsdp - 3
    early = blocks * rows
    marks = [mark(held[1][1]), mark(held[1][2])]
    feat_k, first_rows, second_rows = early_keys(held[0][:blocks], held[1][:blocks], qkv_weight, n_rows)
    values = early_values(first_rows, second_rows, qkv_weight, early)
    first, first_rows = first_pass(held[0][blocks:], first_rows, qkv_weight, early, [values, feat_k] + marks)
    count = heads_here // 2 if heads_here % 2 == 0 else heads_here
    states = []
    for start in range(0, heads_here, count):
        pieces = held[1][blocks:] if start == 0 else []
        second_rows, feat_k, values, state = late_keys_and_values(
            pieces, second_rows, qkv_weight, first, feat_k, values, start, count, head_dim, early
        )
        states.append(state)
    feat_q, within = queries_within((first_rows, second_rows), qkv_weight, feat_k, values, head_dim, n_fsdp, rows)
    exchanged = exchange_states(states, n_ctx)
    soon = 1
    normalized, parts = attend_and_project(
        feat_q, within, initial_state, exchanged, norm_gain, out_weight, soon, rows, head_dim
    )
    parts = project_rest(normalized, out_weight, n_fsdp - soon, rows) + parts
    mirrored = [distance if distance == n_fsdp // 2 else -distance for distance in order]
    return ring_scatter(parts, mirrored, left, right)


def solution(mesh):
    body = functools.partial(per_device, mesh.shape["ctx"], mesh.shape["fsdp"])
    placed = (
        P(("ctx", "fsdp"), None),
        P(None, None, "fsdp"),
        P("fsdp", None),
        P("fsdp"),
        P("fsdp", None, None),
    )
    return jax.shard_map(
        body, mesh=mesh, in_specs=placed, out_specs=P(("ctx", "fsdp"), None), check_vma=False
    )
```

```python
import functools

import jax
import jax.numpy as jnp
from jax import lax
from jax.experimental import pallas as pl
from jax.experimental.pallas import tpu as pltpu
from jax.sharding import PartitionSpec as P

VMEM = pl.BlockSpec(memory_space=pltpu.VMEM)
ANY = pl.BlockSpec(memory_space=pl.ANY)
HBM = pl.BlockSpec(memory_space=pltpu.HBM)
F32, BF16 = jnp.float32, jnp.bfloat16
HOP_FLOPS = 5 * 10**9


def ring_order(size):
    return list(range(0, size, 2)) + list(range(size - 1, 0, -2))


def neighbours(size):
    ring = ring_order(size)
    right = [(ring[i], ring[(i + 1) % size]) for i in range(size)]
    left = [(b, a) for a, b in right]
    return right, left


def slots(size):
    order = [0]
    for step in range(1, size // 2):
        order += [-step, step]
    return order + [size // 2]


def in_hbm(array):
    return pltpu.with_memory_space_constraint(array, pltpu.HBM)


def call(body, out_shape, in_specs, out_specs, flops=0, nbytes=0, limit=12 << 20, **more):
    return pl.pallas_call(
        body,
        out_shape=out_shape,
        in_specs=in_specs,
        out_specs=out_specs,
        cost_estimate=pl.CostEstimate(flops=flops, bytes_accessed=nbytes, transcendentals=0),
        compiler_params=pltpu.CompilerParams(vmem_limit_bytes=limit),
        **more,
    )


def mark(arrived):
    def body(arrived_ref, out_ref):
        out_ref[...] = jnp.zeros_like(out_ref)

    return call(
        body,
        jax.ShapeDtypeStruct((8, 128), F32),
        [ANY],
        VMEM,
        flops=HOP_FLOPS,
        limit=1 << 20,
        name="mark",
    )(arrived)


def ring_gather(block, size, right, left):
    half = block.shape[1] // 2
    going_right = [block[:, :half], block[:, half:]]
    going_left = list(going_right)
    held = [[going_right[0]], [going_right[1]]]
    for _ in range(1, size // 2):
        for part in range(2):
            going_right[part] = lax.ppermute(going_right[part], "fsdp", right)
            going_left[1 - part] = lax.ppermute(going_left[1 - part], "fsdp", left)
        for part in range(2):
            held[part] += [going_right[part], going_left[part]]
    held[0].append(lax.ppermute(going_right[0], "fsdp", right))
    held[1].append(lax.ppermute(going_left[1], "fsdp", left))
    return held


def assemble(pieces, into, first_row):
    rows = pieces[0].shape[0]
    for place, piece in enumerate(pieces):
        into[first_row + place * rows : first_row + (place + 1) * rows, :] = piece[...]


def feature_map(projected):
    return jnp.where(projected > 0.0, projected + 1.0, jnp.exp(jnp.minimum(projected, 0.0)))


def early_keys(first_pieces, second_pieces, weight, n_rows):
    _, width, columns = weight.shape
    half = width // 2
    count = len(first_pieces)
    early = count * first_pieces[0].shape[0]

    def body(*refs):
        weight_ref, feat_ref, first_ref, second_ref = refs[2 * count :]
        assemble(refs[:count], first_ref, 0)
        assemble(refs[count : 2 * count], second_ref, 0)
        projected = jnp.dot(first_ref[:early, :], weight_ref[1, :half, :], preferred_element_type=F32)
        projected += jnp.dot(second_ref[:early, :], weight_ref[1, half:, :], preferred_element_type=F32)
        feat_ref[:early, :] = feature_map(projected).astype(BF16)

    return call(
        body,
        [jax.ShapeDtypeStruct((n_rows, columns), BF16)] + [jax.ShapeDtypeStruct((n_rows, half), BF16)] * 2,
        [VMEM] * (2 * count + 1),
        [VMEM] * 3,
        flops=2 * early * width * columns,
        nbytes=2 * width * columns,
        name="early_keys",
    )(*first_pieces, *second_pieces, weight)


def early_values(first_rows, second_rows, weight, early):
    n_rows, half = first_rows.shape
    columns = weight.shape[2]

    def body(first_ref, second_ref, weight_ref, values_ref):
        projected = jnp.dot(first_ref[:early, :], weight_ref[2, :half, :], preferred_element_type=F32)
        projected += jnp.dot(second_ref[:early, :], weight_ref[2, half:, :], preferred_element_type=F32)
        values_ref[:early, :] = projected.astype(BF16)

    return call(
        body,
        jax.ShapeDtypeStruct((n_rows, columns), BF16),
        [VMEM] * 3,
        VMEM,
        flops=4 * early * half * columns,
        nbytes=4 * half * columns,
        name="early_values",
    )(first_rows, second_rows, weight)


def assemble_late(pieces, halves, early, after):
    count = len(pieces[0])

    def body(*refs):
        for part in range(2):
            assemble(refs[part * count : (part + 1) * count], refs[part - 2], early)

    return call(
        body,
        [jax.ShapeDtypeStruct(half.shape, BF16) for half in halves],
        [VMEM] * (2 * count + 2) + [ANY] * len(after),
        [VMEM] * 2,
        flops=HOP_FLOPS,
        limit=4 << 20,
        input_output_aliases={2 * count: 0, 2 * count + 1: 1},
        name="assemble_late",
    )(*pieces[0], *pieces[1], *halves, *after)


def late_keys_and_values(far, halves, weight, feat_k, values, start, count, head_dim, early, after):
    n_rows, half = halves[0].shape
    columns = count * head_dim
    n_far = len(far)
    span = slice(start * head_dim, start * head_dim + columns)

    def body(*refs):
        weight_ref = refs[n_far + 2]
        rows_refs, (feat_ref, values_ref, state_ref) = refs[-5:-3], refs[-3:]
        for piece, rows_ref in zip(refs[:n_far], rows_refs):
            rows_ref[n_rows - piece.shape[0] :, :] = piece[...]

        def product(which):
            total = jnp.dot(rows_refs[0][early:, :], weight_ref[which, :half, span], preferred_element_type=F32)
            return total + jnp.dot(rows_refs[1][early:, :], weight_ref[which, half:, span], preferred_element_type=F32)

        feat_ref[early:, span] = feature_map(product(1)).astype(BF16)
        values_ref[early:, span] = product(2).astype(BF16)
        for head in range(count):
            at = slice((start + head) * head_dim, (start + head + 1) * head_dim)
            state_ref[head] = lax.dot_general(
                feat_ref[:, at], values_ref[:, at], (((0,), (0,)), ((), ())), preferred_element_type=F32
            ).astype(BF16)

    out = call(
        body,
        [jax.ShapeDtypeStruct(array.shape, BF16) for array in (*halves, feat_k, values)]
        + [jax.ShapeDtypeStruct((count, head_dim, head_dim), BF16)],
        [VMEM] * (n_far + 5) + [ANY] * len(after),
        [VMEM] * 5,
        flops=8 * (n_rows - early) * half * columns if far else HOP_FLOPS,
        nbytes=8 * half * columns,
        input_output_aliases={n_far: 0, n_far + 1: 1, n_far + 3: 2, n_far + 4: 3},
        name="late_keys_and_values",
    )(*far, *halves, weight, feat_k, values, *after)
    return out[:2], *out[2:]


def queries_within(halves, qkv_weight, feat_k, values, head_dim, size, rows):
    n_rows, half = halves[0].shape
    columns = qkv_weight.shape[2]
    order = slots(size)

    def place(shape, axis):
        spot = lax.axis_index("fsdp")
        spot = jnp.where(spot % 2 == 0, spot // 2, size - (spot + 1) // 2)
        row = lax.broadcasted_iota(jnp.int32, shape, axis)
        slot = row // rows
        start = jnp.zeros(shape, jnp.int32)
        for at, distance in enumerate(order):
            there = (spot + distance + size) % size
            holder = jnp.where(there < size // 2, 2 * there, 2 * (size - there) - 1)
            start = jnp.where(slot == at, holder * rows, start)
        return start + row - slot * rows

    def body(first_ref, second_ref, weight_ref, k_ref, v_ref, feat_ref, within_ref):
        causal = place((n_rows, 1), 0) >= place((1, n_rows), 1)
        projected = jnp.dot(first_ref[...], weight_ref[0, :half, :], preferred_element_type=F32)
        projected += jnp.dot(second_ref[...], weight_ref[0, half:, :], preferred_element_type=F32)
        feat_ref[...] = feature_map(projected).astype(BF16)
        for head in range(0, columns, head_dim):
            span = slice(head, head + head_dim)
            scores = lax.dot_general(
                feat_ref[:, span], k_ref[:, span], (((1,), (1,)), ((), ())), preferred_element_type=F32
            )
            scores = jnp.where(causal, scores, 0.0).astype(BF16)
            within_ref[:, span] = jnp.dot(scores, v_ref[:, span], preferred_element_type=F32)

    return call(
        body,
        (jax.ShapeDtypeStruct((n_rows, columns), BF16), jax.ShapeDtypeStruct((n_rows, columns), F32)),
        [VMEM] * 5,
        (VMEM,) * 2,
        flops=4 * n_rows * half * columns + 4 * n_rows * n_rows * columns,
        nbytes=4 * half * columns,
        name="queries_within",
    )(*halves, qkv_weight, feat_k, values)


def project_out(normalized, weight_ref, parts, rows):
    half = weight_ref.shape[1] // 2
    for which in range(2):
        tile = 512 if half % 512 == 0 else 128
        for start in range(0, half, tile):
            span = slice(start, start + tile)
            product = jnp.dot(normalized, weight_ref[:, which * half + start : which * half + start + tile], preferred_element_type=F32).astype(BF16)
            for block in range(len(parts) // 2):
                parts[2 * block + which][:, span] = product[block * rows : (block + 1) * rows, :]


def attend_and_project(feat_q, within, initial, exchanged, gain, out_weight, blocks, rows, head_dim):
    per_group = initial.shape[0] // len(exchanged)
    steps = len(exchanged[0])
    others = [other for group in exchanged for other in group]
    n_rows, columns = feat_q.shape
    half = out_weight.shape[1] // 2

    def body(q_ref, within_ref, initial_ref, gain_ref, weight_ref, *refs):
        other_refs, normalized_ref, parts = refs[: len(others)], refs[len(others)], refs[len(others) + 1 :]
        place = lax.axis_index("ctx")
        for head in range(columns // head_dim):
            at = slice(head * head_dim, (head + 1) * head_dim)
            prefix = initial_ref[head]
            group, within_group = divmod(head, per_group)
            for bit, other_ref in enumerate(other_refs[group * steps : (group + 1) * steps]):
                later = (place // 2**bit) % 2 == 1
                prefix = prefix + jnp.where(later, other_ref[within_group].astype(F32), 0.0)
            high = prefix.astype(BF16)
            low = (prefix - high.astype(F32)).astype(BF16)
            q = q_ref[:, at]
            attended = within_ref[:, at] + jnp.dot(q, high, preferred_element_type=F32)
            attended = attended + jnp.dot(q, low, preferred_element_type=F32)
            scale = lax.rsqrt(jnp.mean(attended * attended, axis=-1, keepdims=True) + 1e-06)
            normalized_ref[:, at] = (attended * scale * gain_ref[:, at]).astype(BF16)
        project_out(normalized_ref[n_rows - blocks * rows :, :], weight_ref, parts, rows)

    out = call(
        body,
        [jax.ShapeDtypeStruct((n_rows, columns), BF16)] + [jax.ShapeDtypeStruct((rows, half), BF16)] * (2 * blocks),
        [VMEM] * (5 + len(others)),
        [VMEM] * (1 + 2 * blocks),
        flops=4 * n_rows * half * columns,
        nbytes=4 * half * columns,
        name="attend_and_project",
    )(feat_q, within, initial, gain.reshape(1, columns), out_weight, *others)
    return out[0], [out[1 + 2 * block : 3 + 2 * block] for block in range(blocks)]


def project_rest(normalized, out_weight, blocks, rows):
    columns = normalized.shape[1]
    half = out_weight.shape[1] // 2

    def body(normalized_ref, weight_ref, *parts):
        project_out(normalized_ref[: blocks * rows, :], weight_ref, parts, rows)

    out = call(
        body,
        [jax.ShapeDtypeStruct((rows, half), BF16)] * (2 * blocks),
        [VMEM] * 2,
        [VMEM] * (2 * blocks),
        flops=HOP_FLOPS,
        nbytes=4 * half * columns,
        name="project_rest",
    )(normalized, out_weight)
    return [out[2 * block : 2 * block + 2] for block in range(blocks)]


def add_step(mine, got):
    def body(mine_ref, got_ref, out_ref):
        out_ref[...] = (mine_ref[...].astype(F32) + got_ref[...].astype(F32)).astype(BF16)

    return call(
        body,
        jax.ShapeDtypeStruct(mine.shape, BF16),
        [VMEM] * 2,
        VMEM,
        nbytes=6 * mine.size,
        limit=4 << 20,
        name="add_step",
    )(mine, got)


def add_own(own, trailing):
    def body(first, second, got_first, got_second, out):
        out[0] = first[...].astype(F32) + got_first[...].astype(F32)
        out[1] = second[...].astype(F32) + got_second[...].astype(F32)

    return call(
        body,
        jax.ShapeDtypeStruct((2,) + own[0].shape, F32),
        [VMEM] * 4,
        VMEM,
        flops=HOP_FLOPS,
        nbytes=16 * own[0].size,
        limit=4 << 20,
        name="add_own",
    )(*own, *trailing)


def finish(gathered, leading):
    rows, half = leading[0].shape

    def body(gathered_ref, first, second, out):
        out[:, :half] = (gathered_ref[0] + first[...].astype(F32)).astype(BF16)
        out[:, half:] = (gathered_ref[1] + second[...].astype(F32)).astype(BF16)

    return call(
        body,
        jax.ShapeDtypeStruct((rows, 2 * half), BF16),
        [VMEM] * 3,
        VMEM,
        nbytes=4 * rows * half,
        limit=4 << 20,
        name="finish",
    )(gathered, *leading)


def ring_scatter(parts, order, right, left):
    far = max(order)

    def part(distance, half):
        return parts[order.index(distance)][half]

    def hop(to_right, to_left):
        return lax.ppermute(to_right, "fsdp", right), lax.ppermute(to_left, "fsdp", left)

    leading = hop(part(far, 0), part(far, 1))
    trailing = hop(part(far - 1, 1), part(1 - far, 0))
    for step in range(far - 1, 0, -1):
        leading = hop(add_step(part(step, 0), leading[0]), add_step(part(-step, 1), leading[1]))
        if step > 1:
            trailing = hop(
                add_step(part(step - 1, 1), trailing[0]), add_step(part(1 - step, 0), trailing[1])
            )
    gathered = add_own(parts[0], (trailing[1], trailing[0]))
    return finish(gathered, leading)


def add_states(one, two, after):
    def body(one_ref, two_ref, *refs):
        refs[-1][...] = (one_ref[...].astype(F32) + two_ref[...].astype(F32)).astype(BF16)

    return call(
        body,
        jax.ShapeDtypeStruct(one.shape, BF16),
        [VMEM] * 2 + [ANY] * len(after),
        VMEM,
        nbytes=6 * one.size,
        limit=4 << 20,
        name="add_states",
    )(one, two, *after)


def exchange_states(states, size):
    received = [[] for _ in states]
    totals = list(states)
    reach = 1
    while reach < size:
        pairs = [(i, i ^ reach) for i in range(size)]
        for at, total in enumerate(totals):
            received[at].append(lax.ppermute(total, "ctx", pairs))
        reach *= 2
        if reach < size:
            after = []
            for at, total in enumerate(totals):
                totals[at] = add_states(total, received[at][-1], after)
                after = [totals[at]]
    return received


def per_device(n_ctx, n_fsdp, tokens, qkv_weight, out_weight, norm_gain, initial_state):
    rows, width = tokens.shape
    heads_here, head_dim = initial_state.shape[:2]
    columns = heads_here * head_dim
    n_rows = rows * n_fsdp
    right, left = neighbours(n_fsdp)
    order = slots(n_fsdp)

    held = ring_gather(tokens, n_fsdp, right, left)

    blocks = n_fsdp - 3
    early = blocks * rows
    feat_k, *halves = early_keys(held[0][:blocks], held[1][:blocks], qkv_weight, n_rows)
    values = early_values(*halves, qkv_weight, early)
    halves = assemble_late([held[0][blocks:-1], held[1][blocks:-1]], halves, early, [values])
    marks = [mark(held[0][1]), mark(held[1][2])]
    count = heads_here // 2 if heads_here % 2 == 0 else heads_here
    states = []
    for start in range(0, heads_here, count):
        far = [held[0][-1], held[1][-1]] if start == 0 else []
        halves, feat_k, values, state = late_keys_and_values(
            far, halves, qkv_weight, feat_k, values, start, count, head_dim, early, marks if start == 0 else []
        )
        states.append(state)
    feat_q, within = queries_within(halves, qkv_weight, feat_k, values, head_dim, n_fsdp, rows)
    exchanged = exchange_states(states, n_ctx)
    soon = 1
    normalized, parts = attend_and_project(
        feat_q, within, initial_state, exchanged, norm_gain, out_weight, soon, rows, head_dim
    )
    parts = project_rest(normalized, out_weight, n_fsdp - soon, rows) + parts
    mirrored = [distance if distance == n_fsdp // 2 else -distance for distance in order]
    return ring_scatter(parts, mirrored, left, right)


def solution(mesh):
    body = functools.partial(per_device, mesh.shape["ctx"], mesh.shape["fsdp"])
    placed = (
        P(("ctx", "fsdp"), None),
        P(None, None, "fsdp"),
        P("fsdp", None),
        P("fsdp"),
        P("fsdp", None, None),
    )
    return jax.shard_map(
        body, mesh=mesh, in_specs=placed, out_specs=P(("ctx", "fsdp"), None), check_vma=False
    )
```

```python
import functools

import jax
import jax.numpy as jnp
from jax import lax
from jax.experimental import pallas as pl
from jax.experimental.pallas import tpu as pltpu
from jax.sharding import PartitionSpec as P

VMEM = pl.BlockSpec(memory_space=pltpu.VMEM)
ANY = pl.BlockSpec(memory_space=pl.ANY)
HBM = pl.BlockSpec(memory_space=pltpu.HBM)
F32, BF16 = jnp.float32, jnp.bfloat16
HOP_FLOPS = 5 * 10**9


def ring_order(size):
    return list(range(0, size, 2)) + list(range(size - 1, 0, -2))


def neighbours(size):
    ring = ring_order(size)
    right = [(ring[i], ring[(i + 1) % size]) for i in range(size)]
    left = [(b, a) for a, b in right]
    return right, left


def slots(size):
    order = [0]
    for step in range(1, size // 2):
        order += [-step, step]
    return order + [size // 2]


def in_hbm(array):
    return pltpu.with_memory_space_constraint(array, pltpu.HBM)


def call(body, out_shape, in_specs, out_specs, flops=0, nbytes=0, limit=12 << 20, **more):
    return pl.pallas_call(
        body,
        out_shape=out_shape,
        in_specs=in_specs,
        out_specs=out_specs,
        cost_estimate=pl.CostEstimate(flops=flops, bytes_accessed=nbytes, transcendentals=0),
        compiler_params=pltpu.CompilerParams(vmem_limit_bytes=limit),
        **more,
    )


def mark(arrived):
    def body(arrived_ref, out_ref):
        out_ref[...] = jnp.zeros_like(out_ref)

    return call(
        body,
        jax.ShapeDtypeStruct((8, 128), F32),
        [ANY],
        VMEM,
        flops=HOP_FLOPS,
        limit=1 << 20,
        name="mark",
    )(arrived)


def ring_gather(block, size, right, left):
    half = block.shape[1] // 2
    going_right = [block[:, :half], block[:, half:]]
    going_left = list(going_right)
    held = [[going_right[0]], [going_right[1]]]
    for _ in range(1, size // 2):
        for part in range(2):
            going_right[part] = lax.ppermute(going_right[part], "fsdp", right)
            going_left[1 - part] = lax.ppermute(going_left[1 - part], "fsdp", left)
        for part in range(2):
            held[part] += [going_right[part], going_left[part]]
    held[0].append(lax.ppermute(going_right[0], "fsdp", right))
    held[1].append(lax.ppermute(going_left[1], "fsdp", left))
    return held


def assemble(pieces, into, first_row):
    rows = pieces[0].shape[0]
    for place, piece in enumerate(pieces):
        into[first_row + place * rows : first_row + (place + 1) * rows, :] = piece[...]


def feature_map(projected):
    return jnp.where(projected > 0.0, projected + 1.0, jnp.exp(jnp.minimum(projected, 0.0)))


def early_keys(first_pieces, second_pieces, weight, n_rows):
    _, width, columns = weight.shape
    half = width // 2
    count = len(first_pieces)
    early = count * first_pieces[0].shape[0]

    def body(*refs):
        weight_ref, feat_ref, first_ref, second_ref = refs[2 * count :]
        assemble(refs[:count], first_ref, 0)
        assemble(refs[count : 2 * count], second_ref, 0)
        projected = jnp.dot(first_ref[:early, :], weight_ref[1, :half, :], preferred_element_type=F32)
        projected += jnp.dot(second_ref[:early, :], weight_ref[1, half:, :], preferred_element_type=F32)
        feat_ref[:early, :] = feature_map(projected).astype(BF16)

    return call(
        body,
        [jax.ShapeDtypeStruct((n_rows, columns), BF16)] + [jax.ShapeDtypeStruct((n_rows, half), BF16)] * 2,
        [VMEM] * (2 * count + 1),
        [VMEM] * 3,
        flops=2 * early * width * columns,
        nbytes=2 * width * columns,
        name="early_keys",
    )(*first_pieces, *second_pieces, weight)


def early_values(first_rows, second_rows, weight, early):
    n_rows, half = first_rows.shape
    columns = weight.shape[2]

    def body(first_ref, second_ref, weight_ref, values_ref):
        projected = jnp.dot(first_ref[:early, :], weight_ref[2, :half, :], preferred_element_type=F32)
        projected += jnp.dot(second_ref[:early, :], weight_ref[2, half:, :], preferred_element_type=F32)
        values_ref[:early, :] = projected.astype(BF16)

    return call(
        body,
        jax.ShapeDtypeStruct((n_rows, columns), BF16),
        [VMEM] * 3,
        VMEM,
        flops=4 * early * half * columns,
        nbytes=4 * half * columns,
        name="early_values",
    )(first_rows, second_rows, weight)


def assemble_late(pieces, halves, early, after):
    count = len(pieces[0])

    def body(*refs):
        for part in range(2):
            assemble(refs[part * count : (part + 1) * count], refs[part - 2], early)

    return call(
        body,
        [jax.ShapeDtypeStruct(half.shape, BF16) for half in halves],
        [VMEM] * (2 * count + 2) + [ANY] * len(after),
        [VMEM] * 2,
        flops=HOP_FLOPS,
        limit=4 << 20,
        input_output_aliases={2 * count: 0, 2 * count + 1: 1},
        name="assemble_late",
    )(*pieces[0], *pieces[1], *halves, *after)


def late_keys_and_values(far, halves, weight, feat_k, values, start, count, head_dim, early, after):
    n_rows, half = halves[0].shape
    columns = count * head_dim
    n_far = len(far)
    span = slice(start * head_dim, start * head_dim + columns)

    def body(*refs):
        weight_ref = refs[n_far + 2]
        rows_refs, (feat_ref, values_ref, state_ref) = refs[-5:-3], refs[-3:]
        for piece, rows_ref in zip(refs[:n_far], rows_refs):
            rows_ref[n_rows - piece.shape[0] :, :] = piece[...]

        def product(which):
            total = jnp.dot(rows_refs[0][early:, :], weight_ref[which, :half, span], preferred_element_type=F32)
            return total + jnp.dot(rows_refs[1][early:, :], weight_ref[which, half:, span], preferred_element_type=F32)

        feat_ref[early:, span] = feature_map(product(1)).astype(BF16)
        values_ref[early:, span] = product(2).astype(BF16)
        for head in range(count):
            at = slice((start + head) * head_dim, (start + head + 1) * head_dim)
            state_ref[head] = lax.dot_general(
                feat_ref[:, at], values_ref[:, at], (((0,), (0,)), ((), ())), preferred_element_type=F32
            ).astype(BF16)

    out = call(
        body,
        [jax.ShapeDtypeStruct(array.shape, BF16) for array in (*halves, feat_k, values)]
        + [jax.ShapeDtypeStruct((count, head_dim, head_dim), BF16)],
        [VMEM] * (n_far + 5) + [ANY] * len(after),
        [VMEM] * 5,
        flops=8 * (n_rows - early) * half * columns if far else HOP_FLOPS,
        nbytes=8 * half * columns,
        input_output_aliases={n_far: 0, n_far + 1: 1, n_far + 3: 2, n_far + 4: 3},
        name="late_keys_and_values",
    )(*far, *halves, weight, feat_k, values, *after)
    return out[:2], *out[2:]


def queries_within(halves, qkv_weight, feat_k, values, head_dim, size, rows):
    n_rows, half = halves[0].shape
    columns = qkv_weight.shape[2]
    order = slots(size)

    def place(shape, axis):
        spot = lax.axis_index("fsdp")
        spot = jnp.where(spot % 2 == 0, spot // 2, size - (spot + 1) // 2)
        row = lax.broadcasted_iota(jnp.int32, shape, axis)
        slot = row // rows
        start = jnp.zeros(shape, jnp.int32)
        for at, distance in enumerate(order):
            there = (spot + distance + size) % size
            holder = jnp.where(there < size // 2, 2 * there, 2 * (size - there) - 1)
            start = jnp.where(slot == at, holder * rows, start)
        return start + row - slot * rows

    def body(first_ref, second_ref, weight_ref, k_ref, v_ref, feat_ref, within_ref):
        causal = place((n_rows, 1), 0) >= place((1, n_rows), 1)
        projected = jnp.dot(first_ref[...], weight_ref[0, :half, :], preferred_element_type=F32)
        projected += jnp.dot(second_ref[...], weight_ref[0, half:, :], preferred_element_type=F32)
        feat_ref[...] = feature_map(projected).astype(BF16)
        for head in range(0, columns, head_dim):
            span = slice(head, head + head_dim)
            scores = lax.dot_general(
                feat_ref[:, span], k_ref[:, span], (((1,), (1,)), ((), ())), preferred_element_type=F32
            )
            scores = jnp.where(causal, scores, 0.0).astype(BF16)
            within_ref[:, span] = jnp.dot(scores, v_ref[:, span], preferred_element_type=F32)

    return call(
        body,
        (jax.ShapeDtypeStruct((n_rows, columns), BF16), jax.ShapeDtypeStruct((n_rows, columns), F32)),
        [VMEM] * 5,
        (VMEM,) * 2,
        flops=4 * n_rows * half * columns + 4 * n_rows * n_rows * columns,
        nbytes=4 * half * columns,
        name="queries_within",
    )(*halves, qkv_weight, feat_k, values)


def project_out(normalized, weight_ref, parts, rows):
    half = weight_ref.shape[1] // 2
    for which in range(2):
        tile = 512 if half % 512 == 0 else 128
        for start in range(0, half, tile):
            span = slice(start, start + tile)
            product = jnp.dot(normalized, weight_ref[:, which * half + start : which * half + start + tile], preferred_element_type=F32).astype(BF16)
            for block in range(len(parts) // 2):
                parts[2 * block + which][:, span] = product[block * rows : (block + 1) * rows, :]


def attend_and_project(feat_q, within, initial, exchanged, gain, out_weight, blocks, rows, head_dim):
    per_group = initial.shape[0] // len(exchanged)
    steps = len(exchanged[0])
    others = [other for group in exchanged for other in group]
    n_rows, columns = feat_q.shape
    half = out_weight.shape[1] // 2

    def body(q_ref, within_ref, initial_ref, gain_ref, weight_ref, *refs):
        other_refs, normalized_ref, parts = refs[: len(others)], refs[len(others)], refs[len(others) + 1 :]
        place = lax.axis_index("ctx")
        for head in range(columns // head_dim):
            at = slice(head * head_dim, (head + 1) * head_dim)
            prefix = initial_ref[head]
            group, within_group = divmod(head, per_group)
            for bit, other_ref in enumerate(other_refs[group * steps : (group + 1) * steps]):
                later = (place // 2**bit) % 2 == 1
                prefix = prefix + jnp.where(later, other_ref[within_group].astype(F32), 0.0)
            high = prefix.astype(BF16)
            low = (prefix - high.astype(F32)).astype(BF16)
            q = q_ref[:, at]
            attended = within_ref[:, at] + jnp.dot(q, high, preferred_element_type=F32)
            attended = attended + jnp.dot(q, low, preferred_element_type=F32)
            scale = lax.rsqrt(jnp.mean(attended * attended, axis=-1, keepdims=True) + 1e-06)
            normalized_ref[:, at] = (attended * scale * gain_ref[:, at]).astype(BF16)
        project_out(normalized_ref[n_rows - blocks * rows :, :], weight_ref, parts, rows)

    out = call(
        body,
        [jax.ShapeDtypeStruct((n_rows, columns), BF16)] + [jax.ShapeDtypeStruct((rows, half), BF16)] * (2 * blocks),
        [VMEM] * (5 + len(others)),
        [VMEM] * (1 + 2 * blocks),
        flops=4 * n_rows * half * columns,
        nbytes=4 * half * columns,
        name="attend_and_project",
    )(feat_q, within, initial, gain.reshape(1, columns), out_weight, *others)
    return out[0], [out[1 + 2 * block : 3 + 2 * block] for block in range(blocks)]


def project_rest(normalized, out_weight, blocks, rows):
    columns = normalized.shape[1]
    half = out_weight.shape[1] // 2

    def body(normalized_ref, weight_ref, *parts):
        project_out(normalized_ref[: blocks * rows, :], weight_ref, parts, rows)

    out = call(
        body,
        [jax.ShapeDtypeStruct((rows, half), BF16)] * (2 * blocks),
        [VMEM] * 2,
        [VMEM] * (2 * blocks),
        flops=HOP_FLOPS,
        nbytes=4 * half * columns,
        name="project_rest",
    )(normalized, out_weight)
    return [out[2 * block : 2 * block + 2] for block in range(blocks)]


def add_step(mine, got):
    def body(mine_ref, got_ref, out_ref):
        out_ref[...] = (mine_ref[...].astype(F32) + got_ref[...].astype(F32)).astype(BF16)

    return call(
        body,
        jax.ShapeDtypeStruct(mine.shape, BF16),
        [VMEM] * 2,
        VMEM,
        nbytes=6 * mine.size,
        limit=4 << 20,
        name="add_step",
    )(mine, got)


def add_own(own, trailing):
    def body(first, second, got_first, got_second, out):
        out[0] = first[...].astype(F32) + got_first[...].astype(F32)
        out[1] = second[...].astype(F32) + got_second[...].astype(F32)

    return call(
        body,
        jax.ShapeDtypeStruct((2,) + own[0].shape, F32),
        [VMEM] * 4,
        VMEM,
        flops=HOP_FLOPS,
        nbytes=16 * own[0].size,
        limit=4 << 20,
        name="add_own",
    )(*own, *trailing)


def finish(gathered, leading):
    rows, half = leading[0].shape

    def body(gathered_ref, first, second, out):
        out[:, :half] = (gathered_ref[0] + first[...].astype(F32)).astype(BF16)
        out[:, half:] = (gathered_ref[1] + second[...].astype(F32)).astype(BF16)

    return call(
        body,
        jax.ShapeDtypeStruct((rows, 2 * half), BF16),
        [VMEM] * 3,
        VMEM,
        nbytes=4 * rows * half,
        limit=4 << 20,
        name="finish",
    )(gathered, *leading)


def ring_scatter(parts, order, right, left):
    far = max(order)

    def part(distance, half):
        return parts[order.index(distance)][half]

    def hop(to_right, to_left):
        return lax.ppermute(to_right, "fsdp", right), lax.ppermute(to_left, "fsdp", left)

    leading = hop(part(far, 0), part(far, 1))
    trailing = hop(part(far - 1, 1), part(1 - far, 0))
    for step in range(far - 1, 0, -1):
        leading = hop(add_step(part(step, 0), leading[0]), add_step(part(-step, 1), leading[1]))
        if step > 1:
            trailing = hop(
                add_step(part(step - 1, 1), trailing[0]), add_step(part(1 - step, 0), trailing[1])
            )
    gathered = add_own(parts[0], (trailing[1], trailing[0]))
    return finish(gathered, leading)


def add_states(one, two, after):
    def body(one_ref, two_ref, *refs):
        refs[-1][...] = (one_ref[...].astype(F32) + two_ref[...].astype(F32)).astype(BF16)

    return call(
        body,
        jax.ShapeDtypeStruct(one.shape, BF16),
        [VMEM] * 2 + [ANY] * len(after),
        VMEM,
        nbytes=6 * one.size,
        limit=4 << 20,
        name="add_states",
    )(one, two, *after)


def exchange_states(states, size):
    received = [[] for _ in states]
    totals = list(states)
    reach = 1
    while reach < size:
        pairs = [(i, i ^ reach) for i in range(size)]
        for at, total in enumerate(totals):
            received[at].append(lax.ppermute(total, "ctx", pairs))
        reach *= 2
        if reach < size:
            after = []
            for at, total in enumerate(totals):
                totals[at] = add_states(total, received[at][-1], after)
                after = [totals[at]]
    return received


def per_device(n_ctx, n_fsdp, tokens, qkv_weight, out_weight, norm_gain, initial_state):
    rows, width = tokens.shape
    heads_here, head_dim = initial_state.shape[:2]
    columns = heads_here * head_dim
    n_rows = rows * n_fsdp
    right, left = neighbours(n_fsdp)
    order = slots(n_fsdp)

    held = ring_gather(tokens, n_fsdp, right, left)

    blocks = n_fsdp - 3
    early = blocks * rows
    feat_k, *halves = early_keys(held[0][:blocks], held[1][:blocks], qkv_weight, n_rows)
    values = early_values(*halves, qkv_weight, early)
    halves = assemble_late([held[0][blocks:-1], held[1][blocks:-1]], halves, early, [values])
    marks = [mark(held[0][1]), mark(held[1][2])]
    count = heads_here // 2 if heads_here % 2 == 0 else heads_here
    states = []
    for start in range(0, heads_here, count):
        far = [held[0][-1], held[1][-1]] if start == 0 else []
        halves, feat_k, values, state = late_keys_and_values(
            far, halves, qkv_weight, feat_k, values, start, count, head_dim, early, marks if start == 0 else []
        )
        states.append(state)
    feat_q, within = queries_within(halves, qkv_weight, feat_k, values, head_dim, n_fsdp, rows)
    exchanged = exchange_states(states, n_ctx)
    soon = 1
    normalized, parts = attend_and_project(
        feat_q, within, initial_state, exchanged, norm_gain, out_weight, soon, rows, head_dim
    )
    parts = project_rest(normalized, out_weight, n_fsdp - soon, rows) + parts

    return ring_scatter(parts, order, right, left)


def solution(mesh):
    body = functools.partial(per_device, mesh.shape["ctx"], mesh.shape["fsdp"])
    placed = (
        P(("ctx", "fsdp"), None),
        P(None, None, "fsdp"),
        P("fsdp", None),
        P("fsdp"),
        P("fsdp", None, None),
    )
    return jax.shard_map(
        body, mesh=mesh, in_specs=placed, out_specs=P(("ctx", "fsdp"), None), check_vma=False
    )
```

```python
import functools

import jax
import jax.numpy as jnp
from jax import lax
from jax.experimental import pallas as pl
from jax.experimental.pallas import tpu as pltpu
from jax.sharding import PartitionSpec as P

VMEM = pl.BlockSpec(memory_space=pltpu.VMEM)
ANY = pl.BlockSpec(memory_space=pl.ANY)
HBM = pl.BlockSpec(memory_space=pltpu.HBM)
F32, BF16 = jnp.float32, jnp.bfloat16
HOP_FLOPS = 5 * 10**9


def ring_order(size):
    return list(range(0, size, 2)) + list(range(size - 1, 0, -2))


def neighbours(size):
    ring = ring_order(size)
    right = [(ring[i], ring[(i + 1) % size]) for i in range(size)]
    left = [(b, a) for a, b in right]
    return right, left


def slots(size):
    order = [0]
    for step in range(1, size // 2):
        order += [-step, step]
    return order + [size // 2]


def in_hbm(array):
    return pltpu.with_memory_space_constraint(array, pltpu.HBM)


def call(body, out_shape, in_specs, out_specs, flops=0, nbytes=0, limit=12 << 20, **more):
    return pl.pallas_call(
        body,
        out_shape=out_shape,
        in_specs=in_specs,
        out_specs=out_specs,
        cost_estimate=pl.CostEstimate(flops=flops, bytes_accessed=nbytes, transcendentals=0),
        compiler_params=pltpu.CompilerParams(vmem_limit_bytes=limit),
        **more,
    )


def mark(arrived):
    def body(arrived_ref, out_ref):
        out_ref[...] = jnp.zeros_like(out_ref)

    return call(
        body,
        jax.ShapeDtypeStruct((8, 128), F32),
        [ANY],
        VMEM,
        flops=HOP_FLOPS,
        limit=1 << 20,
        name="mark",
    )(arrived)


def ring_gather(block, size, right, left):
    half = block.shape[1] // 2
    going_right = [block[:, :half], block[:, half:]]
    going_left = list(going_right)
    held = [[going_right[0]], [going_right[1]]]
    for _ in range(1, size // 2):
        for part in range(2):
            going_right[part] = lax.ppermute(going_right[part], "fsdp", right)
            going_left[1 - part] = lax.ppermute(going_left[1 - part], "fsdp", left)
        for part in range(2):
            held[part] += [going_right[part], going_left[part]]
    held[0].append(lax.ppermute(going_right[0], "fsdp", right))
    held[1].append(lax.ppermute(going_left[1], "fsdp", left))
    return held


def assemble(pieces, into, first_row):
    rows = pieces[0].shape[0]
    for place, piece in enumerate(pieces):
        into[first_row + place * rows : first_row + (place + 1) * rows, :] = piece[...]


def feature_map(projected):
    return jnp.where(projected > 0.0, projected + 1.0, jnp.exp(jnp.minimum(projected, 0.0)))


def early_keys(first_pieces, second_pieces, weight, n_rows):
    _, width, columns = weight.shape
    half = width // 2
    count = len(first_pieces)
    early = count * first_pieces[0].shape[0]

    def body(*refs):
        weight_ref, feat_ref, first_ref, second_ref = refs[2 * count :]
        assemble(refs[:count], first_ref, 0)
        assemble(refs[count : 2 * count], second_ref, 0)
        projected = jnp.dot(first_ref[:early, :], weight_ref[1, :half, :], preferred_element_type=F32)
        projected += jnp.dot(second_ref[:early, :], weight_ref[1, half:, :], preferred_element_type=F32)
        feat_ref[:early, :] = feature_map(projected).astype(BF16)

    return call(
        body,
        [jax.ShapeDtypeStruct((n_rows, columns), BF16)] + [jax.ShapeDtypeStruct((n_rows, half), BF16)] * 2,
        [VMEM] * (2 * count + 1),
        [VMEM] * 3,
        flops=2 * early * width * columns,
        nbytes=2 * width * columns,
        name="early_keys",
    )(*first_pieces, *second_pieces, weight)


def early_values(first_rows, second_rows, weight, early):
    n_rows, half = first_rows.shape
    columns = weight.shape[2]

    def body(first_ref, second_ref, weight_ref, values_ref):
        projected = jnp.dot(first_ref[:early, :], weight_ref[2, :half, :], preferred_element_type=F32)
        projected += jnp.dot(second_ref[:early, :], weight_ref[2, half:, :], preferred_element_type=F32)
        values_ref[:early, :] = projected.astype(BF16)

    return call(
        body,
        jax.ShapeDtypeStruct((n_rows, columns), BF16),
        [VMEM] * 3,
        VMEM,
        flops=4 * early * half * columns,
        nbytes=4 * half * columns,
        name="early_values",
    )(first_rows, second_rows, weight)


def assemble_late(pieces, halves, early, after):
    count = len(pieces[0])

    def body(*refs):
        for part in range(2):
            assemble(refs[part * count : (part + 1) * count], refs[part - 2], early)

    return call(
        body,
        [jax.ShapeDtypeStruct(half.shape, BF16) for half in halves],
        [VMEM] * (2 * count + 2) + [ANY] * len(after),
        [VMEM] * 2,
        flops=HOP_FLOPS,
        limit=4 << 20,
        input_output_aliases={2 * count: 0, 2 * count + 1: 1},
        name="assemble_late",
    )(*pieces[0], *pieces[1], *halves, *after)


def late_keys_and_values(far, halves, weight, feat_k, values, start, count, head_dim, early, after):
    n_rows, half = halves[0].shape
    columns = count * head_dim
    n_far = len(far)
    span = slice(start * head_dim, start * head_dim + columns)

    def body(*refs):
        weight_ref = refs[n_far + 2]
        rows_refs, (feat_ref, values_ref, state_ref) = refs[-5:-3], refs[-3:]
        for piece, rows_ref in zip(refs[:n_far], rows_refs):
            rows_ref[n_rows - piece.shape[0] :, :] = piece[...]

        def product(which):
            total = jnp.dot(rows_refs[0][early:, :], weight_ref[which, :half, span], preferred_element_type=F32)
            return total + jnp.dot(rows_refs[1][early:, :], weight_ref[which, half:, span], preferred_element_type=F32)

        feat_ref[early:, span] = feature_map(product(1)).astype(BF16)
        values_ref[early:, span] = product(2).astype(BF16)
        for head in range(count):
            at = slice((start + head) * head_dim, (start + head + 1) * head_dim)
            state_ref[head] = lax.dot_general(
                feat_ref[:, at], values_ref[:, at], (((0,), (0,)), ((), ())), preferred_element_type=F32
            ).astype(BF16)

    out = call(
        body,
        [jax.ShapeDtypeStruct(array.shape, BF16) for array in (*halves, feat_k, values)]
        + [jax.ShapeDtypeStruct((count, head_dim, head_dim), BF16)],
        [VMEM] * (n_far + 5) + [ANY] * len(after),
        [VMEM] * 5,
        flops=8 * (n_rows - early) * half * columns if far else HOP_FLOPS,
        nbytes=8 * half * columns,
        input_output_aliases={n_far: 0, n_far + 1: 1, n_far + 3: 2, n_far + 4: 3},
        name="late_keys_and_values",
    )(*far, *halves, weight, feat_k, values, *after)
    return out[:2], *out[2:]


def queries_within(halves, qkv_weight, feat_k, values, head_dim, size, rows):
    n_rows, half = halves[0].shape
    columns = qkv_weight.shape[2]
    order = slots(size)

    def place(shape, axis):
        spot = lax.axis_index("fsdp")
        spot = jnp.where(spot % 2 == 0, spot // 2, size - (spot + 1) // 2)
        row = lax.broadcasted_iota(jnp.int32, shape, axis)
        slot = row // rows
        start = jnp.zeros(shape, jnp.int32)
        for at, distance in enumerate(order):
            there = (spot + distance + size) % size
            holder = jnp.where(there < size // 2, 2 * there, 2 * (size - there) - 1)
            start = jnp.where(slot == at, holder * rows, start)
        return start + row - slot * rows

    def body(first_ref, second_ref, weight_ref, k_ref, v_ref, feat_ref, within_ref):
        causal = place((n_rows, 1), 0) >= place((1, n_rows), 1)
        projected = jnp.dot(first_ref[...], weight_ref[0, :half, :], preferred_element_type=F32)
        projected += jnp.dot(second_ref[...], weight_ref[0, half:, :], preferred_element_type=F32)
        feat_ref[...] = feature_map(projected).astype(BF16)
        for head in range(0, columns, head_dim):
            span = slice(head, head + head_dim)
            scores = lax.dot_general(
                feat_ref[:, span], k_ref[:, span], (((1,), (1,)), ((), ())), preferred_element_type=F32
            )
            scores = jnp.where(causal, scores, 0.0).astype(BF16)
            within_ref[:, span] = jnp.dot(scores, v_ref[:, span], preferred_element_type=F32)

    return call(
        body,
        (jax.ShapeDtypeStruct((n_rows, columns), BF16), jax.ShapeDtypeStruct((n_rows, columns), F32)),
        [VMEM] * 5,
        (VMEM,) * 2,
        flops=4 * n_rows * half * columns + 4 * n_rows * n_rows * columns,
        nbytes=4 * half * columns,
        name="queries_within",
    )(*halves, qkv_weight, feat_k, values)


def project_out(normalized, weight_ref, parts, rows):
    half = weight_ref.shape[1] // 2
    for which in range(2):
        tile = 512 if half % 512 == 0 else 128
        for start in range(0, half, tile):
            span = slice(start, start + tile)
            product = jnp.dot(normalized, weight_ref[:, which * half + start : which * half + start + tile], preferred_element_type=F32).astype(BF16)
            for block in range(len(parts) // 2):
                parts[2 * block + which][:, span] = product[block * rows : (block + 1) * rows, :]


def attend_and_project(rows, feat_q, within, initial, exchanged, gain, out_weight, block, head_dim, flops, name):
    columns = feat_q.shape[1]
    half = out_weight.shape[1] // 2
    per_group = initial.shape[0] // len(exchanged)
    steps = len(exchanged[0])
    others = [other for group in exchanged for other in group]
    count = rows.stop - rows.start
    n_parts = 2 * (count // block)

    def body(q_ref, within_ref, initial_ref, gain_ref, weight_ref, *refs):
        other_refs, parts, normalized_ref = refs[: len(others)], refs[len(others) : -1], refs[-1]
        place = lax.axis_index("ctx")
        for head in range(columns // head_dim):
            at = slice(head * head_dim, (head + 1) * head_dim)
            prefix = initial_ref[head]
            group, within_group = divmod(head, per_group)
            for bit, other_ref in enumerate(other_refs[group * steps : (group + 1) * steps]):
                later = (place // 2**bit) % 2 == 1
                prefix = prefix + jnp.where(later, other_ref[within_group].astype(F32), 0.0)
            high = prefix.astype(BF16)
            low = (prefix - high.astype(F32)).astype(BF16)
            q = q_ref[rows, at]
            attended = within_ref[rows, at] + jnp.dot(q, high, preferred_element_type=F32)
            attended = attended + jnp.dot(q, low, preferred_element_type=F32)
            scale = lax.rsqrt(jnp.mean(attended * attended, axis=-1, keepdims=True) + 1e-06)
            normalized_ref[:, at] = (attended * scale * gain_ref[:, at]).astype(BF16)
        project_out(normalized_ref[...], weight_ref, parts, block)

    out = call(
        body,
        [jax.ShapeDtypeStruct((block, half), BF16)] * n_parts,
        [VMEM] * (5 + len(others)),
        [VMEM] * n_parts,
        flops=flops,
        nbytes=4 * half * columns,
        scratch_shapes=[pltpu.VMEM((count, columns), BF16)],
        name=name,
    )(feat_q, within, initial, gain.reshape(1, columns), out_weight, *others)
    return [out[2 * at : 2 * at + 2] for at in range(count // block)]


def add_step(mine, got):
    def body(mine_ref, got_ref, out_ref):
        out_ref[...] = (mine_ref[...].astype(F32) + got_ref[...].astype(F32)).astype(BF16)

    return call(
        body,
        jax.ShapeDtypeStruct(mine.shape, BF16),
        [VMEM] * 2,
        VMEM,
        nbytes=6 * mine.size,
        limit=4 << 20,
        name="add_step",
    )(mine, got)


def add_own(own, trailing):
    def body(first, second, got_first, got_second, out):
        out[0] = first[...].astype(F32) + got_first[...].astype(F32)
        out[1] = second[...].astype(F32) + got_second[...].astype(F32)

    return call(
        body,
        jax.ShapeDtypeStruct((2,) + own[0].shape, F32),
        [VMEM] * 4,
        VMEM,
        flops=HOP_FLOPS,
        nbytes=16 * own[0].size,
        limit=4 << 20,
        name="add_own",
    )(*own, *trailing)


def finish(gathered, leading):
    rows, half = leading[0].shape

    def body(gathered_ref, first, second, out):
        out[:, :half] = (gathered_ref[0] + first[...].astype(F32)).astype(BF16)
        out[:, half:] = (gathered_ref[1] + second[...].astype(F32)).astype(BF16)

    return call(
        body,
        jax.ShapeDtypeStruct((rows, 2 * half), BF16),
        [VMEM] * 3,
        VMEM,
        nbytes=4 * rows * half,
        limit=4 << 20,
        name="finish",
    )(gathered, *leading)


def ring_scatter(parts, order, right, left):
    far = max(order)

    def part(distance, half):
        return parts[order.index(distance)][half]

    def hop(to_right, to_left):
        return lax.ppermute(to_right, "fsdp", right), lax.ppermute(to_left, "fsdp", left)

    leading = hop(part(far, 0), part(far, 1))
    trailing = hop(part(far - 1, 1), part(1 - far, 0))
    for step in range(far - 1, 0, -1):
        leading = hop(add_step(part(step, 0), leading[0]), add_step(part(-step, 1), leading[1]))
        if step > 1:
            trailing = hop(
                add_step(part(step - 1, 1), trailing[0]), add_step(part(1 - step, 0), trailing[1])
            )
    gathered = add_own(parts[0], (trailing[1], trailing[0]))
    return finish(gathered, leading)


def add_states(one, two, after):
    def body(one_ref, two_ref, *refs):
        refs[-1][...] = (one_ref[...].astype(F32) + two_ref[...].astype(F32)).astype(BF16)

    return call(
        body,
        jax.ShapeDtypeStruct(one.shape, BF16),
        [VMEM] * 2 + [ANY] * len(after),
        VMEM,
        nbytes=6 * one.size,
        limit=4 << 20,
        name="add_states",
    )(one, two, *after)


def exchange_states(states, size):
    received = [[] for _ in states]
    totals = list(states)
    reach = 1
    while reach < size:
        pairs = [(i, i ^ reach) for i in range(size)]
        for at, total in enumerate(totals):
            received[at].append(lax.ppermute(total, "ctx", pairs))
        reach *= 2
        if reach < size:
            after = []
            for at, total in enumerate(totals):
                totals[at] = add_states(total, received[at][-1], after)
                after = [totals[at]]
    return received


def per_device(n_ctx, n_fsdp, tokens, qkv_weight, out_weight, norm_gain, initial_state):
    rows, width = tokens.shape
    heads_here, head_dim = initial_state.shape[:2]
    columns = heads_here * head_dim
    n_rows = rows * n_fsdp
    right, left = neighbours(n_fsdp)
    order = slots(n_fsdp)

    held = ring_gather(tokens, n_fsdp, right, left)

    blocks = n_fsdp - 3
    early = blocks * rows
    feat_k, *halves = early_keys(held[0][:blocks], held[1][:blocks], qkv_weight, n_rows)
    values = early_values(*halves, qkv_weight, early)
    halves = assemble_late([held[0][blocks:-1], held[1][blocks:-1]], halves, early, [values])
    marks = [mark(held[0][1]), mark(held[1][2])]
    count = heads_here // 2 if heads_here % 2 == 0 else heads_here
    states = []
    for start in range(0, heads_here, count):
        far = [held[0][-1], held[1][-1]] if start == 0 else []
        halves, feat_k, values, state = late_keys_and_values(
            far, halves, qkv_weight, feat_k, values, start, count, head_dim, early, marks if start == 0 else []
        )
        states.append(state)
    feat_q, within = queries_within(halves, qkv_weight, feat_k, values, head_dim, n_fsdp, rows)
    exchanged = exchange_states(states, n_ctx)
    last = n_rows - rows
    common = (feat_q, within, initial_state, exchanged, norm_gain, out_weight, rows, head_dim)
    farthest = attend_and_project(slice(last, n_rows), *common, 2 * rows * columns * width, "attend_farthest")
    parts = attend_and_project(slice(0, last), *common, HOP_FLOPS, "attend_rest") + farthest
    return ring_scatter(parts, order, right, left)


def solution(mesh):
    body = functools.partial(per_device, mesh.shape["ctx"], mesh.shape["fsdp"])
    placed = (
        P(("ctx", "fsdp"), None),
        P(None, None, "fsdp"),
        P("fsdp", None),
        P("fsdp"),
        P("fsdp", None, None),
    )
    return jax.shard_map(
        body, mesh=mesh, in_specs=placed, out_specs=P(("ctx", "fsdp"), None), check_vma=False
    )
```

```python
import functools

import jax
import jax.numpy as jnp
from jax import lax
from jax.experimental import pallas as pl
from jax.experimental.pallas import tpu as pltpu
from jax.sharding import PartitionSpec as P

VMEM = pl.BlockSpec(memory_space=pltpu.VMEM)
ANY = pl.BlockSpec(memory_space=pl.ANY)
HBM = pl.BlockSpec(memory_space=pltpu.HBM)
F32, BF16 = jnp.float32, jnp.bfloat16
HOP_FLOPS = 5 * 10**9


def ring_order(size):
    return list(range(0, size, 2)) + list(range(size - 1, 0, -2))


def neighbours(size):
    ring = ring_order(size)
    right = [(ring[i], ring[(i + 1) % size]) for i in range(size)]
    left = [(b, a) for a, b in right]
    return right, left


def slots(size):
    order = [0]
    for step in range(1, size // 2):
        order += [-step, step]
    return order + [size // 2]


def in_hbm(array):
    return pltpu.with_memory_space_constraint(array, pltpu.HBM)


def call(body, out_shape, in_specs, out_specs, flops=0, nbytes=0, limit=12 << 20, **more):
    return pl.pallas_call(
        body,
        out_shape=out_shape,
        in_specs=in_specs,
        out_specs=out_specs,
        cost_estimate=pl.CostEstimate(flops=flops, bytes_accessed=nbytes, transcendentals=0),
        compiler_params=pltpu.CompilerParams(vmem_limit_bytes=limit),
        **more,
    )


def mark(arrived):
    def body(arrived_ref, out_ref):
        out_ref[...] = jnp.zeros_like(out_ref)

    return call(
        body,
        jax.ShapeDtypeStruct((8, 128), F32),
        [ANY],
        VMEM,
        flops=HOP_FLOPS,
        limit=1 << 20,
        name="mark",
    )(arrived)


def ring_gather(block, size, right, left):
    half = block.shape[1] // 2
    going_right = [block[:, :half], block[:, half:]]
    going_left = list(going_right)
    held = [[going_right[0]], [going_right[1]]]
    for _ in range(1, size // 2):
        for part in range(2):
            going_right[part] = lax.ppermute(going_right[part], "fsdp", right)
            going_left[1 - part] = lax.ppermute(going_left[1 - part], "fsdp", left)
        for part in range(2):
            held[part] += [going_right[part], going_left[part]]
    held[0].append(lax.ppermute(going_right[0], "fsdp", right))
    held[1].append(lax.ppermute(going_left[1], "fsdp", left))
    return held


def assemble(pieces, into, first_row):
    rows = pieces[0].shape[0]
    for place, piece in enumerate(pieces):
        into[first_row + place * rows : first_row + (place + 1) * rows, :] = piece[...]


def feature_map(projected):
    return jnp.where(projected > 0.0, projected + 1.0, jnp.exp(jnp.minimum(projected, 0.0)))


def early_keys(first_pieces, second_pieces, weight, n_rows):
    _, width, columns = weight.shape
    half = width // 2
    count = len(first_pieces)
    early = count * first_pieces[0].shape[0]

    def body(*refs):
        weight_ref, feat_ref, first_ref, second_ref = refs[2 * count :]
        assemble(refs[:count], first_ref, 0)
        assemble(refs[count : 2 * count], second_ref, 0)
        projected = jnp.dot(first_ref[:early, :], weight_ref[1, :half, :], preferred_element_type=F32)
        projected += jnp.dot(second_ref[:early, :], weight_ref[1, half:, :], preferred_element_type=F32)
        feat_ref[:early, :] = feature_map(projected).astype(BF16)

    return call(
        body,
        [jax.ShapeDtypeStruct((n_rows, columns), BF16)] + [jax.ShapeDtypeStruct((n_rows, half), BF16)] * 2,
        [VMEM] * (2 * count + 1),
        [VMEM] * 3,
        flops=2 * early * width * columns,
        nbytes=2 * width * columns,
        name="early_keys",
    )(*first_pieces, *second_pieces, weight)


def early_values(first_rows, second_rows, weight, early):
    n_rows, half = first_rows.shape
    columns = weight.shape[2]

    def body(first_ref, second_ref, weight_ref, values_ref):
        projected = jnp.dot(first_ref[:early, :], weight_ref[2, :half, :], preferred_element_type=F32)
        projected += jnp.dot(second_ref[:early, :], weight_ref[2, half:, :], preferred_element_type=F32)
        values_ref[:early, :] = projected.astype(BF16)

    return call(
        body,
        jax.ShapeDtypeStruct((n_rows, columns), BF16),
        [VMEM] * 3,
        VMEM,
        flops=4 * early * half * columns,
        nbytes=4 * half * columns,
        name="early_values",
    )(first_rows, second_rows, weight)


def assemble_late(pieces, halves, early, after):
    count = len(pieces[0])

    def body(*refs):
        for part in range(2):
            assemble(refs[part * count : (part + 1) * count], refs[part - 2], early)

    return call(
        body,
        [jax.ShapeDtypeStruct(half.shape, BF16) for half in halves],
        [VMEM] * (2 * count + 2) + [ANY] * len(after),
        [VMEM] * 2,
        flops=HOP_FLOPS,
        limit=4 << 20,
        input_output_aliases={2 * count: 0, 2 * count + 1: 1},
        name="assemble_late",
    )(*pieces[0], *pieces[1], *halves, *after)


def first_pass(far, rows, weight, early, after):
    n_rows, half = rows.shape
    columns = weight.shape[2]

    def body(*refs):
        far_ref, weight_ref, rows_ref, out_ref = refs[0], refs[2], refs[-2], refs[-1]
        rows_ref[n_rows - far_ref.shape[0] :, :] = far_ref[...]
        for place in range(2):
            out_ref[place] = jnp.dot(rows_ref[early:, :], weight_ref[1 + place, :half, :], preferred_element_type=F32)

    return call(
        body,
        [
            jax.ShapeDtypeStruct(rows.shape, BF16),
            jax.ShapeDtypeStruct((2, n_rows - early, columns), F32),
        ],
        [VMEM] * 3 + [ANY] * len(after),
        [VMEM] * 2,
        flops=4 * (n_rows - early) * half * columns,
        nbytes=4 * half * columns,
        input_output_aliases={1: 0},
        name="first_pass",
    )(far, rows, weight, *after)


def late_keys_and_values(far, rows, weight, first, feat_k, values, start, count, head_dim, early):
    n_rows, half = rows.shape
    columns = count * head_dim
    n_far = len(far)
    span = slice(start * head_dim, start * head_dim + columns)

    def body(*refs):
        weight_ref, first_ref = refs[n_far + 1 : n_far + 3]
        rows_ref, feat_ref, values_ref, state_ref = refs[-4:]
        for far_ref in refs[:n_far]:
            rows_ref[n_rows - far_ref.shape[0] :, :] = far_ref[...]

        def product(which):
            return first_ref[which - 1, :, span] + jnp.dot(
                rows_ref[early:, :], weight_ref[which, half:, span], preferred_element_type=F32
            )

        feat_ref[early:, span] = feature_map(product(1)).astype(BF16)
        values_ref[early:, span] = product(2).astype(BF16)
        for head in range(count):
            at = slice((start + head) * head_dim, (start + head + 1) * head_dim)
            state_ref[head] = lax.dot_general(
                feat_ref[:, at], values_ref[:, at], (((0,), (0,)), ((), ())), preferred_element_type=F32
            ).astype(BF16)

    return call(
        body,
        [jax.ShapeDtypeStruct(array.shape, BF16) for array in (rows, feat_k, values)]
        + [jax.ShapeDtypeStruct((count, head_dim, head_dim), BF16)],
        [VMEM] * (n_far + 5),
        [VMEM] * 4,
        flops=4 * (n_rows - early) * half * columns if far else HOP_FLOPS,
        nbytes=4 * half * columns,
        input_output_aliases={n_far: 0, n_far + 3: 1, n_far + 4: 2},
        name="late_keys_and_values",
    )(*far, rows, weight, first, feat_k, values)


def queries_within(halves, qkv_weight, feat_k, values, head_dim, size, rows):
    n_rows, half = halves[0].shape
    columns = qkv_weight.shape[2]
    order = slots(size)

    def place(shape, axis):
        spot = lax.axis_index("fsdp")
        spot = jnp.where(spot % 2 == 0, spot // 2, size - (spot + 1) // 2)
        row = lax.broadcasted_iota(jnp.int32, shape, axis)
        slot = row // rows
        start = jnp.zeros(shape, jnp.int32)
        for at, distance in enumerate(order):
            there = (spot + distance + size) % size
            holder = jnp.where(there < size // 2, 2 * there, 2 * (size - there) - 1)
            start = jnp.where(slot == at, holder * rows, start)
        return start + row - slot * rows

    def body(first_ref, second_ref, weight_ref, k_ref, v_ref, feat_ref, within_ref):
        causal = place((n_rows, 1), 0) >= place((1, n_rows), 1)
        projected = jnp.dot(first_ref[...], weight_ref[0, :half, :], preferred_element_type=F32)
        projected += jnp.dot(second_ref[...], weight_ref[0, half:, :], preferred_element_type=F32)
        feat_ref[...] = feature_map(projected).astype(BF16)
        for head in range(0, columns, head_dim):
            span = slice(head, head + head_dim)
            scores = lax.dot_general(
                feat_ref[:, span], k_ref[:, span], (((1,), (1,)), ((), ())), preferred_element_type=F32
            )
            scores = jnp.where(causal, scores, 0.0).astype(BF16)
            within_ref[:, span] = jnp.dot(scores, v_ref[:, span], preferred_element_type=F32)

    return call(
        body,
        (jax.ShapeDtypeStruct((n_rows, columns), BF16), jax.ShapeDtypeStruct((n_rows, columns), F32)),
        [VMEM] * 5,
        (VMEM,) * 2,
        flops=4 * n_rows * half * columns + 4 * n_rows * n_rows * columns,
        nbytes=4 * half * columns,
        name="queries_within",
    )(*halves, qkv_weight, feat_k, values)


def project_out(normalized, weight_ref, parts, rows):
    half = weight_ref.shape[1] // 2
    for which in range(2):
        tile = 512 if half % 512 == 0 else 128
        for start in range(0, half, tile):
            span = slice(start, start + tile)
            product = jnp.dot(normalized, weight_ref[:, which * half + start : which * half + start + tile], preferred_element_type=F32).astype(BF16)
            for block in range(len(parts) // 2):
                parts[2 * block + which][:, span] = product[block * rows : (block + 1) * rows, :]


def attend_and_project(feat_q, within, initial, exchanged, gain, out_weight, blocks, rows, head_dim):
    per_group = initial.shape[0] // len(exchanged)
    steps = len(exchanged[0])
    others = [other for group in exchanged for other in group]
    n_rows, columns = feat_q.shape
    half = out_weight.shape[1] // 2

    def body(q_ref, within_ref, initial_ref, gain_ref, weight_ref, *refs):
        other_refs, normalized_ref, parts = refs[: len(others)], refs[len(others)], refs[len(others) + 1 :]
        place = lax.axis_index("ctx")
        for head in range(columns // head_dim):
            at = slice(head * head_dim, (head + 1) * head_dim)
            prefix = initial_ref[head]
            group, within_group = divmod(head, per_group)
            for bit, other_ref in enumerate(other_refs[group * steps : (group + 1) * steps]):
                later = (place // 2**bit) % 2 == 1
                prefix = prefix + jnp.where(later, other_ref[within_group].astype(F32), 0.0)
            high = prefix.astype(BF16)
            low = (prefix - high.astype(F32)).astype(BF16)
            q = q_ref[:, at]
            attended = within_ref[:, at] + jnp.dot(q, high, preferred_element_type=F32)
            attended = attended + jnp.dot(q, low, preferred_element_type=F32)
            scale = lax.rsqrt(jnp.mean(attended * attended, axis=-1, keepdims=True) + 1e-06)
            normalized_ref[:, at] = (attended * scale * gain_ref[:, at]).astype(BF16)
        project_out(normalized_ref[n_rows - blocks * rows :, :], weight_ref, parts, rows)

    out = call(
        body,
        [jax.ShapeDtypeStruct((n_rows, columns), BF16)] + [jax.ShapeDtypeStruct((rows, half), BF16)] * (2 * blocks),
        [VMEM] * (5 + len(others)),
        [VMEM] * (1 + 2 * blocks),
        flops=4 * n_rows * half * columns,
        nbytes=4 * half * columns,
        name="attend_and_project",
    )(feat_q, within, initial, gain.reshape(1, columns), out_weight, *others)
    return out[0], [out[1 + 2 * block : 3 + 2 * block] for block in range(blocks)]


def project_rest(normalized, out_weight, blocks, rows):
    columns = normalized.shape[1]
    half = out_weight.shape[1] // 2

    def body(normalized_ref, weight_ref, *parts):
        project_out(normalized_ref[: blocks * rows, :], weight_ref, parts, rows)

    out = call(
        body,
        [jax.ShapeDtypeStruct((rows, half), BF16)] * (2 * blocks),
        [VMEM] * 2,
        [VMEM] * (2 * blocks),
        flops=HOP_FLOPS,
        nbytes=4 * half * columns,
        name="project_rest",
    )(normalized, out_weight)
    return [out[2 * block : 2 * block + 2] for block in range(blocks)]


def add_step(mine, got):
    def body(mine_ref, got_ref, out_ref):
        out_ref[...] = (mine_ref[...].astype(F32) + got_ref[...].astype(F32)).astype(BF16)

    return call(
        body,
        jax.ShapeDtypeStruct(mine.shape, BF16),
        [VMEM] * 2,
        VMEM,
        nbytes=6 * mine.size,
        limit=4 << 20,
        name="add_step",
    )(mine, got)


def add_own(own, trailing):
    def body(first, second, got_first, got_second, out):
        out[0] = first[...].astype(F32) + got_first[...].astype(F32)
        out[1] = second[...].astype(F32) + got_second[...].astype(F32)

    return call(
        body,
        jax.ShapeDtypeStruct((2,) + own[0].shape, F32),
        [VMEM] * 4,
        VMEM,
        flops=HOP_FLOPS,
        nbytes=16 * own[0].size,
        limit=4 << 20,
        name="add_own",
    )(*own, *trailing)


def finish(gathered, leading):
    rows, half = leading[0].shape

    def body(gathered_ref, first, second, out):
        out[:, :half] = (gathered_ref[0] + first[...].astype(F32)).astype(BF16)
        out[:, half:] = (gathered_ref[1] + second[...].astype(F32)).astype(BF16)

    return call(
        body,
        jax.ShapeDtypeStruct((rows, 2 * half), BF16),
        [VMEM] * 3,
        VMEM,
        nbytes=4 * rows * half,
        limit=4 << 20,
        name="finish",
    )(gathered, *leading)


def ring_scatter(parts, order, right, left):
    far = max(order)

    def part(distance, half):
        return parts[order.index(distance)][half]

    def hop(to_right, to_left):
        return lax.ppermute(to_right, "fsdp", right), lax.ppermute(to_left, "fsdp", left)

    leading = hop(part(far, 0), part(far, 1))
    trailing = hop(part(far - 1, 1), part(1 - far, 0))
    for step in range(far - 1, 0, -1):
        leading = hop(add_step(part(step, 0), leading[0]), add_step(part(-step, 1), leading[1]))
        if step > 1:
            trailing = hop(
                add_step(part(step - 1, 1), trailing[0]), add_step(part(1 - step, 0), trailing[1])
            )
    gathered = add_own(parts[0], (trailing[1], trailing[0]))
    return finish(gathered, leading)


def add_states(one, two, after):
    def body(one_ref, two_ref, *refs):
        refs[-1][...] = (one_ref[...].astype(F32) + two_ref[...].astype(F32)).astype(BF16)

    return call(
        body,
        jax.ShapeDtypeStruct(one.shape, BF16),
        [VMEM] * 2 + [ANY] * len(after),
        VMEM,
        nbytes=6 * one.size,
        limit=4 << 20,
        name="add_states",
    )(one, two, *after)


def exchange_states(states, size):
    received = [[] for _ in states]
    totals = list(states)
    reach = 1
    while reach < size:
        pairs = [(i, i ^ reach) for i in range(size)]
        for at, total in enumerate(totals):
            received[at].append(lax.ppermute(total, "ctx", pairs))
        reach *= 2
        if reach < size:
            after = []
            for at, total in enumerate(totals):
                totals[at] = add_states(total, received[at][-1], after)
                after = [totals[at]]
    return received


def per_device(n_ctx, n_fsdp, tokens, qkv_weight, out_weight, norm_gain, initial_state):
    rows, width = tokens.shape
    heads_here, head_dim = initial_state.shape[:2]
    columns = heads_here * head_dim
    n_rows = rows * n_fsdp
    right, left = neighbours(n_fsdp)
    order = slots(n_fsdp)

    held = ring_gather(tokens, n_fsdp, right, left)

    blocks = n_fsdp - 3
    early = blocks * rows
    feat_k, *halves = early_keys(held[0][:blocks], held[1][:blocks], qkv_weight, n_rows)
    values = early_values(*halves, qkv_weight, early)
    first_rows, second_rows = assemble_late([held[0][blocks:-1], held[1][blocks:-1]], halves, early, [values])
    marks = [mark(held[0][1]), mark(held[1][2])]
    first_rows, first = first_pass(held[0][-1], first_rows, qkv_weight, early, marks + [feat_k])
    count = heads_here // 2 if heads_here % 2 == 0 else heads_here
    states = []
    for start in range(0, heads_here, count):
        far = [held[1][-1]] if start == 0 else []
        second_rows, feat_k, values, state = late_keys_and_values(
            far, second_rows, qkv_weight, first, feat_k, values, start, count, head_dim, early
        )
        states.append(state)
    halves = (first_rows, second_rows)
    feat_q, within = queries_within(halves, qkv_weight, feat_k, values, head_dim, n_fsdp, rows)
    exchanged = exchange_states(states, n_ctx)
    soon = 1
    normalized, parts = attend_and_project(
        feat_q, within, initial_state, exchanged, norm_gain, out_weight, soon, rows, head_dim
    )
    parts = project_rest(normalized, out_weight, n_fsdp - soon, rows) + parts

    return ring_scatter(parts, order, right, left)


def solution(mesh):
    body = functools.partial(per_device, mesh.shape["ctx"], mesh.shape["fsdp"])
    placed = (
        P(("ctx", "fsdp"), None),
        P(None, None, "fsdp"),
        P("fsdp", None),
        P("fsdp"),
        P("fsdp", None, None),
    )
    return jax.shard_map(
        body, mesh=mesh, in_specs=placed, out_specs=P(("ctx", "fsdp"), None), check_vma=False
    )
```

```python
import functools

import jax
import jax.numpy as jnp
from jax import lax
from jax.experimental import pallas as pl
from jax.experimental.pallas import tpu as pltpu
from jax.sharding import PartitionSpec as P

VMEM = pl.BlockSpec(memory_space=pltpu.VMEM)
ANY = pl.BlockSpec(memory_space=pl.ANY)
HBM = pl.BlockSpec(memory_space=pltpu.HBM)
F32, BF16 = jnp.float32, jnp.bfloat16
HOP_FLOPS = 5 * 10**9


def ring_order(size):
    return list(range(0, size, 2)) + list(range(size - 1, 0, -2))


def neighbours(size):
    ring = ring_order(size)
    right = [(ring[i], ring[(i + 1) % size]) for i in range(size)]
    left = [(b, a) for a, b in right]
    return right, left


def slots(size):
    order = [0]
    for step in range(1, size // 2):
        order += [-step, step]
    return order + [size // 2]


def in_hbm(array):
    return pltpu.with_memory_space_constraint(array, pltpu.HBM)


def call(body, out_shape, in_specs, out_specs, flops=0, nbytes=0, limit=12 << 20, **more):
    return pl.pallas_call(
        body,
        out_shape=out_shape,
        in_specs=in_specs,
        out_specs=out_specs,
        cost_estimate=pl.CostEstimate(flops=flops, bytes_accessed=nbytes, transcendentals=0),
        compiler_params=pltpu.CompilerParams(vmem_limit_bytes=limit),
        **more,
    )


def mark(arrived):
    def body(arrived_ref, out_ref):
        out_ref[...] = jnp.zeros_like(out_ref)

    return call(
        body,
        jax.ShapeDtypeStruct((8, 128), F32),
        [ANY],
        VMEM,
        flops=HOP_FLOPS,
        limit=1 << 20,
        name="mark",
    )(arrived)


def ring_gather(block, size, right, left):
    half = block.shape[1] // 2
    going_right = [block[:, :half], block[:, half:]]
    going_left = list(going_right)
    held = [[going_right[0]], [going_right[1]]]
    for _ in range(1, size // 2):
        for part in range(2):
            going_right[part] = lax.ppermute(going_right[part], "fsdp", right)
            going_left[1 - part] = lax.ppermute(going_left[1 - part], "fsdp", left)
        for part in range(2):
            held[part] += [going_right[part], going_left[part]]
    held[0].append(lax.ppermute(going_right[0], "fsdp", right))
    held[1].append(lax.ppermute(going_left[1], "fsdp", left))
    return held


def assemble(pieces, into, first_row):
    rows = pieces[0].shape[0]
    for place, piece in enumerate(pieces):
        into[first_row + place * rows : first_row + (place + 1) * rows, :] = piece[...]


def feature_map(projected):
    return jnp.where(projected > 0.0, projected + 1.0, jnp.exp(jnp.minimum(projected, 0.0)))


def early_keys(first_pieces, second_pieces, weight, n_rows):
    _, width, columns = weight.shape
    half = width // 2
    count = len(first_pieces)
    early = count * first_pieces[0].shape[0]

    def body(*refs):
        weight_ref, feat_ref, first_ref, second_ref = refs[2 * count :]
        assemble(refs[:count], first_ref, 0)
        assemble(refs[count : 2 * count], second_ref, 0)
        projected = jnp.dot(first_ref[:early, :], weight_ref[1, :half, :], preferred_element_type=F32)
        projected += jnp.dot(second_ref[:early, :], weight_ref[1, half:, :], preferred_element_type=F32)
        feat_ref[:early, :] = feature_map(projected).astype(BF16)

    return call(
        body,
        [jax.ShapeDtypeStruct((n_rows, columns), BF16)] + [jax.ShapeDtypeStruct((n_rows, half), BF16)] * 2,
        [VMEM] * (2 * count + 1),
        [VMEM] * 3,
        flops=2 * early * width * columns,
        nbytes=2 * width * columns,
        name="early_keys",
    )(*first_pieces, *second_pieces, weight)


def early_values(first_rows, second_rows, weight, early):
    n_rows, half = first_rows.shape
    columns = weight.shape[2]

    def body(first_ref, second_ref, weight_ref, values_ref):
        projected = jnp.dot(first_ref[:early, :], weight_ref[2, :half, :], preferred_element_type=F32)
        projected += jnp.dot(second_ref[:early, :], weight_ref[2, half:, :], preferred_element_type=F32)
        values_ref[:early, :] = projected.astype(BF16)

    return call(
        body,
        jax.ShapeDtypeStruct((n_rows, columns), BF16),
        [VMEM] * 3,
        VMEM,
        flops=4 * early * half * columns,
        nbytes=4 * half * columns,
        name="early_values",
    )(first_rows, second_rows, weight)


def assemble_late(pieces, halves, early, after):
    count = len(pieces[0])

    def body(*refs):
        for part in range(2):
            assemble(refs[part * count : (part + 1) * count], refs[part - 2], early)

    return call(
        body,
        [jax.ShapeDtypeStruct(half.shape, BF16) for half in halves],
        [VMEM] * (2 * count + 2) + [ANY] * len(after),
        [VMEM] * 2,
        flops=HOP_FLOPS,
        limit=4 << 20,
        input_output_aliases={2 * count: 0, 2 * count + 1: 1},
        name="assemble_late",
    )(*pieces[0], *pieces[1], *halves, *after)


def first_pass(far, rows, weight, early, after):
    n_rows, half = rows.shape
    columns = weight.shape[2]

    def body(*refs):
        far_ref, weight_ref, rows_ref, out_ref = refs[0], refs[2], refs[-2], refs[-1]
        rows_ref[n_rows - far_ref.shape[0] :, :] = far_ref[...]
        for place in range(2):
            out_ref[place] = jnp.dot(rows_ref[early:, :], weight_ref[1 + place, :half, :], preferred_element_type=F32)

    return call(
        body,
        [
            jax.ShapeDtypeStruct(rows.shape, BF16),
            jax.ShapeDtypeStruct((2, n_rows - early, columns), F32),
        ],
        [VMEM] * 3 + [ANY] * len(after),
        [VMEM] * 2,
        flops=4 * (n_rows - early) * half * columns,
        nbytes=4 * half * columns,
        input_output_aliases={1: 0},
        name="first_pass",
    )(far, rows, weight, *after)


def late_keys_and_values(far, rows, weight, first, feat_k, values, start, count, head_dim, early):
    n_rows, half = rows.shape
    columns = count * head_dim
    n_far = len(far)
    span = slice(start * head_dim, start * head_dim + columns)

    def body(*refs):
        weight_ref, first_ref = refs[n_far + 1 : n_far + 3]
        rows_ref, feat_ref, values_ref, state_ref = refs[-4:]
        for far_ref in refs[:n_far]:
            rows_ref[n_rows - far_ref.shape[0] :, :] = far_ref[...]

        def product(which):
            return first_ref[which - 1, :, span] + jnp.dot(
                rows_ref[early:, :], weight_ref[which, half:, span], preferred_element_type=F32
            )

        feat_ref[early:, span] = feature_map(product(1)).astype(BF16)
        values_ref[early:, span] = product(2).astype(BF16)
        for head in range(count):
            at = slice((start + head) * head_dim, (start + head + 1) * head_dim)
            state_ref[head] = lax.dot_general(
                feat_ref[:, at], values_ref[:, at], (((0,), (0,)), ((), ())), preferred_element_type=F32
            ).astype(BF16)

    return call(
        body,
        [jax.ShapeDtypeStruct(array.shape, BF16) for array in (rows, feat_k, values)]
        + [jax.ShapeDtypeStruct((count, head_dim, head_dim), BF16)],
        [VMEM] * (n_far + 5),
        [VMEM] * 4,
        flops=4 * (n_rows - early) * half * columns if far else HOP_FLOPS,
        nbytes=4 * half * columns,
        input_output_aliases={n_far: 0, n_far + 3: 1, n_far + 4: 2},
        name="late_keys_and_values",
    )(*far, rows, weight, first, feat_k, values)


def queries_within(halves, qkv_weight, feat_k, values, head_dim, size, rows):
    n_rows, half = halves[0].shape
    columns = qkv_weight.shape[2]
    order = slots(size)

    def place(shape, axis):
        spot = lax.axis_index("fsdp")
        spot = jnp.where(spot % 2 == 0, spot // 2, size - (spot + 1) // 2)
        row = lax.broadcasted_iota(jnp.int32, shape, axis)
        slot = row // rows
        start = jnp.zeros(shape, jnp.int32)
        for at, distance in enumerate(order):
            there = (spot + distance + size) % size
            holder = jnp.where(there < size // 2, 2 * there, 2 * (size - there) - 1)
            start = jnp.where(slot == at, holder * rows, start)
        return start + row - slot * rows

    def body(first_ref, second_ref, weight_ref, k_ref, v_ref, feat_ref, within_ref):
        causal = place((n_rows, 1), 0) >= place((1, n_rows), 1)
        projected = jnp.dot(first_ref[...], weight_ref[0, :half, :], preferred_element_type=F32)
        projected += jnp.dot(second_ref[...], weight_ref[0, half:, :], preferred_element_type=F32)
        feat_ref[...] = feature_map(projected).astype(BF16)
        for head in range(0, columns, head_dim):
            span = slice(head, head + head_dim)
            scores = lax.dot_general(
                feat_ref[:, span], k_ref[:, span], (((1,), (1,)), ((), ())), preferred_element_type=F32
            )
            scores = jnp.where(causal, scores, 0.0).astype(BF16)
            within_ref[:, span] = jnp.dot(scores, v_ref[:, span], preferred_element_type=F32)

    return call(
        body,
        (jax.ShapeDtypeStruct((n_rows, columns), BF16), jax.ShapeDtypeStruct((n_rows, columns), F32)),
        [VMEM] * 5,
        (VMEM,) * 2,
        flops=4 * n_rows * half * columns + 4 * n_rows * n_rows * columns,
        nbytes=4 * half * columns,
        name="queries_within",
    )(*halves, qkv_weight, feat_k, values)


def project_out(normalized, weight_ref, parts, rows):
    half = weight_ref.shape[1] // 2
    for which in range(2):
        tile = 512 if half % 512 == 0 else 128
        for start in range(0, half, tile):
            span = slice(start, start + tile)
            product = jnp.dot(normalized, weight_ref[:, which * half + start : which * half + start + tile], preferred_element_type=F32).astype(BF16)
            for block in range(len(parts) // 2):
                parts[2 * block + which][:, span] = product[block * rows : (block + 1) * rows, :]


def attend_and_project(feat_q, within, initial, exchanged, gain, out_weight, blocks, rows, head_dim):
    per_group = initial.shape[0] // len(exchanged)
    steps = len(exchanged[0])
    others = [other for group in exchanged for other in group]
    n_rows, columns = feat_q.shape
    half = out_weight.shape[1] // 2

    def body(q_ref, within_ref, initial_ref, gain_ref, weight_ref, *refs):
        other_refs, normalized_ref, parts = refs[: len(others)], refs[len(others)], refs[len(others) + 1 :]
        place = lax.axis_index("ctx")
        for head in range(columns // head_dim):
            at = slice(head * head_dim, (head + 1) * head_dim)
            prefix = initial_ref[head]
            group, within_group = divmod(head, per_group)
            for bit, other_ref in enumerate(other_refs[group * steps : (group + 1) * steps]):
                later = (place // 2**bit) % 2 == 1
                prefix = prefix + jnp.where(later, other_ref[within_group].astype(F32), 0.0)
            high = prefix.astype(BF16)
            low = (prefix - high.astype(F32)).astype(BF16)
            q = q_ref[:, at]
            attended = within_ref[:, at] + jnp.dot(q, high, preferred_element_type=F32)
            attended = attended + jnp.dot(q, low, preferred_element_type=F32)
            scale = lax.rsqrt(jnp.mean(attended * attended, axis=-1, keepdims=True) + 1e-06)
            normalized_ref[:, at] = (attended * scale * gain_ref[:, at]).astype(BF16)
        project_out(normalized_ref[n_rows - blocks * rows :, :], weight_ref, parts, rows)

    out = call(
        body,
        [jax.ShapeDtypeStruct((n_rows, columns), BF16)] + [jax.ShapeDtypeStruct((rows, half), BF16)] * (2 * blocks),
        [VMEM] * (5 + len(others)),
        [VMEM] * (1 + 2 * blocks),
        flops=4 * n_rows * half * columns,
        nbytes=4 * half * columns,
        name="attend_and_project",
    )(feat_q, within, initial, gain.reshape(1, columns), out_weight, *others)
    return out[0], [out[1 + 2 * block : 3 + 2 * block] for block in range(blocks)]


def project_rest(normalized, out_weight, blocks, rows):
    columns = normalized.shape[1]
    half = out_weight.shape[1] // 2

    def body(normalized_ref, weight_ref, *parts):
        project_out(normalized_ref[: blocks * rows, :], weight_ref, parts, rows)

    out = call(
        body,
        [jax.ShapeDtypeStruct((rows, half), BF16)] * (2 * blocks),
        [VMEM] * 2,
        [VMEM] * (2 * blocks),
        flops=HOP_FLOPS,
        nbytes=4 * half * columns,
        name="project_rest",
    )(normalized, out_weight)
    return [out[2 * block : 2 * block + 2] for block in range(blocks)]


def add_step(mine, got):
    def body(mine_ref, got_ref, out_ref):
        out_ref[...] = (mine_ref[...].astype(F32) + got_ref[...].astype(F32)).astype(BF16)

    return call(
        body,
        jax.ShapeDtypeStruct(mine.shape, BF16),
        [VMEM] * 2,
        VMEM,
        nbytes=6 * mine.size,
        limit=4 << 20,
        name="add_step",
    )(mine, got)


def add_own(own, trailing):
    def body(first, second, got_first, got_second, out):
        out[0] = first[...].astype(F32) + got_first[...].astype(F32)
        out[1] = second[...].astype(F32) + got_second[...].astype(F32)

    return call(
        body,
        jax.ShapeDtypeStruct((2,) + own[0].shape, F32),
        [VMEM] * 4,
        VMEM,
        flops=HOP_FLOPS,
        nbytes=16 * own[0].size,
        limit=4 << 20,
        name="add_own",
    )(*own, *trailing)


def finish(gathered, leading):
    rows, half = leading[0].shape

    def body(gathered_ref, first, second, out):
        out[:, :half] = (gathered_ref[0] + first[...].astype(F32)).astype(BF16)
        out[:, half:] = (gathered_ref[1] + second[...].astype(F32)).astype(BF16)

    return call(
        body,
        jax.ShapeDtypeStruct((rows, 2 * half), BF16),
        [VMEM] * 3,
        VMEM,
        nbytes=4 * rows * half,
        limit=4 << 20,
        name="finish",
    )(gathered, *leading)


def ring_scatter(parts, order, right, left):
    far = max(order)

    def part(distance, half):
        return parts[order.index(distance)][half]

    def hop(to_right, to_left):
        return lax.ppermute(to_right, "fsdp", right), lax.ppermute(to_left, "fsdp", left)

    leading = hop(part(far, 0), part(far, 1))
    trailing = hop(part(far - 1, 1), part(1 - far, 0))
    for step in range(far - 1, 0, -1):
        leading = hop(add_step(part(step, 0), leading[0]), add_step(part(-step, 1), leading[1]))
        if step > 1:
            trailing = hop(
                add_step(part(step - 1, 1), trailing[0]), add_step(part(1 - step, 0), trailing[1])
            )
    gathered = add_own(parts[0], (trailing[1], trailing[0]))
    return finish(gathered, leading)


def add_states(one, two, after):
    def body(one_ref, two_ref, *refs):
        refs[-1][...] = (one_ref[...].astype(F32) + two_ref[...].astype(F32)).astype(BF16)

    return call(
        body,
        jax.ShapeDtypeStruct(one.shape, BF16),
        [VMEM] * 2 + [ANY] * len(after),
        VMEM,
        nbytes=6 * one.size,
        limit=4 << 20,
        name="add_states",
    )(one, two, *after)


def exchange_states(states, size):
    received = [[] for _ in states]
    totals = list(states)
    reach = 1
    while reach < size:
        pairs = [(i, i ^ reach) for i in range(size)]
        for at, total in enumerate(totals):
            received[at].append(lax.ppermute(total, "ctx", pairs))
        reach *= 2
        if reach < size:
            after = []
            for at, total in enumerate(totals):
                totals[at] = add_states(total, received[at][-1], after)
                after = [totals[at]]
    return received


def per_device(n_ctx, n_fsdp, tokens, qkv_weight, out_weight, norm_gain, initial_state):
    rows, width = tokens.shape
    heads_here, head_dim = initial_state.shape[:2]
    columns = heads_here * head_dim
    n_rows = rows * n_fsdp
    right, left = neighbours(n_fsdp)
    order = slots(n_fsdp)

    held = ring_gather(tokens, n_fsdp, right, left)

    blocks = n_fsdp - 3
    early = blocks * rows
    feat_k, *halves = early_keys(held[0][:blocks], held[1][:blocks], qkv_weight, n_rows)
    values = early_values(*halves, qkv_weight, early)
    first_rows, second_rows = assemble_late([held[0][blocks:-1], held[1][blocks:-1]], halves, early, [values])
    marks = [mark(held[0][1]), mark(held[1][2])]
    first_rows, first = first_pass(held[0][-1], first_rows, qkv_weight, early, marks + [feat_k])
    count = heads_here // 2 if heads_here % 2 == 0 else heads_here
    states = []
    for start in range(0, heads_here, count):
        far = [held[1][-1]] if start == 0 else []
        second_rows, feat_k, values, state = late_keys_and_values(
            far, second_rows, qkv_weight, first, feat_k, values, start, count, head_dim, early
        )
        states.append(state)
    halves = (first_rows, second_rows)
    feat_q, within = queries_within(halves, qkv_weight, feat_k, values, head_dim, n_fsdp, rows)
    exchanged = exchange_states(states, n_ctx)
    soon = 1
    normalized, parts = attend_and_project(
        feat_q, within, initial_state, exchanged, norm_gain, out_weight, soon, rows, head_dim
    )
    parts = project_rest(normalized, out_weight, n_fsdp - soon, rows) + parts

    mirrored = [distance if distance == n_fsdp // 2 else -distance for distance in order]
    return ring_scatter(parts, mirrored, left, right)


def solution(mesh):
    body = functools.partial(per_device, mesh.shape["ctx"], mesh.shape["fsdp"])
    placed = (
        P(("ctx", "fsdp"), None),
        P(None, None, "fsdp"),
        P("fsdp", None),
        P("fsdp"),
        P("fsdp", None, None),
    )
    return jax.shard_map(
        body, mesh=mesh, in_specs=placed, out_specs=P(("ctx", "fsdp"), None), check_vma=False
    )
```

```python
import functools

import jax
import jax.numpy as jnp
from jax import lax
from jax.experimental import pallas as pl
from jax.experimental.pallas import tpu as pltpu
from jax.sharding import PartitionSpec as P

VMEM = pl.BlockSpec(memory_space=pltpu.VMEM)
ANY = pl.BlockSpec(memory_space=pl.ANY)
HBM = pl.BlockSpec(memory_space=pltpu.HBM)
F32, BF16 = jnp.float32, jnp.bfloat16
HOP_FLOPS = 5 * 10**9


def ring_order(size):
    return list(range(0, size, 2)) + list(range(size - 1, 0, -2))


def neighbours(size):
    ring = ring_order(size)
    right = [(ring[i], ring[(i + 1) % size]) for i in range(size)]
    left = [(b, a) for a, b in right]
    return right, left


def slots(size):
    order = [0]
    for step in range(1, size // 2):
        order += [-step, step]
    return order + [size // 2]


def in_hbm(array):
    return pltpu.with_memory_space_constraint(array, pltpu.HBM)


def call(body, out_shape, in_specs, out_specs, flops=0, nbytes=0, limit=12 << 20, **more):
    return pl.pallas_call(
        body,
        out_shape=out_shape,
        in_specs=in_specs,
        out_specs=out_specs,
        cost_estimate=pl.CostEstimate(flops=flops, bytes_accessed=nbytes, transcendentals=0),
        compiler_params=pltpu.CompilerParams(vmem_limit_bytes=limit),
        **more,
    )


def mark(arrived):
    def body(arrived_ref, out_ref):
        out_ref[...] = jnp.zeros_like(out_ref)

    return call(
        body,
        jax.ShapeDtypeStruct((8, 128), F32),
        [ANY],
        VMEM,
        flops=HOP_FLOPS,
        limit=1 << 20,
        name="mark",
    )(arrived)


def ring_gather(block, size, right, left):
    half = block.shape[1] // 2
    going_right = [block[:, :half], block[:, half:]]
    going_left = list(going_right)
    held = [[going_right[0]], [going_right[1]]]
    for _ in range(1, size // 2):
        for part in range(2):
            going_right[part] = lax.ppermute(going_right[part], "fsdp", right)
            going_left[1 - part] = lax.ppermute(going_left[1 - part], "fsdp", left)
        for part in range(2):
            held[part] += [going_right[part], going_left[part]]
    held[0].append(lax.ppermute(going_right[0], "fsdp", right))
    held[1].append(lax.ppermute(going_left[1], "fsdp", left))
    return held


def assemble(pieces, into, first_row):
    rows = pieces[0].shape[0]
    for place, piece in enumerate(pieces):
        into[first_row + place * rows : first_row + (place + 1) * rows, :] = piece[...]


def feature_map(projected):
    return jnp.where(projected > 0.0, projected + 1.0, jnp.exp(jnp.minimum(projected, 0.0)))


def early_keys(first_pieces, second_pieces, weight, n_rows, after):
    _, width, columns = weight.shape
    half = width // 2
    count = len(first_pieces)
    early = count * first_pieces[0].shape[0]

    def body(*refs):
        weight_ref, (feat_ref, first_ref, second_ref) = refs[2 * count], refs[-3:]
        assemble(refs[:count], first_ref, 0)
        assemble(refs[count : 2 * count], second_ref, 0)
        projected = jnp.dot(first_ref[:early, :], weight_ref[1, :half, :], preferred_element_type=F32)
        projected += jnp.dot(second_ref[:early, :], weight_ref[1, half:, :], preferred_element_type=F32)
        feat_ref[:early, :] = feature_map(projected).astype(BF16)

    return call(
        body,
        [jax.ShapeDtypeStruct((n_rows, columns), BF16)] + [jax.ShapeDtypeStruct((n_rows, half), BF16)] * 2,
        [VMEM] * (2 * count + 1) + [ANY] * len(after),
        [VMEM] * 3,
        flops=2 * early * width * columns,
        nbytes=2 * width * columns,
        name="early_keys",
    )(*first_pieces, *second_pieces, weight, *after)


def early_values(first_rows, second_rows, weight, early):
    n_rows, half = first_rows.shape
    columns = weight.shape[2]

    def body(first_ref, second_ref, weight_ref, values_ref):
        projected = jnp.dot(first_ref[:early, :], weight_ref[2, :half, :], preferred_element_type=F32)
        projected += jnp.dot(second_ref[:early, :], weight_ref[2, half:, :], preferred_element_type=F32)
        values_ref[:early, :] = projected.astype(BF16)

    return call(
        body,
        jax.ShapeDtypeStruct((n_rows, columns), BF16),
        [VMEM] * 3,
        VMEM,
        flops=4 * early * half * columns,
        nbytes=4 * half * columns,
        name="early_values",
    )(first_rows, second_rows, weight)


def assemble_late(pieces, halves, early, after):
    count = len(pieces[0])

    def body(*refs):
        for part in range(2):
            assemble(refs[part * count : (part + 1) * count], refs[part - 2], early)

    return call(
        body,
        [jax.ShapeDtypeStruct(half.shape, BF16) for half in halves],
        [VMEM] * (2 * count + 2) + [ANY] * len(after),
        [VMEM] * 2,
        flops=HOP_FLOPS,
        limit=4 << 20,
        input_output_aliases={2 * count: 0, 2 * count + 1: 1},
        name="assemble_late",
    )(*pieces[0], *pieces[1], *halves, *after)


def first_pass(far, rows, weight, early, after):
    n_rows, half = rows.shape
    columns = weight.shape[2]

    def body(*refs):
        far_ref, weight_ref, rows_ref, out_ref = refs[0], refs[2], refs[-2], refs[-1]
        rows_ref[n_rows - far_ref.shape[0] :, :] = far_ref[...]
        for place in range(2):
            out_ref[place] = jnp.dot(rows_ref[early:, :], weight_ref[1 + place, :half, :], preferred_element_type=F32)

    return call(
        body,
        [
            jax.ShapeDtypeStruct(rows.shape, BF16),
            jax.ShapeDtypeStruct((2, n_rows - early, columns), F32),
        ],
        [VMEM] * 3 + [ANY] * len(after),
        [VMEM] * 2,
        flops=4 * (n_rows - early) * half * columns,
        nbytes=4 * half * columns,
        input_output_aliases={1: 0},
        name="first_pass",
    )(far, rows, weight, *after)


def late_keys_and_values(far, rows, weight, first, feat_k, values, start, count, head_dim, early):
    n_rows, half = rows.shape
    columns = count * head_dim
    n_far = len(far)
    span = slice(start * head_dim, start * head_dim + columns)

    def body(*refs):
        weight_ref, first_ref = refs[n_far + 1 : n_far + 3]
        rows_ref, feat_ref, values_ref, state_ref = refs[-4:]
        for far_ref in refs[:n_far]:
            rows_ref[n_rows - far_ref.shape[0] :, :] = far_ref[...]

        def product(which):
            return first_ref[which - 1, :, span] + jnp.dot(
                rows_ref[early:, :], weight_ref[which, half:, span], preferred_element_type=F32
            )

        feat_ref[early:, span] = feature_map(product(1)).astype(BF16)
        values_ref[early:, span] = product(2).astype(BF16)
        for head in range(count):
            at = slice((start + head) * head_dim, (start + head + 1) * head_dim)
            state_ref[head] = lax.dot_general(
                feat_ref[:, at], values_ref[:, at], (((0,), (0,)), ((), ())), preferred_element_type=F32
            ).astype(BF16)

    return call(
        body,
        [jax.ShapeDtypeStruct(array.shape, BF16) for array in (rows, feat_k, values)]
        + [jax.ShapeDtypeStruct((count, head_dim, head_dim), BF16)],
        [VMEM] * (n_far + 5),
        [VMEM] * 4,
        flops=4 * (n_rows - early) * half * columns if far else HOP_FLOPS,
        nbytes=4 * half * columns,
        input_output_aliases={n_far: 0, n_far + 3: 1, n_far + 4: 2},
        name="late_keys_and_values",
    )(*far, rows, weight, first, feat_k, values)


def queries_within(halves, qkv_weight, feat_k, values, head_dim, size, rows):
    n_rows, half = halves[0].shape
    columns = qkv_weight.shape[2]
    order = slots(size)

    def place(shape, axis):
        spot = lax.axis_index("fsdp")
        spot = jnp.where(spot % 2 == 0, spot // 2, size - (spot + 1) // 2)
        row = lax.broadcasted_iota(jnp.int32, shape, axis)
        slot = row // rows
        start = jnp.zeros(shape, jnp.int32)
        for at, distance in enumerate(order):
            there = (spot + distance + size) % size
            holder = jnp.where(there < size // 2, 2 * there, 2 * (size - there) - 1)
            start = jnp.where(slot == at, holder * rows, start)
        return start + row - slot * rows

    def body(first_ref, second_ref, weight_ref, k_ref, v_ref, feat_ref, within_ref):
        causal = place((n_rows, 1), 0) >= place((1, n_rows), 1)
        projected = jnp.dot(first_ref[...], weight_ref[0, :half, :], preferred_element_type=F32)
        projected += jnp.dot(second_ref[...], weight_ref[0, half:, :], preferred_element_type=F32)
        feat_ref[...] = feature_map(projected).astype(BF16)
        for head in range(0, columns, head_dim):
            span = slice(head, head + head_dim)
            scores = lax.dot_general(
                feat_ref[:, span], k_ref[:, span], (((1,), (1,)), ((), ())), preferred_element_type=F32
            )
            scores = jnp.where(causal, scores, 0.0).astype(BF16)
            within_ref[:, span] = jnp.dot(scores, v_ref[:, span], preferred_element_type=F32)

    return call(
        body,
        (jax.ShapeDtypeStruct((n_rows, columns), BF16), jax.ShapeDtypeStruct((n_rows, columns), F32)),
        [VMEM] * 5,
        (VMEM,) * 2,
        flops=4 * n_rows * half * columns + 4 * n_rows * n_rows * columns,
        nbytes=4 * half * columns,
        name="queries_within",
    )(*halves, qkv_weight, feat_k, values)


def project_out(normalized, weight_ref, parts, rows):
    half = weight_ref.shape[1] // 2
    for which in range(2):
        tile = 512 if half % 512 == 0 else 128
        for start in range(0, half, tile):
            span = slice(start, start + tile)
            product = jnp.dot(normalized, weight_ref[:, which * half + start : which * half + start + tile], preferred_element_type=F32).astype(BF16)
            for block in range(len(parts) // 2):
                parts[2 * block + which][:, span] = product[block * rows : (block + 1) * rows, :]


def attend_and_project(feat_q, within, initial, exchanged, gain, out_weight, blocks, rows, head_dim):
    per_group = initial.shape[0] // len(exchanged)
    steps = len(exchanged[0])
    others = [other for group in exchanged for other in group]
    n_rows, columns = feat_q.shape
    half = out_weight.shape[1] // 2

    def body(q_ref, within_ref, initial_ref, gain_ref, weight_ref, *refs):
        other_refs, normalized_ref, parts = refs[: len(others)], refs[len(others)], refs[len(others) + 1 :]
        place = lax.axis_index("ctx")
        for head in range(columns // head_dim):
            at = slice(head * head_dim, (head + 1) * head_dim)
            prefix = initial_ref[head]
            group, within_group = divmod(head, per_group)
            for bit, other_ref in enumerate(other_refs[group * steps : (group + 1) * steps]):
                later = (place // 2**bit) % 2 == 1
                prefix = prefix + jnp.where(later, other_ref[within_group].astype(F32), 0.0)
            high = prefix.astype(BF16)
            low = (prefix - high.astype(F32)).astype(BF16)
            q = q_ref[:, at]
            attended = within_ref[:, at] + jnp.dot(q, high, preferred_element_type=F32)
            attended = attended + jnp.dot(q, low, preferred_element_type=F32)
            scale = lax.rsqrt(jnp.mean(attended * attended, axis=-1, keepdims=True) + 1e-06)
            normalized_ref[:, at] = (attended * scale * gain_ref[:, at]).astype(BF16)
        project_out(normalized_ref[n_rows - blocks * rows :, :], weight_ref, parts, rows)

    out = call(
        body,
        [jax.ShapeDtypeStruct((n_rows, columns), BF16)] + [jax.ShapeDtypeStruct((rows, half), BF16)] * (2 * blocks),
        [VMEM] * (5 + len(others)),
        [VMEM] * (1 + 2 * blocks),
        flops=4 * n_rows * half * columns,
        nbytes=4 * half * columns,
        name="attend_and_project",
    )(feat_q, within, initial, gain.reshape(1, columns), out_weight, *others)
    return out[0], [out[1 + 2 * block : 3 + 2 * block] for block in range(blocks)]


def project_rest(normalized, out_weight, blocks, rows):
    columns = normalized.shape[1]
    half = out_weight.shape[1] // 2

    def body(normalized_ref, weight_ref, *parts):
        project_out(normalized_ref[: blocks * rows, :], weight_ref, parts, rows)

    out = call(
        body,
        [jax.ShapeDtypeStruct((rows, half), BF16)] * (2 * blocks),
        [VMEM] * 2,
        [VMEM] * (2 * blocks),
        flops=HOP_FLOPS,
        nbytes=4 * half * columns,
        name="project_rest",
    )(normalized, out_weight)
    return [out[2 * block : 2 * block + 2] for block in range(blocks)]


def add_step(mine, got):
    def body(mine_ref, got_ref, out_ref):
        out_ref[...] = (mine_ref[...].astype(F32) + got_ref[...].astype(F32)).astype(BF16)

    return call(
        body,
        jax.ShapeDtypeStruct(mine.shape, BF16),
        [VMEM] * 2,
        VMEM,
        nbytes=6 * mine.size,
        limit=4 << 20,
        name="add_step",
    )(mine, got)


def add_own(own, trailing):
    def body(first, second, got_first, got_second, out):
        out[0] = first[...].astype(F32) + got_first[...].astype(F32)
        out[1] = second[...].astype(F32) + got_second[...].astype(F32)

    return call(
        body,
        jax.ShapeDtypeStruct((2,) + own[0].shape, F32),
        [VMEM] * 4,
        VMEM,
        flops=HOP_FLOPS,
        nbytes=16 * own[0].size,
        limit=4 << 20,
        name="add_own",
    )(*own, *trailing)


def finish(gathered, leading):
    rows, half = leading[0].shape

    def body(gathered_ref, first, second, out):
        out[:, :half] = (gathered_ref[0] + first[...].astype(F32)).astype(BF16)
        out[:, half:] = (gathered_ref[1] + second[...].astype(F32)).astype(BF16)

    return call(
        body,
        jax.ShapeDtypeStruct((rows, 2 * half), BF16),
        [VMEM] * 3,
        VMEM,
        nbytes=4 * rows * half,
        limit=4 << 20,
        name="finish",
    )(gathered, *leading)


def ring_scatter(parts, order, right, left):
    far = max(order)

    def part(distance, half):
        return parts[order.index(distance)][half]

    def hop(to_right, to_left):
        return lax.ppermute(to_right, "fsdp", right), lax.ppermute(to_left, "fsdp", left)

    leading = hop(part(far, 0), part(far, 1))
    trailing = hop(part(far - 1, 1), part(1 - far, 0))
    for step in range(far - 1, 0, -1):
        leading = hop(add_step(part(step, 0), leading[0]), add_step(part(-step, 1), leading[1]))
        if step > 1:
            trailing = hop(
                add_step(part(step - 1, 1), trailing[0]), add_step(part(1 - step, 0), trailing[1])
            )
    gathered = add_own(parts[0], (trailing[1], trailing[0]))
    return finish(gathered, leading)


def add_states(one, two, after):
    def body(one_ref, two_ref, *refs):
        refs[-1][...] = (one_ref[...].astype(F32) + two_ref[...].astype(F32)).astype(BF16)

    return call(
        body,
        jax.ShapeDtypeStruct(one.shape, BF16),
        [VMEM] * 2 + [ANY] * len(after),
        VMEM,
        nbytes=6 * one.size,
        limit=4 << 20,
        name="add_states",
    )(one, two, *after)


def exchange_states(states, size):
    received = [[] for _ in states]
    totals = list(states)
    reach = 1
    while reach < size:
        pairs = [(i, i ^ reach) for i in range(size)]
        for at, total in enumerate(totals):
            received[at].append(lax.ppermute(total, "ctx", pairs))
        reach *= 2
        if reach < size:
            after = []
            for at, total in enumerate(totals):
                totals[at] = add_states(total, received[at][-1], after)
                after = [totals[at]]
    return received


def per_device(n_ctx, n_fsdp, tokens, qkv_weight, out_weight, norm_gain, initial_state):
    rows, width = tokens.shape
    heads_here, head_dim = initial_state.shape[:2]
    columns = heads_here * head_dim
    n_rows = rows * n_fsdp
    right, left = neighbours(n_fsdp)
    order = slots(n_fsdp)

    held = ring_gather(tokens, n_fsdp, right, left)

    blocks = n_fsdp - 3
    early = blocks * rows
    feat_k, *halves = early_keys(held[0][:blocks], held[1][:blocks], qkv_weight, n_rows, [held[1][-2]])
    values = early_values(*halves, qkv_weight, early)
    first_rows, second_rows = assemble_late([held[0][blocks:-1], held[1][blocks:-1]], halves, early, [values])
    marks = [mark(held[0][1]), mark(held[1][2])]
    first_rows, first = first_pass(held[0][-1], first_rows, qkv_weight, early, marks + [feat_k])
    count = heads_here // 2 if heads_here % 2 == 0 else heads_here
    states = []
    for start in range(0, heads_here, count):
        far = [held[1][-1]] if start == 0 else []
        second_rows, feat_k, values, state = late_keys_and_values(
            far, second_rows, qkv_weight, first, feat_k, values, start, count, head_dim, early
        )
        states.append(state)
    halves = (first_rows, second_rows)
    feat_q, within = queries_within(halves, qkv_weight, feat_k, values, head_dim, n_fsdp, rows)
    exchanged = exchange_states(states, n_ctx)
    soon = 1
    normalized, parts = attend_and_project(
        feat_q, within, initial_state, exchanged, norm_gain, out_weight, soon, rows, head_dim
    )
    parts = project_rest(normalized, out_weight, n_fsdp - soon, rows) + parts

    mirrored = [distance if distance == n_fsdp // 2 else -distance for distance in order]
    return ring_scatter(parts, mirrored, left, right)


def solution(mesh):
    body = functools.partial(per_device, mesh.shape["ctx"], mesh.shape["fsdp"])
    placed = (
        P(("ctx", "fsdp"), None),
        P(None, None, "fsdp"),
        P("fsdp", None),
        P("fsdp"),
        P("fsdp", None, None),
    )
    return jax.shard_map(
        body, mesh=mesh, in_specs=placed, out_specs=P(("ctx", "fsdp"), None), check_vma=False
    )
```

```python
import functools

import jax
import jax.numpy as jnp
from jax import lax
from jax.experimental import pallas as pl
from jax.experimental.pallas import tpu as pltpu
from jax.sharding import PartitionSpec as P

VMEM = pl.BlockSpec(memory_space=pltpu.VMEM)
ANY = pl.BlockSpec(memory_space=pl.ANY)
HBM = pl.BlockSpec(memory_space=pltpu.HBM)
F32, BF16 = jnp.float32, jnp.bfloat16
HOP_FLOPS = 5 * 10**9


def ring_order(size):
    return list(range(0, size, 2)) + list(range(size - 1, 0, -2))


def neighbours(size):
    ring = ring_order(size)
    right = [(ring[i], ring[(i + 1) % size]) for i in range(size)]
    left = [(b, a) for a, b in right]
    return right, left


def slots(size):
    order = [0]
    for step in range(1, size // 2):
        order += [-step, step]
    return order + [size // 2]


def in_hbm(array):
    return pltpu.with_memory_space_constraint(array, pltpu.HBM)


def call(body, out_shape, in_specs, out_specs, flops=0, nbytes=0, limit=12 << 20, **more):
    return pl.pallas_call(
        body,
        out_shape=out_shape,
        in_specs=in_specs,
        out_specs=out_specs,
        cost_estimate=pl.CostEstimate(flops=flops, bytes_accessed=nbytes, transcendentals=0),
        compiler_params=pltpu.CompilerParams(vmem_limit_bytes=limit),
        **more,
    )


def mark(arrived):
    def body(arrived_ref, out_ref):
        out_ref[...] = jnp.zeros_like(out_ref)

    return call(
        body,
        jax.ShapeDtypeStruct((8, 128), F32),
        [ANY],
        VMEM,
        flops=HOP_FLOPS,
        limit=1 << 20,
        name="mark",
    )(arrived)


def ring_gather(block, size, right, left):
    half = block.shape[1] // 2
    going_right = [block[:, :half], block[:, half:]]
    going_left = list(going_right)
    held = [[going_right[0]], [going_right[1]]]
    for _ in range(1, size // 2):
        for part in range(2):
            going_right[part] = lax.ppermute(going_right[part], "fsdp", right)
            going_left[1 - part] = lax.ppermute(going_left[1 - part], "fsdp", left)
        for part in range(2):
            held[part] += [going_right[part], going_left[part]]
    held[0].append(lax.ppermute(going_right[0], "fsdp", right))
    held[1].append(lax.ppermute(going_left[1], "fsdp", left))
    return held


def assemble(pieces, into, first_row):
    rows = pieces[0].shape[0]
    for place, piece in enumerate(pieces):
        into[first_row + place * rows : first_row + (place + 1) * rows, :] = piece[...]


def feature_map(projected):
    return jnp.where(projected > 0.0, projected + 1.0, jnp.exp(jnp.minimum(projected, 0.0)))


def early_keys(first_pieces, second_pieces, weight, n_rows, after):
    _, width, columns = weight.shape
    half = width // 2
    count = len(first_pieces)
    early = count * first_pieces[0].shape[0]

    def body(*refs):
        weight_ref, (feat_ref, first_ref, second_ref) = refs[2 * count], refs[-3:]
        assemble(refs[:count], first_ref, 0)
        assemble(refs[count : 2 * count], second_ref, 0)
        projected = jnp.dot(first_ref[:early, :], weight_ref[1, :half, :], preferred_element_type=F32)
        projected += jnp.dot(second_ref[:early, :], weight_ref[1, half:, :], preferred_element_type=F32)
        feat_ref[:early, :] = feature_map(projected).astype(BF16)

    return call(
        body,
        [jax.ShapeDtypeStruct((n_rows, columns), BF16)] + [jax.ShapeDtypeStruct((n_rows, half), BF16)] * 2,
        [VMEM] * (2 * count + 1) + [ANY] * len(after),
        [VMEM] * 3,
        flops=2 * early * width * columns,
        nbytes=2 * width * columns,
        name="early_keys",
    )(*first_pieces, *second_pieces, weight, *after)


def early_values(first_rows, second_rows, weight, early):
    n_rows, half = first_rows.shape
    columns = weight.shape[2]

    def body(first_ref, second_ref, weight_ref, values_ref):
        projected = jnp.dot(first_ref[:early, :], weight_ref[2, :half, :], preferred_element_type=F32)
        projected += jnp.dot(second_ref[:early, :], weight_ref[2, half:, :], preferred_element_type=F32)
        values_ref[:early, :] = projected.astype(BF16)

    return call(
        body,
        jax.ShapeDtypeStruct((n_rows, columns), BF16),
        [VMEM] * 3,
        VMEM,
        flops=4 * early * half * columns,
        nbytes=4 * half * columns,
        name="early_values",
    )(first_rows, second_rows, weight)


def assemble_late(pieces, halves, early, after):
    count = len(pieces[0])

    def body(*refs):
        for part in range(2):
            assemble(refs[part * count : (part + 1) * count], refs[part - 2], early)

    return call(
        body,
        [jax.ShapeDtypeStruct(half.shape, BF16) for half in halves],
        [VMEM] * (2 * count + 2) + [ANY] * len(after),
        [VMEM] * 2,
        flops=HOP_FLOPS,
        limit=4 << 20,
        input_output_aliases={2 * count: 0, 2 * count + 1: 1},
        name="assemble_late",
    )(*pieces[0], *pieces[1], *halves, *after)


def first_pass(far, rows, weight, early, after):
    n_rows, half = rows.shape
    columns = weight.shape[2]

    def body(*refs):
        far_ref, weight_ref, rows_ref, out_ref = refs[0], refs[2], refs[-2], refs[-1]
        rows_ref[n_rows - far_ref.shape[0] :, :] = far_ref[...]
        for place in range(2):
            out_ref[place] = jnp.dot(rows_ref[early:, :], weight_ref[1 + place, :half, :], preferred_element_type=F32)

    return call(
        body,
        [
            jax.ShapeDtypeStruct(rows.shape, BF16),
            jax.ShapeDtypeStruct((2, n_rows - early, columns), F32),
        ],
        [VMEM] * 3 + [ANY] * len(after),
        [VMEM] * 2,
        flops=4 * (n_rows - early) * half * columns,
        nbytes=4 * half * columns,
        input_output_aliases={1: 0},
        name="first_pass",
    )(far, rows, weight, *after)


def late_keys_and_values(far, rows, weight, first, feat_k, values, start, count, head_dim, early):
    n_rows, half = rows.shape
    columns = count * head_dim
    n_far = len(far)
    span = slice(start * head_dim, start * head_dim + columns)

    def body(*refs):
        weight_ref, first_ref = refs[n_far + 1 : n_far + 3]
        rows_ref, feat_ref, values_ref, state_ref = refs[-4:]
        for far_ref in refs[:n_far]:
            rows_ref[n_rows - far_ref.shape[0] :, :] = far_ref[...]

        def product(which):
            return first_ref[which - 1, :, span] + jnp.dot(
                rows_ref[early:, :], weight_ref[which, half:, span], preferred_element_type=F32
            )

        feat_ref[early:, span] = feature_map(product(1)).astype(BF16)
        values_ref[early:, span] = product(2).astype(BF16)
        for head in range(count):
            at = slice((start + head) * head_dim, (start + head + 1) * head_dim)
            state_ref[head] = lax.dot_general(
                feat_ref[:, at], values_ref[:, at], (((0,), (0,)), ((), ())), preferred_element_type=F32
            ).astype(BF16)

    return call(
        body,
        [jax.ShapeDtypeStruct(array.shape, BF16) for array in (rows, feat_k, values)]
        + [jax.ShapeDtypeStruct((count, head_dim, head_dim), BF16)],
        [VMEM] * (n_far + 5),
        [VMEM] * 4,
        flops=4 * (n_rows - early) * half * columns if far else HOP_FLOPS,
        nbytes=4 * half * columns,
        input_output_aliases={n_far: 0, n_far + 3: 1, n_far + 4: 2},
        name="late_keys_and_values",
    )(*far, rows, weight, first, feat_k, values)


def queries_within(halves, qkv_weight, feat_k, values, head_dim, size, rows):
    n_rows, half = halves[0].shape
    columns = qkv_weight.shape[2]
    order = slots(size)

    def place(shape, axis):
        spot = lax.axis_index("fsdp")
        spot = jnp.where(spot % 2 == 0, spot // 2, size - (spot + 1) // 2)
        row = lax.broadcasted_iota(jnp.int32, shape, axis)
        slot = row // rows
        start = jnp.zeros(shape, jnp.int32)
        for at, distance in enumerate(order):
            there = (spot + distance + size) % size
            holder = jnp.where(there < size // 2, 2 * there, 2 * (size - there) - 1)
            start = jnp.where(slot == at, holder * rows, start)
        return start + row - slot * rows

    def body(first_ref, second_ref, weight_ref, k_ref, v_ref, feat_ref, within_ref):
        causal = place((n_rows, 1), 0) >= place((1, n_rows), 1)
        projected = jnp.dot(first_ref[...], weight_ref[0, :half, :], preferred_element_type=F32)
        projected += jnp.dot(second_ref[...], weight_ref[0, half:, :], preferred_element_type=F32)
        feat_ref[...] = feature_map(projected).astype(BF16)
        for head in range(0, columns, head_dim):
            span = slice(head, head + head_dim)
            scores = lax.dot_general(
                feat_ref[:, span], k_ref[:, span], (((1,), (1,)), ((), ())), preferred_element_type=F32
            )
            scores = jnp.where(causal, scores, 0.0).astype(BF16)
            within_ref[:, span] = jnp.dot(scores, v_ref[:, span], preferred_element_type=F32)

    return call(
        body,
        (jax.ShapeDtypeStruct((n_rows, columns), BF16), jax.ShapeDtypeStruct((n_rows, columns), F32)),
        [VMEM] * 5,
        (VMEM,) * 2,
        flops=4 * n_rows * half * columns + 4 * n_rows * n_rows * columns,
        nbytes=4 * half * columns,
        name="queries_within",
    )(*halves, qkv_weight, feat_k, values)


def project_out(normalized, weight_ref, parts, rows):
    half = weight_ref.shape[1] // 2
    for which in range(2):
        tile = 512 if half % 512 == 0 else 128
        for start in range(0, half, tile):
            span = slice(start, start + tile)
            product = jnp.dot(normalized, weight_ref[:, which * half + start : which * half + start + tile], preferred_element_type=F32).astype(BF16)
            for block in range(len(parts) // 2):
                parts[2 * block + which][:, span] = product[block * rows : (block + 1) * rows, :]


def attend_and_project(feat_q, within, initial, exchanged, gain, out_weight, blocks, rows, head_dim):
    per_group = initial.shape[0] // len(exchanged)
    steps = len(exchanged[0])
    others = [other for group in exchanged for other in group]
    n_rows, columns = feat_q.shape
    half = out_weight.shape[1] // 2

    def body(q_ref, within_ref, initial_ref, gain_ref, weight_ref, *refs):
        other_refs, normalized_ref, parts = refs[: len(others)], refs[len(others)], refs[len(others) + 1 :]
        place = lax.axis_index("ctx")
        for head in range(columns // head_dim):
            at = slice(head * head_dim, (head + 1) * head_dim)
            prefix = initial_ref[head]
            group, within_group = divmod(head, per_group)
            for bit, other_ref in enumerate(other_refs[group * steps : (group + 1) * steps]):
                later = (place // 2**bit) % 2 == 1
                prefix = prefix + jnp.where(later, other_ref[within_group].astype(F32), 0.0)
            high = prefix.astype(BF16)
            low = (prefix - high.astype(F32)).astype(BF16)
            q = q_ref[:, at]
            attended = within_ref[:, at] + jnp.dot(q, high, preferred_element_type=F32)
            attended = attended + jnp.dot(q, low, preferred_element_type=F32)
            scale = lax.rsqrt(jnp.mean(attended * attended, axis=-1, keepdims=True) + 1e-06)
            normalized_ref[:, at] = (attended * scale * gain_ref[:, at]).astype(BF16)
        project_out(normalized_ref[n_rows - blocks * rows :, :], weight_ref, parts, rows)

    out = call(
        body,
        [jax.ShapeDtypeStruct((n_rows, columns), BF16)] + [jax.ShapeDtypeStruct((rows, half), BF16)] * (2 * blocks),
        [VMEM] * (5 + len(others)),
        [VMEM] * (1 + 2 * blocks),
        flops=4 * n_rows * half * columns,
        nbytes=4 * half * columns,
        name="attend_and_project",
    )(feat_q, within, initial, gain.reshape(1, columns), out_weight, *others)
    return out[0], [out[1 + 2 * block : 3 + 2 * block] for block in range(blocks)]


def project_rest(normalized, out_weight, blocks, rows):
    columns = normalized.shape[1]
    half = out_weight.shape[1] // 2

    def body(normalized_ref, weight_ref, *parts):
        project_out(normalized_ref[: blocks * rows, :], weight_ref, parts, rows)

    out = call(
        body,
        [jax.ShapeDtypeStruct((rows, half), BF16)] * (2 * blocks),
        [VMEM] * 2,
        [VMEM] * (2 * blocks),
        flops=HOP_FLOPS,
        nbytes=4 * half * columns,
        name="project_rest",
    )(normalized, out_weight)
    return [out[2 * block : 2 * block + 2] for block in range(blocks)]


def add_step(mine, got):
    def body(mine_ref, got_ref, out_ref):
        out_ref[...] = (mine_ref[...].astype(F32) + got_ref[...].astype(F32)).astype(BF16)

    return call(
        body,
        jax.ShapeDtypeStruct(mine.shape, BF16),
        [VMEM] * 2,
        VMEM,
        nbytes=6 * mine.size,
        limit=4 << 20,
        name="add_step",
    )(mine, got)


def add_own(own, trailing):
    def body(first, second, got_first, got_second, out):
        out[0] = first[...].astype(F32) + got_first[...].astype(F32)
        out[1] = second[...].astype(F32) + got_second[...].astype(F32)

    return call(
        body,
        jax.ShapeDtypeStruct((2,) + own[0].shape, F32),
        [VMEM] * 4,
        VMEM,
        flops=HOP_FLOPS,
        nbytes=16 * own[0].size,
        limit=4 << 20,
        name="add_own",
    )(*own, *trailing)


def finish(gathered, leading):
    rows, half = leading[0].shape

    def body(gathered_ref, first, second, out):
        out[:, :half] = (gathered_ref[0] + first[...].astype(F32)).astype(BF16)
        out[:, half:] = (gathered_ref[1] + second[...].astype(F32)).astype(BF16)

    return call(
        body,
        jax.ShapeDtypeStruct((rows, 2 * half), BF16),
        [VMEM] * 3,
        VMEM,
        nbytes=4 * rows * half,
        limit=4 << 20,
        name="finish",
    )(gathered, *leading)


def ring_scatter(parts, order, right, left):
    far = max(order)

    def part(distance, half):
        return parts[order.index(distance)][half]

    def hop(to_right, to_left):
        return lax.ppermute(to_right, "fsdp", right), lax.ppermute(to_left, "fsdp", left)

    leading = hop(part(far, 0), part(far, 1))
    trailing = hop(part(far - 1, 1), part(1 - far, 0))
    for step in range(far - 1, 0, -1):
        leading = hop(add_step(part(step, 0), leading[0]), add_step(part(-step, 1), leading[1]))
        if step > 1:
            trailing = hop(
                add_step(part(step - 1, 1), trailing[0]), add_step(part(1 - step, 0), trailing[1])
            )
    gathered = add_own(parts[0], (trailing[1], trailing[0]))
    return finish(gathered, leading)


def add_states(one, two, after):
    def body(one_ref, two_ref, *refs):
        refs[-1][...] = (one_ref[...].astype(F32) + two_ref[...].astype(F32)).astype(BF16)

    return call(
        body,
        jax.ShapeDtypeStruct(one.shape, BF16),
        [VMEM] * 2 + [ANY] * len(after),
        VMEM,
        nbytes=6 * one.size,
        limit=4 << 20,
        name="add_states",
    )(one, two, *after)


def exchange_states(states, size):
    received = [[] for _ in states]
    totals = list(states)
    reach = 1
    while reach < size:
        pairs = [(i, i ^ reach) for i in range(size)]
        for at, total in enumerate(totals):
            received[at].append(lax.ppermute(total, "ctx", pairs))
        reach *= 2
        if reach < size:
            after = []
            for at, total in enumerate(totals):
                totals[at] = add_states(total, received[at][-1], after)
                after = [totals[at]]
    return received


def per_device(n_ctx, n_fsdp, tokens, qkv_weight, out_weight, norm_gain, initial_state):
    rows, width = tokens.shape
    heads_here, head_dim = initial_state.shape[:2]
    columns = heads_here * head_dim
    n_rows = rows * n_fsdp
    right, left = neighbours(n_fsdp)
    order = slots(n_fsdp)

    held = ring_gather(tokens, n_fsdp, right, left)

    blocks = n_fsdp - 3
    early = blocks * rows
    feat_k, *halves = early_keys(held[0][:blocks], held[1][:blocks], qkv_weight, n_rows, [held[1][-2]])
    values = early_values(*halves, qkv_weight, early)
    first_rows, second_rows = assemble_late([held[0][blocks:-1], held[1][blocks:-1]], halves, early, [values])
    marks = [mark(held[0][1]), mark(held[1][2])]
    first_rows, first = first_pass(held[0][-1], first_rows, qkv_weight, early, marks + [feat_k])
    count = heads_here // 2 if heads_here % 2 == 0 else heads_here
    states = []
    for start in range(0, heads_here, count):
        far = [held[1][-1]] if start == 0 else []
        second_rows, feat_k, values, state = late_keys_and_values(
            far, second_rows, qkv_weight, first, feat_k, values, start, count, head_dim, early
        )
        states.append(state)
    halves = (first_rows, second_rows)
    feat_q, within = queries_within(halves, qkv_weight, feat_k, values, head_dim, n_fsdp, rows)
    exchanged = exchange_states(states, n_ctx)
    soon = 1
    normalized, parts = attend_and_project(
        feat_q, within, initial_state, exchanged, norm_gain, out_weight, soon, rows, head_dim
    )
    parts = project_rest(normalized, out_weight, n_fsdp - soon, rows) + parts

    return ring_scatter(parts, order, right, left)


def solution(mesh):
    body = functools.partial(per_device, mesh.shape["ctx"], mesh.shape["fsdp"])
    placed = (
        P(("ctx", "fsdp"), None),
        P(None, None, "fsdp"),
        P("fsdp", None),
        P("fsdp"),
        P("fsdp", None, None),
    )
    return jax.shard_map(
        body, mesh=mesh, in_specs=placed, out_specs=P(("ctx", "fsdp"), None), check_vma=False
    )
```

```python
import functools

import jax
import jax.numpy as jnp
from jax import lax
from jax.experimental import pallas as pl
from jax.experimental.pallas import tpu as pltpu
from jax.sharding import PartitionSpec as P

VMEM = pl.BlockSpec(memory_space=pltpu.VMEM)
ANY = pl.BlockSpec(memory_space=pl.ANY)
HBM = pl.BlockSpec(memory_space=pltpu.HBM)
F32, BF16 = jnp.float32, jnp.bfloat16
HOP_FLOPS = 5 * 10**9


def ring_order(size):
    return list(range(0, size, 2)) + list(range(size - 1, 0, -2))


def neighbours(size):
    ring = ring_order(size)
    right = [(ring[i], ring[(i + 1) % size]) for i in range(size)]
    left = [(b, a) for a, b in right]
    return right, left


def slots(size):
    order = [0]
    for step in range(1, size // 2):
        order += [-step, step]
    return order + [size // 2]


def in_hbm(array):
    return pltpu.with_memory_space_constraint(array, pltpu.HBM)


def call(body, out_shape, in_specs, out_specs, flops=0, nbytes=0, limit=12 << 20, **more):
    return pl.pallas_call(
        body,
        out_shape=out_shape,
        in_specs=in_specs,
        out_specs=out_specs,
        cost_estimate=pl.CostEstimate(flops=flops, bytes_accessed=nbytes, transcendentals=0),
        compiler_params=pltpu.CompilerParams(vmem_limit_bytes=limit),
        **more,
    )


def mark(arrived):
    def body(arrived_ref, out_ref):
        out_ref[...] = jnp.zeros_like(out_ref)

    return call(
        body,
        jax.ShapeDtypeStruct((8, 128), F32),
        [ANY],
        VMEM,
        flops=HOP_FLOPS,
        limit=1 << 20,
        name="mark",
    )(arrived)


def ring_gather(block, size, right, left):
    half = block.shape[1] // 2
    going_right = [block[:, :half], block[:, half:]]
    going_left = list(going_right)
    held = [[going_right[0]], [going_right[1]]]
    for _ in range(1, size // 2):
        for part in range(2):
            going_right[part] = lax.ppermute(going_right[part], "fsdp", right)
            going_left[1 - part] = lax.ppermute(going_left[1 - part], "fsdp", left)
        for part in range(2):
            held[part] += [going_right[part], going_left[part]]
    held[0].append(lax.ppermute(going_right[0], "fsdp", right))
    held[1].append(lax.ppermute(going_left[1], "fsdp", left))
    return held


def assemble(pieces, into, first_row):
    rows = pieces[0].shape[0]
    for place, piece in enumerate(pieces):
        into[first_row + place * rows : first_row + (place + 1) * rows, :] = piece[...]


def feature_map(projected):
    return jnp.where(projected > 0.0, projected + 1.0, jnp.exp(jnp.minimum(projected, 0.0)))


def early_keys(first_pieces, second_pieces, weight, n_rows, after):
    _, width, columns = weight.shape
    half = width // 2
    count = len(first_pieces)
    early = count * first_pieces[0].shape[0]

    def body(*refs):
        weight_ref, (feat_ref, first_ref, second_ref) = refs[2 * count], refs[-3:]
        assemble(refs[:count], first_ref, 0)
        assemble(refs[count : 2 * count], second_ref, 0)
        projected = jnp.dot(first_ref[:early, :], weight_ref[1, :half, :], preferred_element_type=F32)
        projected += jnp.dot(second_ref[:early, :], weight_ref[1, half:, :], preferred_element_type=F32)
        feat_ref[:early, :] = feature_map(projected).astype(BF16)

    return call(
        body,
        [jax.ShapeDtypeStruct((n_rows, columns), BF16)] + [jax.ShapeDtypeStruct((n_rows, half), BF16)] * 2,
        [VMEM] * (2 * count + 1) + [ANY] * len(after),
        [VMEM] * 3,
        flops=2 * early * width * columns,
        nbytes=2 * width * columns,
        name="early_keys",
    )(*first_pieces, *second_pieces, weight, *after)


def early_values(first_rows, second_rows, weight, early):
    n_rows, half = first_rows.shape
    columns = weight.shape[2]

    def body(first_ref, second_ref, weight_ref, values_ref):
        projected = jnp.dot(first_ref[:early, :], weight_ref[2, :half, :], preferred_element_type=F32)
        projected += jnp.dot(second_ref[:early, :], weight_ref[2, half:, :], preferred_element_type=F32)
        values_ref[:early, :] = projected.astype(BF16)

    return call(
        body,
        jax.ShapeDtypeStruct((n_rows, columns), BF16),
        [VMEM] * 3,
        VMEM,
        flops=4 * early * half * columns,
        nbytes=4 * half * columns,
        name="early_values",
    )(first_rows, second_rows, weight)


def assemble_late(pieces, halves, early, after):
    count = len(pieces[0])

    def body(*refs):
        for part in range(2):
            assemble(refs[part * count : (part + 1) * count], refs[part - 2], early)

    return call(
        body,
        [jax.ShapeDtypeStruct(half.shape, BF16) for half in halves],
        [VMEM] * (2 * count + 2) + [ANY] * len(after),
        [VMEM] * 2,
        flops=HOP_FLOPS,
        limit=4 << 20,
        input_output_aliases={2 * count: 0, 2 * count + 1: 1},
        name="assemble_late",
    )(*pieces[0], *pieces[1], *halves, *after)


def first_pass(far, rows, weight, early, after):
    n_rows, half = rows.shape
    columns = weight.shape[2]

    def body(*refs):
        far_ref, weight_ref, rows_ref, out_ref = refs[0], refs[2], refs[-2], refs[-1]
        rows_ref[n_rows - far_ref.shape[0] :, :] = far_ref[...]
        for place in range(2):
            out_ref[place] = jnp.dot(rows_ref[early:, :], weight_ref[1 + place, :half, :], preferred_element_type=F32)

    return call(
        body,
        [
            jax.ShapeDtypeStruct(rows.shape, BF16),
            jax.ShapeDtypeStruct((2, n_rows - early, columns), F32),
        ],
        [VMEM] * 3 + [ANY] * len(after),
        [VMEM] * 2,
        flops=4 * (n_rows - early) * half * columns,
        nbytes=4 * half * columns,
        input_output_aliases={1: 0},
        name="first_pass",
    )(far, rows, weight, *after)


def late_keys_and_values(far, rows, weight, first, feat_k, values, start, count, head_dim, early):
    n_rows, half = rows.shape
    columns = count * head_dim
    n_far = len(far)
    span = slice(start * head_dim, start * head_dim + columns)

    def body(*refs):
        weight_ref, first_ref = refs[n_far + 1 : n_far + 3]
        rows_ref, feat_ref, values_ref, state_ref = refs[-4:]
        for far_ref in refs[:n_far]:
            rows_ref[n_rows - far_ref.shape[0] :, :] = far_ref[...]

        def product(which):
            return first_ref[which - 1, :, span] + jnp.dot(
                rows_ref[early:, :], weight_ref[which, half:, span], preferred_element_type=F32
            )

        feat_ref[early:, span] = feature_map(product(1)).astype(BF16)
        values_ref[early:, span] = product(2).astype(BF16)
        for head in range(count):
            at = slice((start + head) * head_dim, (start + head + 1) * head_dim)
            state_ref[head] = lax.dot_general(
                feat_ref[:, at], values_ref[:, at], (((0,), (0,)), ((), ())), preferred_element_type=F32
            ).astype(BF16)

    return call(
        body,
        [jax.ShapeDtypeStruct(array.shape, BF16) for array in (rows, feat_k, values)]
        + [jax.ShapeDtypeStruct((count, head_dim, head_dim), BF16)],
        [VMEM] * (n_far + 5),
        [VMEM] * 4,
        flops=4 * (n_rows - early) * half * columns if far else HOP_FLOPS,
        nbytes=4 * half * columns,
        input_output_aliases={n_far: 0, n_far + 3: 1, n_far + 4: 2},
        name="late_keys_and_values",
    )(*far, rows, weight, first, feat_k, values)


def queries_within(halves, qkv_weight, feat_k, values, head_dim, size, rows):
    n_rows, half = halves[0].shape
    columns = qkv_weight.shape[2]
    order = slots(size)

    def place(shape, axis):
        spot = lax.axis_index("fsdp")
        spot = jnp.where(spot % 2 == 0, spot // 2, size - (spot + 1) // 2)
        row = lax.broadcasted_iota(jnp.int32, shape, axis)
        slot = row // rows
        start = jnp.zeros(shape, jnp.int32)
        for at, distance in enumerate(order):
            there = (spot + distance + size) % size
            holder = jnp.where(there < size // 2, 2 * there, 2 * (size - there) - 1)
            start = jnp.where(slot == at, holder * rows, start)
        return start + row - slot * rows

    def body(first_ref, second_ref, weight_ref, k_ref, v_ref, feat_ref, within_ref):
        causal = place((n_rows, 1), 0) >= place((1, n_rows), 1)
        projected = jnp.dot(first_ref[...], weight_ref[0, :half, :], preferred_element_type=F32)
        projected += jnp.dot(second_ref[...], weight_ref[0, half:, :], preferred_element_type=F32)
        feat_ref[...] = feature_map(projected).astype(BF16)
        for head in range(0, columns, head_dim):
            span = slice(head, head + head_dim)
            scores = lax.dot_general(
                feat_ref[:, span], k_ref[:, span], (((1,), (1,)), ((), ())), preferred_element_type=F32
            )
            scores = jnp.where(causal, scores, 0.0).astype(BF16)
            within_ref[:, span] = jnp.dot(scores, v_ref[:, span], preferred_element_type=F32)

    return call(
        body,
        (jax.ShapeDtypeStruct((n_rows, columns), BF16), jax.ShapeDtypeStruct((n_rows, columns), F32)),
        [VMEM] * 5,
        (VMEM,) * 2,
        flops=4 * n_rows * half * columns + 4 * n_rows * n_rows * columns,
        nbytes=4 * half * columns,
        name="queries_within",
    )(*halves, qkv_weight, feat_k, values)


def project_out(normalized, weight_ref, parts, rows):
    half = weight_ref.shape[1] // 2
    for which in range(2):
        tile = 512 if half % 512 == 0 else 128
        for start in range(0, half, tile):
            span = slice(start, start + tile)
            product = jnp.dot(normalized, weight_ref[:, which * half + start : which * half + start + tile], preferred_element_type=F32).astype(BF16)
            for block in range(len(parts) // 2):
                parts[2 * block + which][:, span] = product[block * rows : (block + 1) * rows, :]


def attend_and_project(rows, feat_q, within, initial, exchanged, gain, out_weight, block, head_dim, flops, name):
    columns = feat_q.shape[1]
    half = out_weight.shape[1] // 2
    per_group = initial.shape[0] // len(exchanged)
    steps = len(exchanged[0])
    others = [other for group in exchanged for other in group]
    count = rows.stop - rows.start
    n_parts = 2 * (count // block)

    def body(q_ref, within_ref, initial_ref, gain_ref, weight_ref, *refs):
        other_refs, parts, normalized_ref = refs[: len(others)], refs[len(others) : -1], refs[-1]
        place = lax.axis_index("ctx")
        for head in range(columns // head_dim):
            at = slice(head * head_dim, (head + 1) * head_dim)
            prefix = initial_ref[head]
            group, within_group = divmod(head, per_group)
            for bit, other_ref in enumerate(other_refs[group * steps : (group + 1) * steps]):
                later = (place // 2**bit) % 2 == 1
                prefix = prefix + jnp.where(later, other_ref[within_group].astype(F32), 0.0)
            high = prefix.astype(BF16)
            low = (prefix - high.astype(F32)).astype(BF16)
            q = q_ref[rows, at]
            attended = within_ref[rows, at] + jnp.dot(q, high, preferred_element_type=F32)
            attended = attended + jnp.dot(q, low, preferred_element_type=F32)
            scale = lax.rsqrt(jnp.mean(attended * attended, axis=-1, keepdims=True) + 1e-06)
            normalized_ref[:, at] = (attended * scale * gain_ref[:, at]).astype(BF16)
        project_out(normalized_ref[...], weight_ref, parts, block)

    out = call(
        body,
        [jax.ShapeDtypeStruct((block, half), BF16)] * n_parts,
        [VMEM] * (5 + len(others)),
        [VMEM] * n_parts,
        flops=flops,
        nbytes=4 * half * columns,
        scratch_shapes=[pltpu.VMEM((count, columns), BF16)],
        name=name,
    )(feat_q, within, initial, gain.reshape(1, columns), out_weight, *others)
    return [out[2 * at : 2 * at + 2] for at in range(count // block)]


def add_step(mine, got):
    def body(mine_ref, got_ref, out_ref):
        out_ref[...] = (mine_ref[...].astype(F32) + got_ref[...].astype(F32)).astype(BF16)

    return call(
        body,
        jax.ShapeDtypeStruct(mine.shape, BF16),
        [VMEM] * 2,
        VMEM,
        nbytes=6 * mine.size,
        limit=4 << 20,
        name="add_step",
    )(mine, got)


def add_own(own, trailing):
    def body(first, second, got_first, got_second, out):
        out[0] = first[...].astype(F32) + got_first[...].astype(F32)
        out[1] = second[...].astype(F32) + got_second[...].astype(F32)

    return call(
        body,
        jax.ShapeDtypeStruct((2,) + own[0].shape, F32),
        [VMEM] * 4,
        VMEM,
        flops=HOP_FLOPS,
        nbytes=16 * own[0].size,
        limit=4 << 20,
        name="add_own",
    )(*own, *trailing)


def finish(gathered, leading):
    rows, half = leading[0].shape

    def body(gathered_ref, first, second, out):
        out[:, :half] = (gathered_ref[0] + first[...].astype(F32)).astype(BF16)
        out[:, half:] = (gathered_ref[1] + second[...].astype(F32)).astype(BF16)

    return call(
        body,
        jax.ShapeDtypeStruct((rows, 2 * half), BF16),
        [VMEM] * 3,
        VMEM,
        nbytes=4 * rows * half,
        limit=4 << 20,
        name="finish",
    )(gathered, *leading)


def ring_scatter(parts, order, right, left):
    far = max(order)

    def part(distance, half):
        return parts[order.index(distance)][half]

    def hop(to_right, to_left):
        return lax.ppermute(to_right, "fsdp", right), lax.ppermute(to_left, "fsdp", left)

    leading = hop(part(far, 0), part(far, 1))
    trailing = hop(part(far - 1, 1), part(1 - far, 0))
    for step in range(far - 1, 0, -1):
        leading = hop(add_step(part(step, 0), leading[0]), add_step(part(-step, 1), leading[1]))
        if step > 1:
            trailing = hop(
                add_step(part(step - 1, 1), trailing[0]), add_step(part(1 - step, 0), trailing[1])
            )
    gathered = add_own(parts[0], (trailing[1], trailing[0]))
    return finish(gathered, leading)


def add_states(one, two, after):
    def body(one_ref, two_ref, *refs):
        refs[-1][...] = (one_ref[...].astype(F32) + two_ref[...].astype(F32)).astype(BF16)

    return call(
        body,
        jax.ShapeDtypeStruct(one.shape, BF16),
        [VMEM] * 2 + [ANY] * len(after),
        VMEM,
        nbytes=6 * one.size,
        limit=4 << 20,
        name="add_states",
    )(one, two, *after)


def exchange_states(states, size):
    received = [[] for _ in states]
    totals = list(states)
    reach = 1
    while reach < size:
        pairs = [(i, i ^ reach) for i in range(size)]
        for at, total in enumerate(totals):
            received[at].append(lax.ppermute(total, "ctx", pairs))
        reach *= 2
        if reach < size:
            after = []
            for at, total in enumerate(totals):
                totals[at] = add_states(total, received[at][-1], after)
                after = [totals[at]]
    return received


def per_device(n_ctx, n_fsdp, tokens, qkv_weight, out_weight, norm_gain, initial_state):
    rows, width = tokens.shape
    heads_here, head_dim = initial_state.shape[:2]
    columns = heads_here * head_dim
    n_rows = rows * n_fsdp
    right, left = neighbours(n_fsdp)
    order = slots(n_fsdp)

    held = ring_gather(tokens, n_fsdp, right, left)

    blocks = n_fsdp - 3
    early = blocks * rows
    feat_k, *halves = early_keys(held[0][:blocks], held[1][:blocks], qkv_weight, n_rows, [held[1][-2]])
    values = early_values(*halves, qkv_weight, early)
    first_rows, second_rows = assemble_late([held[0][blocks:-1], held[1][blocks:-1]], halves, early, [values])
    marks = [mark(held[0][1]), mark(held[1][2])]
    first_rows, first = first_pass(held[0][-1], first_rows, qkv_weight, early, marks + [feat_k])
    count = heads_here // 2 if heads_here % 2 == 0 else heads_here
    states = []
    for start in range(0, heads_here, count):
        far = [held[1][-1]] if start == 0 else []
        second_rows, feat_k, values, state = late_keys_and_values(
            far, second_rows, qkv_weight, first, feat_k, values, start, count, head_dim, early
        )
        states.append(state)
    halves = (first_rows, second_rows)
    feat_q, within = queries_within(halves, qkv_weight, feat_k, values, head_dim, n_fsdp, rows)
    exchanged = exchange_states(states, n_ctx)
    last = n_rows - rows
    common = (feat_q, within, initial_state, exchanged, norm_gain, out_weight, rows, head_dim)
    farthest = attend_and_project(slice(last, n_rows), *common, 2 * rows * columns * width, "attend_farthest")
    parts = attend_and_project(slice(0, last), *common, HOP_FLOPS, "attend_rest") + farthest
    mirrored = [distance if distance == n_fsdp // 2 else -distance for distance in order]
    return ring_scatter(parts, mirrored, left, right)


def solution(mesh):
    body = functools.partial(per_device, mesh.shape["ctx"], mesh.shape["fsdp"])
    placed = (
        P(("ctx", "fsdp"), None),
        P(None, None, "fsdp"),
        P("fsdp", None),
        P("fsdp"),
        P("fsdp", None, None),
    )
    return jax.shard_map(
        body, mesh=mesh, in_specs=placed, out_specs=P(("ctx", "fsdp"), None), check_vma=False
    )
```
